32 devices in a mesh: groups: 2 (over y), ex: 8 (over z, x), dim: 2 (over core).
Axes of the slice: x: 2, y: 2, z: 4, core: 2. Of those that a mesh axis runs over, the one named last changes fastest.
Arguments:
- store: bfloat16 [12288, 4096], P(('groups', 'ex'), 'dim'), parts along dimension 0, may hold values from -6 to 6
- queries: bfloat16 [2048, 4096], P(('groups', 'ex'), 'dim'), parts along dimension 0, may hold values from -0.09375 to 0.09375
- precond: float32 [4096], P('dim'), may hold values from 0.25 to 4
- query_rank: int32 [16, 128], P(('groups', 'ex')), parts along dimension 0, may hold values from 0 to 127, each once within a row
- valid_rows: int32 [16], P(('groups', 'ex')), parts along dimension 0, may hold values from 1 to 768, 4608 in all
Outputs:
- scores: float32 [12288, 512], P(('groups', 'ex', 'dim')), parts along dimension 0
The draws below stay inside these ranges and needn't reach their ends.
There are 2 independent parts, one for each index of `groups`. The reference program is written for one: setup_inputs(seed, part) draws one part's arguments, and reference() takes and returns one part's arrays. A program takes and returns all parts, laid end to end along the dimension named above; an argument that names none is the same for every part. Nothing has to cross between parts.
Inputs may be any that keep to these rules, and one draw needn't show every extreme that they name: `query_rank`: each row is a permutation of 0 to 127. `valid_rows`: the counts sum to 8 * 768 * 3 // 4.
All inputs are finite; a program needn't handle non-finite values. No bound on the sum of `valid_rows` on one device may be relied on, other than what follows from the above.
Results may differ from the reference program's by a relative error of at most 0.0029.
Values may be sent and summed in bfloat16 or wider, within the bound.
No kernel may reach another device: no remote copies, remote signals or barrier semaphores. Data moves between devices by JAX's collectives and lax.ppermute only.
A program may use at most 64 MiB of HBM per device.

```python
import math
import jax
import jax.numpy as jnp
import numpy as np
from jax import lax

D = 4096
EX_DEV = 768
QB = 128
STEPS = 4
QUERIES = 1024
EXAMPLES = 6144
N_EX = 8


def shard_levels(rng, dims, shards, least, largest):
    def one(dim, parts):
        heights = jax.random.uniform(jax.random.fold_in(jax.random.fold_in(rng, 6), dim), (parts,), jnp.float32, least / len(shards), largest / len(shards))
        return jnp.repeat(jnp.exp(heights), dims[dim] // parts).reshape((-1,) + (1,) * (len(dims) - dim - 1))

    factor_of = one(*shards[0])
    for cut in shards[1:]:
        factor_of = factor_of * one(*cut)
    return factor_of


def split_up(amount, total, most, slope):
    portions = [(1 << 20) // math.isqrt(rank ** slope) + 1 for rank in range(2, amount + 1)]
    surplus, given = total - most - (amount - 1), [1] * (amount - 1)
    while surplus > 0:
        movable = [i for i in range(amount - 1) if given[i] < most]
        whole, left = sum([portions[i] for i in movable]), surplus
        for i in movable:
            extra = min(most - given[i], max(1, left * portions[i] // whole), surplus)
            given[i] = given[i] + extra
            surplus = surplus - extra
    return np.array([most] + given)


def ragged(rng, amount, total, most, lean):
    if amount == 2:
        one = jax.random.randint(rng, (), max(1, total - most), min(most, total - 1) + 1)
        return jnp.stack([one, total - one])
    sizes = jnp.asarray(split_up(amount, total, most, lean), jnp.int32)
    pairs = (amount - 1) // 2
    giver, taker = sizes[1:1 + 2 * pairs:2], sizes[2:2 + 2 * pairs:2]
    margin = jnp.minimum(giver - 1, most - taker)
    moved = jax.random.randint(jax.random.fold_in(rng, 1), (pairs,), 0, 1 << 20) % (margin + 1)
    sizes = sizes.at[1:1 + 2 * pairs:2].set(giver - moved).at[2:2 + 2 * pairs:2].set(taker + moved)
    return sizes[jax.random.permutation(jax.random.fold_in(rng, 2), amount)]


def centred(stream_key, extent, spread, bound, shards=(), kind=jnp.bfloat16):
    gain = shard_levels(stream_key, extent, shards, -0.22, 0.18) if shards else 1.0
    array = jax.random.normal(stream_key, extent, jnp.float32) * spread * gain
    return jnp.minimum(jnp.maximum(array, -bound), bound).astype(kind)


def setup_inputs(seed: int = 0, part: int = 0) -> dict:
    splits = jax.random.split(jax.random.key(seed), 6)
    part_splits = jax.random.split(jax.random.fold_in(splits[5], part), 6)
    store = centred(part_splits[0], (EXAMPLES, D), 1.0, 6.0, ((0, 8), (1, 2)))
    queries = centred(part_splits[1], (QUERIES, D), D ** -0.5, 0.09375, ((0, 8), (1, 2)))
    precond = jnp.clip(jnp.exp(math.log(4.0) - 2.7725887 * jax.random.uniform(splits[2], (D,), jnp.float32) ** shard_levels(splits[2], (D,), ((0, 2),), -0.2, 0.2)), 0.25, 4.0)
    query_rank = jax.vmap(lambda own: jax.random.permutation(own, QB))(jax.random.split(part_splits[3], N_EX)).reshape((N_EX, QB)).astype(jnp.int32)
    valid_rows = ragged(part_splits[4], N_EX, N_EX * EX_DEV * 3 // 4, EX_DEV, 1).astype(jnp.int32)
    return {"store": store, "queries": queries, "precond": precond, "query_rank": query_rank, "valid_rows": valid_rows}


def reference(store, queries, precond, query_rank, valid_rows):
    pre = (queries.astype(jnp.float32) * precond[None, :]).astype(jnp.bfloat16)
    blocks = pre.reshape(N_EX, QB, D)

    def place(block, rank):
        return jnp.zeros((QB, D), jnp.bfloat16).at[rank].set(block)

    ordered = jax.vmap(place)(blocks, query_rank)
    store_blocks = store.reshape(N_EX, EX_DEV, D)
    row_ids = jnp.arange(EX_DEV, dtype=jnp.int32)

    def one_block(index):
        rows = store_blocks[index]
        picked = [ordered[(index - step) % N_EX] for step in range(STEPS)]
        stacked = jnp.concatenate(picked, axis=0)
        result = jnp.dot(rows, stacked.T, preferred_element_type=jnp.float32)
        keep = row_ids < valid_rows[index]
        return jnp.where(keep[:, None], result, jnp.float32(0.0))

    out = lax.map(one_block, jnp.arange(N_EX, dtype=jnp.int32))
    return out.reshape(N_EX * EX_DEV, STEPS * QB)
```

```python
import functools

import jax
import jax.numpy as jnp
from jax import lax
from jax.experimental import pallas as pl
from jax.experimental.pallas import tpu as pltpu
from jax.sharding import PartitionSpec as P

STEPS = 4
CHUNKS = 2
VMEM_BYTES = 16 * 1024 * 1024


def params():
    return pltpu.CompilerParams(vmem_limit_bytes=VMEM_BYTES)


def whole_spec():
    return pl.BlockSpec(memory_space=pltpu.VMEM)


def prepare_kernel(queries, precond, rank, *chunks):
    rows = queries.shape[0]
    positions = lax.broadcasted_iota(jnp.int32, (rows, rows), 0)
    placing = (positions == rank[...]).astype(jnp.bfloat16)
    width = chunks[0].shape[1]
    for n, chunk in enumerate(chunks):
        cut = slice(n * width, (n + 1) * width)
        pre = (queries[:, cut].astype(jnp.float32) * precond[:, cut]).astype(jnp.bfloat16)
        chunk[...] = jnp.dot(placing, pre, preferred_element_type=jnp.float32).astype(jnp.bfloat16)


def prepare(queries, precond, rank):
    rows, depth = queries.shape
    shape = jax.ShapeDtypeStruct((rows, depth // CHUNKS), jnp.bfloat16)
    return pl.pallas_call(
        prepare_kernel,
        out_shape=[shape] * CHUNKS,
        in_specs=[whole_spec()] * 3,
        out_specs=[whole_spec()] * CHUNKS,
        compiler_params=params(),
        cost_estimate=pl.CostEstimate(
            flops=2 * rows * rows * depth, bytes_accessed=4 * rows * depth, transcendentals=0
        ),
    )(queries, precond, rank)


def scores_kernel(cuts, carried, *refs):
    store, blocks = refs[0], refs[1:1 + len(cuts)]
    carry = refs[1 + len(cuts):-2]
    send, own = refs[-2:]
    half = send.shape[0]
    me = lax.axis_index("dim")
    for where, out in ((1 - me, send), (me, own)):
        rows = pl.ds(pl.multiple_of(where * half, half), half)
        total = None
        if carried:
            total = (carry[0] if out is send else carry[1])[...]
        for n, block in zip(cuts, blocks):
            width = block.shape[1]
            part = lax.dot_general(
                store[rows, n * width:(n + 1) * width],
                block[...],
                (((1,), (1,)), ((), ())),
                preferred_element_type=jnp.float32,
            )
            total = part if total is None else total + part
        out[...] = total


def partial_scores(store, blocks, carry=()):
    cuts = [n for n, _ in blocks]
    blocks = [block for _, block in blocks]
    rows, columns = store.shape[0], blocks[0].shape[0]
    shape = jax.ShapeDtypeStruct((rows // 2, columns), jnp.float32)
    operands = [store, *blocks, *carry]
    depth = sum(block.shape[1] for block in blocks)
    return pl.pallas_call(
        functools.partial(scores_kernel, cuts, bool(carry)),
        out_shape=[shape] * 2,
        in_specs=[whole_spec()] * len(operands),
        out_specs=[whole_spec()] * 2,
        compiler_params=params(),
        cost_estimate=pl.CostEstimate(
            flops=2 * rows * columns * depth,
            bytes_accessed=2 * (rows + columns) * depth + 4 * rows * columns,
            transcendentals=0,
        ),
    )(*operands)


def finish_kernel(places, valid, *refs):
    out = refs[-1]
    half, columns = refs[0].shape
    me = lax.axis_index("dim")
    odd = lax.rem(lax.axis_index("ex"), 2)
    row_ids = lax.broadcasted_iota(jnp.int32, (half, columns), 0) + me * half
    keep = row_ids < valid[0]
    for n, place in enumerate(places):
        step = place[0] + odd * (place[1] - place[0])
        total = refs[2 * n][...] + refs[2 * n + 1][...]
        out[:, pl.ds(pl.multiple_of(step * columns, columns), columns)] = jnp.where(keep, total, 0.0)


def finish(valid, pairs, places):
    half, columns = pairs[0][0].shape
    operands = [ref for pair in pairs for ref in pair]
    return pl.pallas_call(
        functools.partial(finish_kernel, places),
        out_shape=jax.ShapeDtypeStruct((half, columns * len(pairs)), jnp.float32),
        in_specs=[pl.BlockSpec(memory_space=pltpu.SMEM)] + [whole_spec()] * len(operands),
        out_specs=whole_spec(),
        compiler_params=params(),
        cost_estimate=pl.CostEstimate(
            flops=half * columns * len(pairs),
            bytes_accessed=12 * half * columns * len(pairs),
            transcendentals=0,
        ),
    )(valid, *operands)


def shards(store, queries, precond, query_rank, valid_rows):
    size = lax.axis_size("ex")
    ahead = [(i, (i + 2) % size) for i in range(size)]
    swap = [(i, i ^ 1) for i in range(size)]
    to_odd = [(i, i + 1) for i in range(0, size, 2)]
    even_ahead = [(i, (i + 2) % size) for i in range(0, size, 2)]
    over_dim = [(0, 1), (1, 0)]

    own = prepare(queries, precond[None, :], query_rank)
    chunks = range(CHUNKS)
    two_back = [lax.ppermute(own[n], "ex", ahead) for n in chunks]
    odd_one_back = [lax.ppermute(own[n], "ex", to_odd) for n in chunks]
    swapped = [lax.ppermute(two_back[n], "ex", swap) for n in chunks]
    even_three_back = [lax.ppermute(swapped[n], "ex", even_ahead) for n in chunks]

    pairs = []
    for blocks in (own, two_back, swapped):
        send, kept = partial_scores(store, list(enumerate(blocks)))
        pairs.append((kept, lax.ppermute(send, "dim", over_dim)))
    carry = partial_scores(store, list(enumerate(odd_one_back)))
    for n in chunks:
        carry = partial_scores(store, [(n, even_three_back[n])], (carry[0], carry[1]))
    pairs.append((carry[1], lax.ppermute(carry[0], "dim", over_dim)))
    return finish(valid_rows, pairs, ((0, 0), (2, 2), (1, 3), (3, 1)))


def solution(mesh):
    return jax.shard_map(
        shards,
        mesh=mesh,
        in_specs=(
            P(("groups", "ex"), "dim"),
            P(("groups", "ex"), "dim"),
            P("dim"),
            P(("groups", "ex"), None),
            P(("groups", "ex")),
        ),
        out_specs=P(("groups", "ex", "dim"), None),
        check_vma=False,
    )
```

```python
import functools

import jax
import jax.numpy as jnp
from jax import lax
from jax.experimental import pallas as pl
from jax.experimental.pallas import tpu as pltpu
from jax.sharding import PartitionSpec as P

STEPS = 4
CHUNKS = 2
VMEM_BYTES = 16 * 1024 * 1024


def params():
    return pltpu.CompilerParams(vmem_limit_bytes=VMEM_BYTES)


def whole_spec():
    return pl.BlockSpec(memory_space=pltpu.VMEM)


def far_spec():
    return pl.BlockSpec(memory_space=pltpu.HBM)


def prepare_kernel(queries, precond, rank, *refs):
    chunks, (held, scale, places, ready, arrived, left) = refs[:CHUNKS], refs[CHUNKS:]
    rows, width = chunks[0].shape
    cuts = [slice(n * width, (n + 1) * width) for n in range(CHUNKS)]
    loads = [pltpu.make_async_copy(rank, places, arrived.at[CHUNKS])]
    loads.append(pltpu.make_async_copy(precond, scale, arrived.at[CHUNKS + 1]))
    for n, cut in enumerate(cuts):
        loads.append(pltpu.make_async_copy(queries.at[:, cut], held.at[:, cut], arrived.at[n]))
    for load in loads:
        load.start()
    loads[0].wait()
    loads[1].wait()
    positions = lax.broadcasted_iota(jnp.int32, (rows, rows), 0)
    placing = (positions == places[...]).astype(jnp.bfloat16)
    stores = []
    for n, cut in enumerate(cuts):
        loads[2 + n].wait()
        pre = (held[:, cut].astype(jnp.float32) * scale[:, cut]).astype(jnp.bfloat16)
        ready[:, cut] = jnp.dot(placing, pre, preferred_element_type=jnp.float32).astype(jnp.bfloat16)
        stores.append(pltpu.make_async_copy(ready.at[:, cut], chunks[n], left.at[n]))
        stores[n].start()
    for store in stores:
        store.wait()


def prepare(queries, precond, rank):
    rows, depth = queries.shape
    shape = jax.ShapeDtypeStruct((rows, depth // CHUNKS), jnp.bfloat16)
    return pl.pallas_call(
        prepare_kernel,
        out_shape=[shape] * CHUNKS,
        in_specs=[far_spec()] * 3,
        out_specs=[far_spec()] * CHUNKS,
        scratch_shapes=[
            pltpu.VMEM((rows, depth), jnp.bfloat16),
            pltpu.VMEM((1, depth), jnp.float32),
            pltpu.VMEM((1, rows), jnp.int32),
            pltpu.VMEM((rows, depth), jnp.bfloat16),
            pltpu.SemaphoreType.DMA((CHUNKS + 2,)),
            pltpu.SemaphoreType.DMA((CHUNKS,)),
        ],
        compiler_params=params(),
        cost_estimate=pl.CostEstimate(
            flops=2 * rows * rows * depth, bytes_accessed=4 * rows * depth, transcendentals=0
        ),
    )(queries, precond, rank)


def scores_kernel(cuts, carried, *refs):
    store, blocks = refs[0], refs[1:1 + len(cuts)]
    carry = refs[1 + len(cuts):-4]
    send, own, held, arrived = refs[-4:]
    half = send.shape[0]
    me = lax.axis_index("dim")
    loads = [
        pltpu.make_async_copy(block, held.at[n], arrived.at[n]) for n, block in enumerate(blocks)
    ]
    for load in loads:
        load.start()
    for load in loads:
        load.wait()
    for where, out in ((1 - me, send), (me, own)):
        rows = pl.ds(pl.multiple_of(where * half, half), half)
        total = None
        if carried:
            total = (carry[0] if out is send else carry[1])[...]
        for slot, n in enumerate(cuts):
            width = held.shape[2]
            part = lax.dot_general(
                store[rows, n * width:(n + 1) * width],
                held[slot],
                (((1,), (1,)), ((), ())),
                preferred_element_type=jnp.float32,
            )
            total = part if total is None else total + part
        out[...] = total


def partial_scores(store, blocks, carry=()):
    cuts = [n for n, _ in blocks]
    blocks = [block for _, block in blocks]
    rows, (columns, width) = store.shape[0], blocks[0].shape
    shape = jax.ShapeDtypeStruct((rows // 2, columns), jnp.float32)
    depth = len(blocks) * width
    return pl.pallas_call(
        functools.partial(scores_kernel, cuts, bool(carry)),
        out_shape=[shape] * 2,
        in_specs=[whole_spec()] + [far_spec()] * len(blocks) + [whole_spec()] * len(carry),
        out_specs=[whole_spec()] * 2,
        scratch_shapes=[
            pltpu.VMEM((len(blocks), columns, width), jnp.bfloat16),
            pltpu.SemaphoreType.DMA((len(blocks),)),
        ],
        compiler_params=params(),
        cost_estimate=pl.CostEstimate(
            flops=2 * rows * columns * depth,
            bytes_accessed=2 * (rows + columns) * depth + 4 * rows * columns,
            transcendentals=0,
        ),
    )(store, *blocks, *carry)


def finish_kernel(places, valid, *refs):
    out = refs[-1]
    half, columns = refs[0].shape
    me = lax.axis_index("dim")
    odd = lax.rem(lax.axis_index("ex"), 2)
    row_ids = lax.broadcasted_iota(jnp.int32, (half, columns), 0) + me * half
    keep = row_ids < valid[0]
    for n, place in enumerate(places):
        step = place[0] + odd * (place[1] - place[0])
        total = refs[2 * n][...] + refs[2 * n + 1][...]
        out[:, pl.ds(pl.multiple_of(step * columns, columns), columns)] = jnp.where(keep, total, 0.0)


def finish(valid, pairs, places):
    half, columns = pairs[0][0].shape
    operands = [ref for pair in pairs for ref in pair]
    return pl.pallas_call(
        functools.partial(finish_kernel, places),
        out_shape=jax.ShapeDtypeStruct((half, columns * len(pairs)), jnp.float32),
        in_specs=[pl.BlockSpec(memory_space=pltpu.SMEM)] + [whole_spec()] * len(operands),
        out_specs=whole_spec(),
        compiler_params=params(),
        cost_estimate=pl.CostEstimate(
            flops=half * columns * len(pairs),
            bytes_accessed=12 * half * columns * len(pairs),
            transcendentals=0,
        ),
    )(valid, *operands)


def shards(store, queries, precond, query_rank, valid_rows):
    size = lax.axis_size("ex")
    ahead = [(i, (i + 2) % size) for i in range(size)]
    swap = [(i, i ^ 1) for i in range(size)]
    to_odd = [(i, i + 1) for i in range(0, size, 2)]
    even_ahead = [(i, (i + 2) % size) for i in range(0, size, 2)]
    over_dim = [(0, 1), (1, 0)]

    own = prepare(queries, precond[None, :], query_rank)
    chunks = range(CHUNKS)
    two_back = [lax.ppermute(own[n], "ex", ahead) for n in chunks]
    odd_one_back = [lax.ppermute(own[n], "ex", to_odd) for n in chunks]
    swapped = [lax.ppermute(two_back[n], "ex", swap) for n in chunks]
    even_three_back = [lax.ppermute(swapped[n], "ex", even_ahead) for n in chunks]

    pairs = []
    for blocks in (own, two_back, swapped):
        send, kept = partial_scores(store, list(enumerate(blocks)))
        pairs.append((kept, lax.ppermute(send, "dim", over_dim)))
    carry = partial_scores(store, list(enumerate(odd_one_back)))
    for n in chunks:
        carry = partial_scores(store, [(n, even_three_back[n])], (carry[0], carry[1]))
    pairs.append((carry[1], lax.ppermute(carry[0], "dim", over_dim)))
    return finish(valid_rows, pairs, ((0, 0), (2, 2), (1, 3), (3, 1)))


def solution(mesh):
    return jax.shard_map(
        shards,
        mesh=mesh,
        in_specs=(
            P(("groups", "ex"), "dim"),
            P(("groups", "ex"), "dim"),
            P("dim"),
            P(("groups", "ex"), None),
            P(("groups", "ex")),
        ),
        out_specs=P(("groups", "ex", "dim"), None),
        check_vma=False,
    )
```

```python
import functools

import jax
import jax.numpy as jnp
from jax import lax
from jax.experimental import pallas as pl
from jax.experimental.pallas import tpu as pltpu
from jax.sharding import PartitionSpec as P

STEPS = 4
CHUNKS = 2
VMEM_BYTES = 16 * 1024 * 1024


def params():
    return pltpu.CompilerParams(vmem_limit_bytes=VMEM_BYTES)


def whole_spec():
    return pl.BlockSpec(memory_space=pltpu.VMEM)


def in_hbm(x):
    return pltpu.with_memory_space_constraint(x, pltpu.HBM)


def prepare_kernel(queries, precond, rank, *refs):
    chunks, (held, scale, places, arrived) = refs[:CHUNKS], refs[CHUNKS:]
    rows, width = chunks[0].shape
    cuts = [slice(n * width, (n + 1) * width) for n in range(CHUNKS)]
    loads = [pltpu.make_async_copy(rank, places, arrived.at[CHUNKS])]
    loads.append(pltpu.make_async_copy(precond, scale, arrived.at[CHUNKS + 1]))
    for n, cut in enumerate(cuts):
        loads.append(pltpu.make_async_copy(queries.at[:, cut], held.at[:, cut], arrived.at[n]))
    for load in loads:
        load.start()
    loads[0].wait()
    loads[1].wait()
    positions = lax.broadcasted_iota(jnp.int32, (rows, rows), 0)
    placing = (positions == places[...]).astype(jnp.bfloat16)
    for n, cut in enumerate(cuts):
        loads[2 + n].wait()
        pre = (held[:, cut].astype(jnp.float32) * scale[:, cut]).astype(jnp.bfloat16)
        chunks[n][...] = jnp.dot(placing, pre, preferred_element_type=jnp.float32).astype(
            jnp.bfloat16
        )


def prepare(queries, precond, rank):
    rows, depth = queries.shape
    shape = jax.ShapeDtypeStruct((rows, depth // CHUNKS), jnp.bfloat16)
    queries, precond, rank = [in_hbm(x) for x in (queries, precond, rank)]
    return pl.pallas_call(
        prepare_kernel,
        out_shape=[shape] * CHUNKS,
        in_specs=[pl.BlockSpec(memory_space=pltpu.HBM)] * 3,
        out_specs=[whole_spec()] * CHUNKS,
        scratch_shapes=[
            pltpu.VMEM((rows, depth), jnp.bfloat16),
            pltpu.VMEM((1, depth), jnp.float32),
            pltpu.VMEM((1, rows), jnp.int32),
            pltpu.SemaphoreType.DMA((CHUNKS + 2,)),
        ],
        compiler_params=params(),
        cost_estimate=pl.CostEstimate(
            flops=2 * rows * rows * depth, bytes_accessed=4 * rows * depth, transcendentals=0
        ),
    )(queries, precond, rank)


def scores_kernel(cuts, carried, *refs):
    store, blocks = refs[0], refs[1:1 + len(cuts)]
    carry = refs[1 + len(cuts):-2]
    send, own = refs[-2:]
    half = send.shape[0]
    me = lax.axis_index("dim")
    for where, out in ((1 - me, send), (me, own)):
        rows = pl.ds(pl.multiple_of(where * half, half), half)
        total = None
        if carried:
            total = (carry[0] if out is send else carry[1])[...]
        for n, block in zip(cuts, blocks):
            width = block.shape[1]
            part = lax.dot_general(
                store[rows, n * width:(n + 1) * width],
                block[...],
                (((1,), (1,)), ((), ())),
                preferred_element_type=jnp.float32,
            )
            total = part if total is None else total + part
        out[...] = total


def partial_scores(store, blocks, carry=()):
    cuts = [n for n, _ in blocks]
    blocks = [block for _, block in blocks]
    rows, columns = store.shape[0], blocks[0].shape[0]
    shape = jax.ShapeDtypeStruct((rows // 2, columns), jnp.float32)
    operands = [store, *blocks, *carry]
    depth = sum(block.shape[1] for block in blocks)
    return pl.pallas_call(
        functools.partial(scores_kernel, cuts, bool(carry)),
        out_shape=[shape] * 2,
        in_specs=[whole_spec()] * len(operands),
        out_specs=[whole_spec()] * 2,
        compiler_params=params(),
        cost_estimate=pl.CostEstimate(
            flops=2 * rows * columns * depth,
            bytes_accessed=2 * (rows + columns) * depth + 4 * rows * columns,
            transcendentals=0,
        ),
    )(*operands)


def finish_kernel(valid, *refs):
    out = refs[-1]
    half, columns = refs[0].shape
    row_ids = lax.broadcasted_iota(jnp.int32, (half, columns), 0) + lax.axis_index("dim") * half
    keep = row_ids < valid[0]
    for n in range(len(refs) // 2):
        total = refs[2 * n][...] + refs[2 * n + 1][...]
        out[:, n * columns:(n + 1) * columns] = jnp.where(keep, total, 0.0)


def finish(valid, pairs):
    half, columns = pairs[0][0].shape
    operands = [ref for pair in pairs for ref in pair]
    return pl.pallas_call(
        finish_kernel,
        out_shape=jax.ShapeDtypeStruct((half, columns * len(pairs)), jnp.float32),
        in_specs=[pl.BlockSpec(memory_space=pltpu.SMEM)] + [whole_spec()] * len(operands),
        out_specs=whole_spec(),
        compiler_params=params(),
        cost_estimate=pl.CostEstimate(
            flops=half * columns * len(pairs),
            bytes_accessed=12 * half * columns * len(pairs),
            transcendentals=0,
        ),
    )(valid, *operands)


def after(x, *earlier):
    return lax.optimization_barrier((x, *earlier))[0]


def shards(store, queries, precond, query_rank, valid_rows):
    size = lax.axis_size("ex")
    odd = lax.rem(lax.axis_index("ex"), 2) == 1
    ahead = [(i, (i + 2) % size) for i in range(size)]
    swap = [(i, i ^ 1) for i in range(size)]
    over_dim = [(0, 1), (1, 0)]

    own = prepare(queries, precond[None, :], query_rank)
    two_back, one_back, three_back = [], [], []
    for n in range(CHUNKS):
        block = after(own[n], *two_back)
        two_back.append(lax.ppermute(block, "ex", ahead))
    for n in range(CHUNKS):
        one_back.append(lax.ppermute(jnp.where(odd, two_back[n], own[n]), "ex", swap))
    for n in range(CHUNKS):
        block = after(one_back[n], *two_back, *three_back)
        three_back.append(lax.ppermute(block, "ex", ahead))

    pairs = []
    for blocks in (own, one_back, two_back):
        send, kept = partial_scores(store, list(enumerate(blocks)))
        pairs.append((kept, lax.ppermute(send, "dim", over_dim)))
    carry = ()
    for n in range(CHUNKS):
        carry = partial_scores(store, [(n, three_back[n])], carry)
    pairs.append((carry[1], lax.ppermute(carry[0], "dim", over_dim)))
    return finish(valid_rows, pairs)


def solution(mesh):
    return jax.shard_map(
        shards,
        mesh=mesh,
        in_specs=(
            P(("groups", "ex"), "dim"),
            P(("groups", "ex"), "dim"),
            P("dim"),
            P(("groups", "ex"), None),
            P(("groups", "ex")),
        ),
        out_specs=P(("groups", "ex", "dim"), None),
        check_vma=False,
    )
```

```python
import functools

import jax
import jax.numpy as jnp
from jax import lax
from jax.experimental import pallas as pl
from jax.experimental.pallas import tpu as pltpu
from jax.sharding import PartitionSpec as P

STEPS = 4
PARTS = (4, 4, 4, 4)
CHUNKS = len(PARTS)
VMEM_BYTES = 16 * 1024 * 1024


def params():
    return pltpu.CompilerParams(vmem_limit_bytes=VMEM_BYTES)


def whole_spec():
    return pl.BlockSpec(memory_space=pltpu.VMEM)


def in_hbm(x):
    return pltpu.with_memory_space_constraint(x, pltpu.HBM)


def cuts_of(depth):
    ends = [depth * sum(PARTS[:n + 1]) // sum(PARTS) for n in range(CHUNKS)]
    return [slice(start, end) for start, end in zip([0] + ends, ends)]


def prepare_kernel(queries, precond, rank, *refs):
    chunks, (held, scale, places, arrived) = refs[:CHUNKS], refs[CHUNKS:]
    rows, depth = queries.shape
    cuts = cuts_of(depth)
    loads = [pltpu.make_async_copy(rank, places, arrived.at[CHUNKS])]
    loads.append(pltpu.make_async_copy(precond, scale, arrived.at[CHUNKS + 1]))
    for n, cut in enumerate(cuts):
        loads.append(pltpu.make_async_copy(queries.at[:, cut], held.at[:, cut], arrived.at[n]))
    for load in loads:
        load.start()
    loads[0].wait()
    loads[1].wait()
    positions = lax.broadcasted_iota(jnp.int32, (rows, rows), 0)
    placing = (positions == places[...]).astype(jnp.bfloat16)
    for n, cut in enumerate(cuts):
        loads[2 + n].wait()
        pre = (held[:, cut].astype(jnp.float32) * scale[:, cut]).astype(jnp.bfloat16)
        chunks[n][...] = jnp.dot(placing, pre, preferred_element_type=jnp.float32).astype(
            jnp.bfloat16
        )


def prepare(queries, precond, rank):
    rows, depth = queries.shape
    shapes = [
        jax.ShapeDtypeStruct((rows, cut.stop - cut.start), jnp.bfloat16) for cut in cuts_of(depth)
    ]
    queries, precond, rank = [in_hbm(x) for x in (queries, precond, rank)]
    return pl.pallas_call(
        prepare_kernel,
        out_shape=shapes,
        in_specs=[pl.BlockSpec(memory_space=pltpu.HBM)] * 3,
        out_specs=[whole_spec()] * CHUNKS,
        scratch_shapes=[
            pltpu.VMEM((rows, depth), jnp.bfloat16),
            pltpu.VMEM((1, depth), jnp.float32),
            pltpu.VMEM((1, rows), jnp.int32),
            pltpu.SemaphoreType.DMA((CHUNKS + 2,)),
        ],
        compiler_params=params(),
        cost_estimate=pl.CostEstimate(
            flops=2 * rows * rows * depth, bytes_accessed=4 * rows * depth, transcendentals=0
        ),
    )(queries, precond, rank)


def scores_kernel(cuts, carried, *refs):
    store, blocks = refs[0], refs[1:1 + len(cuts)]
    carry = refs[1 + len(cuts):-2]
    send, own = refs[-2:]
    half = send.shape[0]
    me = lax.axis_index("dim")
    for where, out in ((1 - me, send), (me, own)):
        rows = pl.ds(pl.multiple_of(where * half, half), half)
        total = None
        if carried:
            total = (carry[0] if out is send else carry[1])[...]
        for n, block in zip(cuts, blocks):
            part = lax.dot_general(
                store[rows, cuts_of(store.shape[1])[n]],
                block[...],
                (((1,), (1,)), ((), ())),
                preferred_element_type=jnp.float32,
            )
            total = part if total is None else total + part
        out[...] = total


def partial_scores(store, blocks, carry=()):
    cuts = [n for n, _ in blocks]
    blocks = [block for _, block in blocks]
    rows, columns = store.shape[0], blocks[0].shape[0]
    shape = jax.ShapeDtypeStruct((rows // 2, columns), jnp.float32)
    operands = [store, *blocks, *carry]
    depth = sum(block.shape[1] for block in blocks)
    return pl.pallas_call(
        functools.partial(scores_kernel, cuts, bool(carry)),
        out_shape=[shape] * 2,
        in_specs=[whole_spec()] * len(operands),
        out_specs=[whole_spec()] * 2,
        compiler_params=params(),
        cost_estimate=pl.CostEstimate(
            flops=2 * rows * columns * depth,
            bytes_accessed=2 * (rows + columns) * depth + 4 * rows * columns,
            transcendentals=0,
        ),
    )(*operands)


def finish_kernel(valid, *refs):
    out = refs[-1]
    half, columns = refs[0].shape
    row_ids = lax.broadcasted_iota(jnp.int32, (half, columns), 0) + lax.axis_index("dim") * half
    keep = row_ids < valid[0]
    for n in range(len(refs) // 2):
        total = refs[2 * n][...] + refs[2 * n + 1][...]
        out[:, n * columns:(n + 1) * columns] = jnp.where(keep, total, 0.0)


def finish(valid, pairs):
    half, columns = pairs[0][0].shape
    operands = [ref for pair in pairs for ref in pair]
    return pl.pallas_call(
        finish_kernel,
        out_shape=jax.ShapeDtypeStruct((half, columns * len(pairs)), jnp.float32),
        in_specs=[pl.BlockSpec(memory_space=pltpu.SMEM)] + [whole_spec()] * len(operands),
        out_specs=whole_spec(),
        compiler_params=params(),
        cost_estimate=pl.CostEstimate(
            flops=half * columns * len(pairs),
            bytes_accessed=12 * half * columns * len(pairs),
            transcendentals=0,
        ),
    )(valid, *operands)


def after(x, *earlier):
    return lax.optimization_barrier((x, *earlier))[0]


def shards(store, queries, precond, query_rank, valid_rows):
    size = lax.axis_size("ex")
    odd = lax.rem(lax.axis_index("ex"), 2) == 1
    ahead = [(i, (i + 2) % size) for i in range(size)]
    swap = [(i, i ^ 1) for i in range(size)]
    over_dim = [(0, 1), (1, 0)]

    own = prepare(queries, precond[None, :], query_rank)
    two_back, one_back, three_back = [], [], []
    for n in range(CHUNKS):
        two_back.append(lax.ppermute(own[n], "ex", ahead))
    for n in range(CHUNKS):
        block = two_back[n]
        if n == CHUNKS - 1:
            block = after(block, one_back[0])
        one_back.append(lax.ppermute(jnp.where(odd, block, own[n]), "ex", swap))
    for n in range(CHUNKS):
        three_back.append(lax.ppermute(one_back[n], "ex", ahead))

    pairs = []
    for blocks in (own, one_back, two_back):
        send, kept = partial_scores(store, list(enumerate(blocks)))
        pairs.append((kept, lax.ppermute(send, "dim", over_dim)))
    carry = ()
    for n in range(CHUNKS):
        carry = partial_scores(store, [(n, three_back[n])], carry)
    pairs.append((carry[1], lax.ppermute(carry[0], "dim", over_dim)))
    return finish(valid_rows, pairs)


def solution(mesh):
    return jax.shard_map(
        shards,
        mesh=mesh,
        in_specs=(
            P(("groups", "ex"), "dim"),
            P(("groups", "ex"), "dim"),
            P("dim"),
            P(("groups", "ex"), None),
            P(("groups", "ex")),
        ),
        out_specs=P(("groups", "ex", "dim"), None),
        check_vma=False,
    )
```

```python
import functools

import jax
import jax.numpy as jnp
from jax import lax
from jax.experimental import pallas as pl
from jax.experimental.pallas import tpu as pltpu
from jax.sharding import PartitionSpec as P

STEPS = 4
PARTS = (5, 5, 6)
CHUNKS = len(PARTS)
VMEM_BYTES = 16 * 1024 * 1024


def params():
    return pltpu.CompilerParams(vmem_limit_bytes=VMEM_BYTES)


def whole_spec():
    return pl.BlockSpec(memory_space=pltpu.VMEM)


def in_hbm(x):
    return pltpu.with_memory_space_constraint(x, pltpu.HBM)


def cuts_of(depth):
    ends = [depth * sum(PARTS[:n + 1]) // sum(PARTS) for n in range(CHUNKS)]
    return [slice(start, end) for start, end in zip([0] + ends, ends)]


def prepare_kernel(queries, precond, rank, *refs):
    own, chunks, (held, scale, places, arrived) = refs[0], refs[1:1 + CHUNKS], refs[1 + CHUNKS:]
    rows, depth = queries.shape
    cuts = cuts_of(depth)
    loads = [pltpu.make_async_copy(rank, places, arrived.at[CHUNKS])]
    loads.append(pltpu.make_async_copy(precond, scale, arrived.at[CHUNKS + 1]))
    for n, cut in enumerate(cuts):
        loads.append(pltpu.make_async_copy(queries.at[:, cut], held.at[:, cut], arrived.at[n]))
    for load in loads:
        load.start()
    loads[0].wait()
    loads[1].wait()
    positions = lax.broadcasted_iota(jnp.int32, (rows, rows), 0)
    placing = (positions == places[...]).astype(jnp.bfloat16)
    for n, cut in enumerate(cuts):
        loads[2 + n].wait()
        pre = (held[:, cut].astype(jnp.float32) * scale[:, cut]).astype(jnp.bfloat16)
        ordered = jnp.dot(placing, pre, preferred_element_type=jnp.float32).astype(jnp.bfloat16)
        own[:, cut] = ordered
        chunks[n][...] = ordered


def prepare(queries, precond, rank):
    rows, depth = queries.shape
    shapes = [jax.ShapeDtypeStruct((rows, depth), jnp.bfloat16)]
    shapes += [
        jax.ShapeDtypeStruct((rows, cut.stop - cut.start), jnp.bfloat16) for cut in cuts_of(depth)
    ]
    queries, precond, rank = [in_hbm(x) for x in (queries, precond, rank)]
    return pl.pallas_call(
        prepare_kernel,
        out_shape=shapes,
        in_specs=[pl.BlockSpec(memory_space=pltpu.HBM)] * 3,
        out_specs=[whole_spec()] * (1 + CHUNKS),
        scratch_shapes=[
            pltpu.VMEM((rows, depth), jnp.bfloat16),
            pltpu.VMEM((1, depth), jnp.float32),
            pltpu.VMEM((1, rows), jnp.int32),
            pltpu.SemaphoreType.DMA((CHUNKS + 2,)),
        ],
        compiler_params=params(),
        cost_estimate=pl.CostEstimate(
            flops=2 * rows * rows * depth, bytes_accessed=4 * rows * depth, transcendentals=0
        ),
    )(queries, precond, rank)


def scores_kernel(pieces, carried, *refs):
    store, (send, own) = refs[0], refs[-2:]
    carry = refs[-4:-2] if carried else (None, None)
    half, depth = send.shape[0], store.shape[1]
    cuts = cuts_of(depth)
    me = lax.axis_index("dim")
    odd = lax.rem(lax.axis_index("ex"), 2) == 1

    def block(place, n):
        ref = refs[1 + place]
        return ref[:, cuts[n]] if ref.shape[1] == depth else ref[...]

    blocks = []
    for n, even_place, odd_place in pieces:
        value = block(even_place, n)
        if odd_place != even_place:
            value = jnp.where(odd, block(odd_place, n), value)
        blocks.append((n, value))
    for where, out, start in ((1 - me, send, carry[0]), (me, own, carry[1])):
        rows = pl.ds(pl.multiple_of(where * half, half), half)
        total = start[...] if carried else None
        for n, value in blocks:
            part = lax.dot_general(
                store[rows, cuts[n]],
                value,
                (((1,), (1,)), ((), ())),
                preferred_element_type=jnp.float32,
            )
            total = part if total is None else total + part
        out[...] = total


def partial_scores(store, pieces, carry=()):
    operands, placed = [], []
    for n, *blocks in pieces:
        places = []
        for block in blocks:
            known = [i for i, operand in enumerate(operands) if operand is block]
            places.append(known[0] if known else len(operands))
            operands += [] if known else [block]
        placed.append((n, places[0], places[-1]))
    (rows, depth), columns = store.shape, operands[0].shape[0]
    depth = sum(cuts_of(depth)[n].stop - cuts_of(depth)[n].start for n, *_ in pieces)
    operands = [store, *operands, *carry]
    shape = jax.ShapeDtypeStruct((rows // 2, columns), jnp.float32)
    return pl.pallas_call(
        functools.partial(scores_kernel, tuple(placed), bool(carry)),
        out_shape=[shape] * 2,
        in_specs=[whole_spec()] * len(operands),
        out_specs=[whole_spec()] * 2,
        compiler_params=params(),
        cost_estimate=pl.CostEstimate(
            flops=2 * rows * columns * depth,
            bytes_accessed=2 * (rows + columns) * depth + 4 * rows * columns,
            transcendentals=0,
        ),
    )(*operands)


def finish_kernel(valid, *refs):
    out = refs[-1]
    half, columns = refs[0].shape
    row_ids = lax.broadcasted_iota(jnp.int32, (half, columns), 0) + lax.axis_index("dim") * half
    keep = row_ids < valid[0]
    for n in range(len(refs) // 2):
        total = refs[2 * n][...] + refs[2 * n + 1][...]
        out[:, n * columns:(n + 1) * columns] = jnp.where(keep, total, 0.0)


def finish(valid, pairs):
    half, columns = pairs[0][0].shape
    operands = [ref for pair in pairs for ref in pair]
    return pl.pallas_call(
        finish_kernel,
        out_shape=jax.ShapeDtypeStruct((half, columns * len(pairs)), jnp.float32),
        in_specs=[pl.BlockSpec(memory_space=pltpu.SMEM)] + [whole_spec()] * len(operands),
        out_specs=whole_spec(),
        compiler_params=params(),
        cost_estimate=pl.CostEstimate(
            flops=half * columns * len(pairs),
            bytes_accessed=12 * half * columns * len(pairs),
            transcendentals=0,
        ),
    )(valid, *operands)


def after(x, *earlier):
    return lax.optimization_barrier((x, *earlier))[0]


def shards(store, queries, precond, query_rank, valid_rows):
    size = lax.axis_size("ex")
    odd = lax.rem(lax.axis_index("ex"), 2) == 1
    ahead = [(i, (i + 2) % size) for i in range(size)]
    swap = [(i, i ^ 1) for i in range(size)]
    to_odd = [(i, i + 1) for i in range(0, size, 2)]
    to_even = [(i + 1, i) for i in range(0, size, 2)]
    over_dim = [(0, 1), (1, 0)]

    def send(block, route, axis="ex"):
        return lax.ppermute(block, axis, route)

    own, *chunks = prepare(queries, precond[None, :], query_rank)
    cuts = cuts_of(own.shape[1])
    two_back = [send(chunk, ahead) for chunk in chunks]
    odd_one_back = send(own, to_odd)
    even_one_back = [send(block, to_even) for block in two_back]
    up = send(jnp.where(odd, two_back[1], even_one_back[0]), ahead)
    last_up = send(jnp.where(odd, odd_one_back[:, cuts[2]], even_one_back[2]), ahead)
    odd_three_back = send(two_back[0], to_odd)
    across = send(jnp.where(odd, up, two_back[1]), swap)

    every = range(CHUNKS)
    pairs = []
    for pieces in (
        [(n, own) for n in every],
        [(n, even_one_back[n], odd_one_back) for n in every],
        [(n, two_back[n]) for n in every],
    ):
        theirs, ours = partial_scores(store, pieces)
        pairs.append((ours, send(theirs, over_dim, "dim")))
    carry = partial_scores(store, [(0, up, odd_three_back)])
    carry = partial_scores(store, [(1, across)], carry)
    carry = partial_scores(store, [(2, last_up)], carry)
    pairs.append((carry[1], send(carry[0], over_dim, "dim")))
    return finish(valid_rows, pairs)


def solution(mesh):
    return jax.shard_map(
        shards,
        mesh=mesh,
        in_specs=(
            P(("groups", "ex"), "dim"),
            P(("groups", "ex"), "dim"),
            P("dim"),
            P(("groups", "ex"), None),
            P(("groups", "ex")),
        ),
        out_specs=P(("groups", "ex", "dim"), None),
        check_vma=False,
    )
```

```python
import functools

import jax
import jax.numpy as jnp
from jax import lax
from jax.experimental import pallas as pl
from jax.experimental.pallas import tpu as pltpu
from jax.sharding import PartitionSpec as P

STEPS = 4
PARTS = (3, 4, 4, 5)
CHUNKS = len(PARTS)
VMEM_BYTES = 16 * 1024 * 1024


def params():
    return pltpu.CompilerParams(vmem_limit_bytes=VMEM_BYTES)


def whole_spec():
    return pl.BlockSpec(memory_space=pltpu.VMEM)


def in_hbm(x):
    return pltpu.with_memory_space_constraint(x, pltpu.HBM)


def cuts_of(depth):
    ends = [depth * sum(PARTS[:n + 1]) // sum(PARTS) for n in range(CHUNKS)]
    return [slice(start, end) for start, end in zip([0] + ends, ends)]


def prepare_kernel(queries, precond, rank, *refs):
    chunks, (held, scale, places, arrived) = refs[:CHUNKS], refs[CHUNKS:]
    rows, depth = queries.shape
    cuts = cuts_of(depth)
    loads = [pltpu.make_async_copy(rank, places, arrived.at[CHUNKS])]
    loads.append(pltpu.make_async_copy(precond, scale, arrived.at[CHUNKS + 1]))
    for n, cut in enumerate(cuts):
        loads.append(pltpu.make_async_copy(queries.at[:, cut], held.at[:, cut], arrived.at[n]))
    for load in loads:
        load.start()
    loads[0].wait()
    loads[1].wait()
    positions = lax.broadcasted_iota(jnp.int32, (rows, rows), 0)
    placing = (positions == places[...]).astype(jnp.bfloat16)
    for n, cut in enumerate(cuts):
        loads[2 + n].wait()
        pre = (held[:, cut].astype(jnp.float32) * scale[:, cut]).astype(jnp.bfloat16)
        chunks[n][...] = jnp.dot(placing, pre, preferred_element_type=jnp.float32).astype(
            jnp.bfloat16
        )


def prepare(queries, precond, rank):
    rows, depth = queries.shape
    shapes = [
        jax.ShapeDtypeStruct((rows, cut.stop - cut.start), jnp.bfloat16) for cut in cuts_of(depth)
    ]
    queries, precond, rank = [in_hbm(x) for x in (queries, precond, rank)]
    return pl.pallas_call(
        prepare_kernel,
        out_shape=shapes,
        in_specs=[pl.BlockSpec(memory_space=pltpu.HBM)] * 3,
        out_specs=[whole_spec()] * CHUNKS,
        scratch_shapes=[
            pltpu.VMEM((rows, depth), jnp.bfloat16),
            pltpu.VMEM((1, depth), jnp.float32),
            pltpu.VMEM((1, rows), jnp.int32),
            pltpu.SemaphoreType.DMA((CHUNKS + 2,)),
        ],
        compiler_params=params(),
        cost_estimate=pl.CostEstimate(
            flops=2 * rows * rows * depth, bytes_accessed=4 * rows * depth, transcendentals=0
        ),
    )(queries, precond, rank)


def scores_kernel(pieces, carried, *refs):
    store, (send, own) = refs[0], refs[-2:]
    carry = refs[-4:-2] if carried else (None, None)
    half, depth = send.shape[0], store.shape[1]
    cuts = cuts_of(depth)
    me = lax.axis_index("dim")
    odd = lax.rem(lax.axis_index("ex"), 2) == 1

    def block(place, n):
        ref = refs[1 + place]
        return ref[:, cuts[n]] if ref.shape[1] == depth else ref[...]

    blocks = []
    for n, even_place, odd_place in pieces:
        value = block(even_place, n)
        if odd_place != even_place:
            value = jnp.where(odd, block(odd_place, n), value)
        blocks.append((n, value))
    for where, out, start in ((1 - me, send, carry[0]), (me, own, carry[1])):
        rows = pl.ds(pl.multiple_of(where * half, half), half)
        total = start[...] if carried else None
        for n, value in blocks:
            part = lax.dot_general(
                store[rows, cuts[n]],
                value,
                (((1,), (1,)), ((), ())),
                preferred_element_type=jnp.float32,
            )
            total = part if total is None else total + part
        out[...] = total


def partial_scores(store, pieces, carry=()):
    operands, placed = [], []
    for n, *blocks in pieces:
        places = []
        for block in blocks:
            known = [i for i, operand in enumerate(operands) if operand is block]
            places.append(known[0] if known else len(operands))
            operands += [] if known else [block]
        placed.append((n, places[0], places[-1]))
    (rows, depth), columns = store.shape, operands[0].shape[0]
    depth = sum(cuts_of(depth)[n].stop - cuts_of(depth)[n].start for n, *_ in pieces)
    operands = [store, *operands, *carry]
    shape = jax.ShapeDtypeStruct((rows // 2, columns), jnp.float32)
    return pl.pallas_call(
        functools.partial(scores_kernel, tuple(placed), bool(carry)),
        out_shape=[shape] * 2,
        in_specs=[whole_spec()] * len(operands),
        out_specs=[whole_spec()] * 2,
        compiler_params=params(),
        cost_estimate=pl.CostEstimate(
            flops=2 * rows * columns * depth,
            bytes_accessed=2 * (rows + columns) * depth + 4 * rows * columns,
            transcendentals=0,
        ),
    )(*operands)


def finish_kernel(valid, *refs):
    out = refs[-1]
    half, columns = refs[0].shape
    row_ids = lax.broadcasted_iota(jnp.int32, (half, columns), 0) + lax.axis_index("dim") * half
    keep = row_ids < valid[0]
    for n in range(len(refs) // 2):
        total = refs[2 * n][...] + refs[2 * n + 1][...]
        out[:, n * columns:(n + 1) * columns] = jnp.where(keep, total, 0.0)


def finish(valid, pairs):
    half, columns = pairs[0][0].shape
    operands = [ref for pair in pairs for ref in pair]
    return pl.pallas_call(
        finish_kernel,
        out_shape=jax.ShapeDtypeStruct((half, columns * len(pairs)), jnp.float32),
        in_specs=[pl.BlockSpec(memory_space=pltpu.SMEM)] + [whole_spec()] * len(operands),
        out_specs=whole_spec(),
        compiler_params=params(),
        cost_estimate=pl.CostEstimate(
            flops=half * columns * len(pairs),
            bytes_accessed=12 * half * columns * len(pairs),
            transcendentals=0,
        ),
    )(valid, *operands)


def shards(store, queries, precond, query_rank, valid_rows):
    size = lax.axis_size("ex")
    odd = lax.rem(lax.axis_index("ex"), 2) == 1
    one_ahead = [(i, (i + 1) % size) for i in range(size)]
    ahead = [(i, (i + 2) % size) for i in range(size)]
    swap = [(i, i ^ 1) for i in range(size)]
    over_dim = [(0, 1), (1, 0)]

    def send(block, route, axis="ex"):
        return lax.ppermute(block, axis, route)

    own = prepare(queries, precond[None, :], query_rank)
    every, last = range(CHUNKS), CHUNKS - 1
    two_back = [send(own[n], ahead) for n in every]
    one_back = [send(jnp.where(odd, two_back[n], own[n]), swap) for n in every[:last]]
    three_back = [send(one_back[n], ahead) for n in every[:last]]
    direct = send(jnp.where(odd, two_back[last], own[last]), one_ahead)
    swapped = send(two_back[last], swap)
    one_back.append((swapped, direct))
    three_back.append((direct, swapped))

    pairs = []
    for blocks in (own, one_back, two_back):
        theirs, ours = partial_scores(store, pieces_of(blocks))
        pairs.append((ours, send(theirs, over_dim, "dim")))
    carry = ()
    for piece in pieces_of(three_back):
        carry = partial_scores(store, [piece], carry)
    pairs.append((carry[1], send(carry[0], over_dim, "dim")))
    return finish(valid_rows, pairs)


def pieces_of(blocks):
    return [(n, *block) if isinstance(block, tuple) else (n, block) for n, block in enumerate(blocks)]


def solution(mesh):
    return jax.shard_map(
        shards,
        mesh=mesh,
        in_specs=(
            P(("groups", "ex"), "dim"),
            P(("groups", "ex"), "dim"),
            P("dim"),
            P(("groups", "ex"), None),
            P(("groups", "ex")),
        ),
        out_specs=P(("groups", "ex", "dim"), None),
        check_vma=False,
    )
```

```python
import functools

import jax
import jax.numpy as jnp
from jax import lax
from jax.experimental import pallas as pl
from jax.experimental.pallas import tpu as pltpu
from jax.sharding import PartitionSpec as P

STEPS = 4
PARTS = (3, 4, 4, 5)
CHUNKS = len(PARTS)
TILES = 6
VMEM_BYTES = 16 * 1024 * 1024


def params():
    return pltpu.CompilerParams(vmem_limit_bytes=VMEM_BYTES)


def whole_spec():
    return pl.BlockSpec(memory_space=pltpu.VMEM)


def far_spec():
    return pl.BlockSpec(memory_space=pltpu.HBM)


def in_hbm(x):
    return pltpu.with_memory_space_constraint(x, pltpu.HBM)


def cost(flops, traffic):
    return pl.CostEstimate(flops=flops, bytes_accessed=traffic, transcendentals=0)


def cuts_of(depth):
    ends = [depth * sum(PARTS[:n + 1]) // sum(PARTS) for n in range(CHUNKS)]
    return [slice(start, end) for start, end in zip([0] + ends, ends)]


def product(rows, block):
    return lax.dot_general(
        rows, block, (((1,), (1,)), ((), ())), preferred_element_type=jnp.float32
    )


def prepare_kernel(queries, precond, rank, *refs):
    chunks, (held, scale, places, arrived) = refs[:CHUNKS], refs[CHUNKS:]
    rows, depth = queries.shape
    cuts = cuts_of(depth)
    loads = [pltpu.make_async_copy(rank, places, arrived.at[CHUNKS])]
    loads.append(pltpu.make_async_copy(precond, scale, arrived.at[CHUNKS + 1]))
    for n, cut in enumerate(cuts):
        loads.append(pltpu.make_async_copy(queries.at[:, cut], held.at[:, cut], arrived.at[n]))
    for load in loads:
        load.start()
    loads[0].wait()
    loads[1].wait()
    positions = lax.broadcasted_iota(jnp.int32, (rows, rows), 0)
    placing = (positions == places[...]).astype(jnp.bfloat16)
    for n, cut in enumerate(cuts):
        loads[2 + n].wait()
        pre = (held[:, cut].astype(jnp.float32) * scale[:, cut]).astype(jnp.bfloat16)
        chunks[n][...] = jnp.dot(placing, pre, preferred_element_type=jnp.float32).astype(
            jnp.bfloat16
        )


def prepare(queries, precond, rank):
    rows, depth = queries.shape
    shapes = [
        jax.ShapeDtypeStruct((rows, cut.stop - cut.start), jnp.bfloat16) for cut in cuts_of(depth)
    ]
    return pl.pallas_call(
        prepare_kernel,
        out_shape=shapes,
        in_specs=[far_spec()] * 3,
        out_specs=[whole_spec()] * CHUNKS,
        scratch_shapes=[
            pltpu.VMEM((rows, depth), jnp.bfloat16),
            pltpu.VMEM((1, depth), jnp.float32),
            pltpu.VMEM((1, rows), jnp.int32),
            pltpu.SemaphoreType.DMA((CHUNKS + 2,)),
        ],
        compiler_params=params(),
        cost_estimate=cost(2 * rows * rows * depth, 4 * rows * depth),
    )(in_hbm(queries), in_hbm(precond), in_hbm(rank))


def first_kernel(*refs):
    store, blocks, (held, send, own, arrived) = refs[0], refs[1:-4], refs[-4:]
    rows, depth = store.shape
    half, tile = rows // 2, rows // TILES
    cuts = cuts_of(depth)
    me = lax.axis_index("dim")
    loads, outs = [], []
    for n in range(TILES):
        out, where = (send, 1 - me) if n < TILES // 2 else (own, me)
        within = pl.ds(n % (TILES // 2) * tile, tile)
        place = pl.ds(pl.multiple_of(where * half + n % (TILES // 2) * tile, tile), tile)
        loads.append(pltpu.make_async_copy(store.at[place], held.at[place], arrived.at[n]))
        loads[n].start()
        outs.append((out, within, place))
    for n, (out, within, place) in enumerate(outs):
        loads[n].wait()
        total = None
        for cut, block in zip(cuts, blocks):
            part = product(held[place, cut], block[...])
            total = part if total is None else total + part
        out[within] = total


def first_scores(store, blocks):
    (rows, depth), columns = store.shape, blocks[0].shape[0]
    shape = jax.ShapeDtypeStruct((rows // 2, columns), jnp.float32)
    return pl.pallas_call(
        first_kernel,
        out_shape=[jax.ShapeDtypeStruct(store.shape, store.dtype), shape, shape],
        in_specs=[far_spec()] + [whole_spec()] * len(blocks),
        out_specs=[whole_spec()] * 3,
        scratch_shapes=[pltpu.SemaphoreType.DMA((TILES,))],
        compiler_params=params(),
        cost_estimate=cost(2 * rows * columns * depth, 2 * (rows + columns) * depth),
    )(in_hbm(store), *blocks)


def scores_kernel(pieces, fresh, *refs):
    count = len(fresh)
    store, outs = refs[0], refs[-2 * count:]
    carried = refs[-2 * count - 2 * (count - sum(fresh)):-2 * count]
    half = outs[0].shape[0]
    cuts = cuts_of(store.shape[1])
    me = lax.axis_index("dim")
    odd = lax.rem(lax.axis_index("ex"), 2) == 1
    sums = {}
    for side, where in enumerate((1 - me, me)):
        rows = pl.ds(pl.multiple_of(where * half, half), half)
        at = 0
        for i, new in enumerate(fresh):
            if not new:
                sums[i] = carried[at + side][...]
                at += 2
            else:
                sums[i] = None
        for n, targets in pieces:
            values = []
            for _, even_place, odd_place in targets:
                value = refs[1 + even_place][...]
                if odd_place != even_place:
                    value = jnp.where(odd, refs[1 + odd_place][...], value)
                values.append(value)
            columns = values[0].shape[0]
            stacked = values[0] if len(values) == 1 else jnp.concatenate(values, axis=0)
            part = product(store[rows, cuts[n]], stacked)
            for k, (i, _, _) in enumerate(targets):
                mine = part[:, k * columns:(k + 1) * columns]
                sums[i] = mine if sums[i] is None else sums[i] + mine
        for i in range(count):
            outs[2 * i + side][...] = sums[i]


def more_scores(store, pieces, carries):
    operands, placed = [], []

    def place(block):
        known = [i for i, operand in enumerate(operands) if operand is block]
        if not known:
            operands.append(block)
        return known[0] if known else len(operands) - 1

    (rows, depth), flops, traffic = store.shape, 0, 0
    for n, targets in pieces:
        kept = []
        for which, *blocks in targets:
            places = [place(block) for block in blocks]
            kept.append((which, places[0], places[-1]))
            flops += 2 * rows * blocks[0].size
        placed.append((n, tuple(kept)))
        traffic += 2 * rows * blocks[0].shape[1]
    columns = operands[0].shape[0]
    fresh = tuple(carry is None for carry in carries)
    operands = [store, *operands, *(half for carry in carries if carry for half in carry)]
    shape = jax.ShapeDtypeStruct((rows // 2, columns), jnp.float32)
    outs = pl.pallas_call(
        functools.partial(scores_kernel, tuple(placed), fresh),
        out_shape=[shape] * (2 * len(carries)),
        in_specs=[whole_spec()] * len(operands),
        out_specs=[whole_spec()] * (2 * len(carries)),
        compiler_params=params(),
        cost_estimate=cost(flops, traffic + 4 * rows * columns * len(carries)),
    )(*operands)
    return [(outs[2 * i], outs[2 * i + 1]) for i in range(len(carries))]


def finish_kernel(places, valid, *refs):
    out, summed, left = refs[-3:]
    half, columns = refs[0].shape
    row_ids = lax.broadcasted_iota(jnp.int32, (half, columns), 0) + lax.axis_index("dim") * half
    keep = row_ids < valid[0]
    stores = []
    for n, place in enumerate(places):
        cut = slice(n * columns, (n + 1) * columns)
        summed[:, cut] = jnp.where(keep, refs[2 * n][...] + refs[2 * n + 1][...], 0.0)
        to = out.at[:, place * columns:(place + 1) * columns]
        stores.append(pltpu.make_async_copy(summed.at[:, cut], to, left.at[n]))
        stores[n].start()
    for store in stores:
        store.wait()


def finish(valid, pairs, places, steps, out=None):
    half, columns = pairs[0][0].shape
    operands = [ref for pair in pairs for ref in pair]
    given = [] if out is None else [in_hbm(out)]
    return pl.pallas_call(
        functools.partial(finish_kernel, places),
        out_shape=pltpu.HBM((half, columns * steps), jnp.float32),
        in_specs=[pl.BlockSpec(memory_space=pltpu.SMEM)]
        + [whole_spec()] * len(operands)
        + [far_spec()] * len(given),
        out_specs=far_spec(),
        scratch_shapes=[
            pltpu.VMEM((half, columns * len(places)), jnp.float32),
            pltpu.SemaphoreType.DMA((len(places),)),
        ],
        input_output_aliases={1 + len(operands): 0} if given else {},
        compiler_params=params(),
        cost_estimate=cost(half * columns * len(pairs), 12 * half * columns * len(pairs)),
    )(valid, *operands, *given)


def after(x, *earlier):
    return lax.optimization_barrier((x, *earlier))[0]


def shards(store, queries, precond, query_rank, valid_rows):
    size = lax.axis_size("ex")
    odd = lax.rem(lax.axis_index("ex"), 2) == 1
    one_ahead = [(i, (i + 1) % size) for i in range(size)]
    ahead = [(i, (i + 2) % size) for i in range(size)]
    swap = [(i, i ^ 1) for i in range(size)]
    over_dim = [(0, 1), (1, 0)]

    def send(block, route, axis="ex"):
        return lax.ppermute(block, axis, route)

    def exchanged(total):
        theirs, ours = total
        return ours, send(theirs, over_dim, "dim")

    own = prepare(queries, precond[None, :], query_rank)
    every, last = range(CHUNKS), CHUNKS - 1
    two_back = [send(own[n], ahead) for n in every]
    store, *own_total = first_scores(store, own)
    own_pair = exchanged(own_total)

    blocks = [after(two_back[0], own_total[0]), *two_back[1:]]
    one_back = [send(jnp.where(odd, blocks[n], own[n]), swap) for n in every[:last]]
    three_back = [send(one_back[n], ahead) for n in every[:last]]
    direct = send(jnp.where(odd, two_back[last], own[last]), one_ahead)
    swapped = send(two_back[last], swap)

    two, one = more_scores(
        store,
        [(n, [(0, two_back[n]), (1, one_back[n])]) for n in every[:last]]
        + [(last, [(0, two_back[last])])],
        [None, None],
    )
    two_pair = exchanged(two)
    one, three = more_scores(
        store, [(last, [(0, swapped, direct), (1, direct, swapped)])], [one, None]
    )
    one_pair = exchanged(one)
    out = finish(valid_rows, [own_pair, one_pair, two_pair], (0, 1, 2), STEPS)
    [three] = more_scores(store, [(n, [(0, three_back[n])]) for n in every[:last - 1]], [three])
    [three] = more_scores(store, [(last - 1, [(0, three_back[last - 1])])], [three])
    return finish(valid_rows, [exchanged(three)], (3,), STEPS, out)


def solution(mesh):
    return jax.shard_map(
        shards,
        mesh=mesh,
        in_specs=(
            P(("groups", "ex"), "dim"),
            P(("groups", "ex"), "dim"),
            P("dim"),
            P(("groups", "ex"), None),
            P(("groups", "ex")),
        ),
        out_specs=P(("groups", "ex", "dim"), None),
        check_vma=False,
    )
```

```python
import functools

import jax
import jax.numpy as jnp
from jax import lax
from jax.experimental import pallas as pl
from jax.experimental.pallas import tpu as pltpu
from jax.sharding import PartitionSpec as P

STEPS = 4
PARTS = (3, 4, 4, 5)
CHUNKS = len(PARTS)
TILES = 2
VMEM_BYTES = 16 * 1024 * 1024


def params():
    return pltpu.CompilerParams(vmem_limit_bytes=VMEM_BYTES)


def whole_spec():
    return pl.BlockSpec(memory_space=pltpu.VMEM)


def far_spec():
    return pl.BlockSpec(memory_space=pltpu.HBM)


def in_hbm(x):
    return pltpu.with_memory_space_constraint(x, pltpu.HBM)


def cost(flops, traffic):
    return pl.CostEstimate(flops=flops, bytes_accessed=traffic, transcendentals=0)


def cuts_of(depth):
    ends = [depth * sum(PARTS[:n + 1]) // sum(PARTS) for n in range(CHUNKS)]
    return [slice(start, end) for start, end in zip([0] + ends, ends)]


def product(rows, block):
    return lax.dot_general(
        rows, block, (((1,), (1,)), ((), ())), preferred_element_type=jnp.float32
    )


def prepare_kernel(queries, precond, rank, *refs):
    chunks, (held, scale, places, arrived) = refs[:CHUNKS], refs[CHUNKS:]
    rows, depth = queries.shape
    cuts = cuts_of(depth)
    loads = [pltpu.make_async_copy(rank, places, arrived.at[CHUNKS])]
    loads.append(pltpu.make_async_copy(precond, scale, arrived.at[CHUNKS + 1]))
    for n, cut in enumerate(cuts):
        loads.append(pltpu.make_async_copy(queries.at[:, cut], held.at[:, cut], arrived.at[n]))
    for load in loads:
        load.start()
    loads[0].wait()
    loads[1].wait()
    positions = lax.broadcasted_iota(jnp.int32, (rows, rows), 0)
    placing = (positions == places[...]).astype(jnp.bfloat16)
    for n, cut in enumerate(cuts):
        loads[2 + n].wait()
        pre = (held[:, cut].astype(jnp.float32) * scale[:, cut]).astype(jnp.bfloat16)
        chunks[n][...] = jnp.dot(placing, pre, preferred_element_type=jnp.float32).astype(
            jnp.bfloat16
        )


def prepare(queries, precond, rank):
    rows, depth = queries.shape
    shapes = [
        jax.ShapeDtypeStruct((rows, cut.stop - cut.start), jnp.bfloat16) for cut in cuts_of(depth)
    ]
    return pl.pallas_call(
        prepare_kernel,
        out_shape=shapes,
        in_specs=[far_spec()] * 3,
        out_specs=[whole_spec()] * CHUNKS,
        scratch_shapes=[
            pltpu.VMEM((rows, depth), jnp.bfloat16),
            pltpu.VMEM((1, depth), jnp.float32),
            pltpu.VMEM((1, rows), jnp.int32),
            pltpu.SemaphoreType.DMA((CHUNKS + 2,)),
        ],
        compiler_params=params(),
        cost_estimate=cost(2 * rows * rows * depth, 4 * rows * depth),
    )(in_hbm(queries), in_hbm(precond), in_hbm(rank))


def first_kernel(*refs):
    store, valid, blocks, (held, keep, send, own, count, arrived) = refs[0], refs[1], refs[2:-6], refs[-6:]
    rows, depth = store.shape
    half, tile = rows // 2, rows // TILES
    cuts = cuts_of(depth)
    me = lax.axis_index("dim")
    counted = pltpu.make_async_copy(valid, count, arrived.at[TILES])
    counted.start()
    loads, outs = [], []
    for n in range(TILES):
        out, where = (send, 1 - me) if n < TILES // 2 else (own, me)
        within = pl.ds(n % (TILES // 2) * tile, tile)
        place = pl.ds(pl.multiple_of(where * half + n % (TILES // 2) * tile, tile), tile)
        loads.append(pltpu.make_async_copy(store.at[place], held.at[place], arrived.at[n]))
        loads[n].start()
        outs.append((out, within, place))
    counted.wait()
    row_ids = lax.broadcasted_iota(jnp.int32, keep.shape, 0) + me * half
    keep[...] = (row_ids < count[0]).astype(jnp.float32)
    for n, (out, within, place) in enumerate(outs):
        loads[n].wait()
        total = None
        for cut, block in zip(cuts, blocks):
            part = product(held[place, cut], block[...])
            total = part if total is None else total + part
        out[within] = total


def first_scores(store, valid, blocks):
    (rows, depth), columns = store.shape, blocks[0].shape[0]
    shape = jax.ShapeDtypeStruct((rows // 2, columns), jnp.float32)
    return pl.pallas_call(
        first_kernel,
        out_shape=[jax.ShapeDtypeStruct(store.shape, store.dtype), shape, shape, shape],
        in_specs=[far_spec()] * 2 + [whole_spec()] * len(blocks),
        out_specs=[whole_spec()] * 4,
        scratch_shapes=[
            pltpu.SMEM((1,), jnp.int32),
            pltpu.SemaphoreType.DMA((TILES + 1,)),
        ],
        compiler_params=params(),
        cost_estimate=cost(2 * rows * columns * depth, 2 * (rows + columns) * depth),
    )(in_hbm(store), valid, *blocks)


def scores_kernel(pieces, fresh, *refs):
    count = len(fresh)
    store, outs = refs[0], refs[-2 * count:]
    carried = refs[-2 * count - 2 * (count - sum(fresh)):-2 * count]
    half = outs[0].shape[0]
    cuts = cuts_of(store.shape[1])
    me = lax.axis_index("dim")
    odd = lax.rem(lax.axis_index("ex"), 2) == 1
    sums = {}
    for side, where in enumerate((1 - me, me)):
        rows = pl.ds(pl.multiple_of(where * half, half), half)
        at = 0
        for i, new in enumerate(fresh):
            if not new:
                sums[i] = carried[at + side][...]
                at += 2
            else:
                sums[i] = None
        for n, targets in pieces:
            values = []
            for _, even_place, odd_place in targets:
                value = refs[1 + even_place][...]
                if odd_place != even_place:
                    value = jnp.where(odd, refs[1 + odd_place][...], value)
                values.append(value)
            columns = values[0].shape[0]
            stacked = values[0] if len(values) == 1 else jnp.concatenate(values, axis=0)
            part = product(store[rows, cuts[n]], stacked)
            for k, (i, _, _) in enumerate(targets):
                mine = part[:, k * columns:(k + 1) * columns]
                sums[i] = mine if sums[i] is None else sums[i] + mine
        for i in range(count):
            outs[2 * i + side][...] = sums[i]


def more_scores(store, pieces, carries):
    operands, placed = [], []

    def place(block):
        known = [i for i, operand in enumerate(operands) if operand is block]
        if not known:
            operands.append(block)
        return known[0] if known else len(operands) - 1

    (rows, depth), flops, traffic = store.shape, 0, 0
    for n, targets in pieces:
        kept = []
        for which, *blocks in targets:
            places = [place(block) for block in blocks]
            kept.append((which, places[0], places[-1]))
            flops += 2 * rows * blocks[0].size
        placed.append((n, tuple(kept)))
        traffic += 2 * rows * blocks[0].shape[1]
    columns = operands[0].shape[0]
    fresh = tuple(carry is None for carry in carries)
    operands = [store, *operands, *(half for carry in carries if carry for half in carry)]
    shape = jax.ShapeDtypeStruct((rows // 2, columns), jnp.float32)
    outs = pl.pallas_call(
        functools.partial(scores_kernel, tuple(placed), fresh),
        out_shape=[shape] * (2 * len(carries)),
        in_specs=[whole_spec()] * len(operands),
        out_specs=[whole_spec()] * (2 * len(carries)),
        compiler_params=params(),
        cost_estimate=cost(flops, traffic + 4 * rows * columns * len(carries)),
    )(*operands)
    return [(outs[2 * i], outs[2 * i + 1]) for i in range(len(carries))]


def finish_kernel(places, keep, *refs):
    out, summed, left = refs[-3:]
    half, columns = refs[0].shape
    inside = keep[...] > 0.5
    stores = []
    for n, place in enumerate(places):
        cut = slice(n * columns, (n + 1) * columns)
        summed[:, cut] = jnp.where(inside, refs[2 * n][...] + refs[2 * n + 1][...], 0.0)
        to = out.at[:, place * columns:(place + 1) * columns]
        stores.append(pltpu.make_async_copy(summed.at[:, cut], to, left.at[n]))
        stores[n].start()
    for store in stores:
        store.wait()


def finish(keep, pairs, places, steps, out=None):
    half, columns = pairs[0][0].shape
    operands = [ref for pair in pairs for ref in pair]
    given = [] if out is None else [in_hbm(out)]
    return pl.pallas_call(
        functools.partial(finish_kernel, places),
        out_shape=pltpu.HBM((half, columns * steps), jnp.float32),
        in_specs=[whole_spec()] * (1 + len(operands))
        + [far_spec()] * len(given),
        out_specs=far_spec(),
        scratch_shapes=[
            pltpu.VMEM((half, columns * len(places)), jnp.float32),
            pltpu.SemaphoreType.DMA((len(places),)),
        ],
        input_output_aliases={1 + len(operands): 0} if given else {},
        compiler_params=params(),
        cost_estimate=cost(half * columns * len(pairs), 12 * half * columns * len(pairs)),
    )(keep, *operands, *given)


def after(x, *earlier):
    return lax.optimization_barrier((x, *earlier))[0]


def shards(store, queries, precond, query_rank, valid_rows):
    size = lax.axis_size("ex")
    odd = lax.rem(lax.axis_index("ex"), 2) == 1
    one_ahead = [(i, (i + 1) % size) for i in range(size)]
    ahead = [(i, (i + 2) % size) for i in range(size)]
    even_ahead = ahead[::2]
    swap = [(i, i ^ 1) for i in range(size)]
    over_dim = [(0, 1), (1, 0)]

    def send(block, route, axis="ex"):
        return lax.ppermute(block, axis, route)

    def exchanged(total):
        theirs, ours = total
        return ours, send(theirs, over_dim, "dim")

    own = prepare(queries, precond[None, :], query_rank)
    two_back = [send(block, ahead) for block in own]
    early = send(own[0], swap)
    store, keep, *own_total = first_scores(store, valid_rows, own)
    own_pair = exchanged(own_total)

    scored = own_total[0]
    swapped = [send(after(two_back[0], scored), swap)]
    swapped += [send(jnp.where(odd, after(two_back[n], scored), own[n]), swap) for n in (1, 2)]
    shifted = [send(swapped[0], even_ahead)] + [send(swapped[n], ahead) for n in (1, 2)]
    direct = send(jnp.where(odd, two_back[3], own[3]), one_ahead)
    swapped.append(send(two_back[3], swap))

    two, one = more_scores(
        store,
        [
            (0, [(0, two_back[0]), (1, swapped[0], early)]),
            (1, [(0, two_back[1]), (1, swapped[1])]),
            (2, [(0, two_back[2]), (1, swapped[2])]),
            (3, [(0, two_back[3])]),
        ],
        [None, None],
    )
    two_pair = exchanged(two)
    one, three = more_scores(
        store, [(3, [(0, swapped[3], direct), (1, direct, swapped[3])])], [one, None]
    )
    one_pair = exchanged(one)
    [three] = more_scores(
        store, [(0, [(0, shifted[0], swapped[0])]), (1, [(0, shifted[1])])], [three]
    )
    out = finish(keep, [own_pair, one_pair, two_pair], (0, 1, 2), STEPS)
    [three] = more_scores(store, [(2, [(0, shifted[2])])], [three])
    return finish(keep, [exchanged(three)], (3,), STEPS, out)


def solution(mesh):
    return jax.shard_map(
        shards,
        mesh=mesh,
        in_specs=(
            P(("groups", "ex"), "dim"),
            P(("groups", "ex"), "dim"),
            P("dim"),
            P(("groups", "ex"), None),
            P(("groups", "ex")),
        ),
        out_specs=P(("groups", "ex", "dim"), None),
        check_vma=False,
    )
```

```python
import functools

import jax
import jax.numpy as jnp
from jax import lax
from jax.experimental import pallas as pl
from jax.experimental.pallas import tpu as pltpu
from jax.sharding import PartitionSpec as P

STEPS = 4
PARTS = (3, 4, 4, 5)
CHUNKS = len(PARTS)
TILES = 2
VMEM_BYTES = 16 * 1024 * 1024


def params():
    return pltpu.CompilerParams(vmem_limit_bytes=VMEM_BYTES)


def whole_spec():
    return pl.BlockSpec(memory_space=pltpu.VMEM)


def far_spec():
    return pl.BlockSpec(memory_space=pltpu.HBM)


def in_hbm(x):
    return pltpu.with_memory_space_constraint(x, pltpu.HBM)


def cost(flops, traffic):
    return pl.CostEstimate(flops=flops, bytes_accessed=traffic, transcendentals=0)


def cuts_of(depth):
    ends = [depth * sum(PARTS[:n + 1]) // sum(PARTS) for n in range(CHUNKS)]
    return [slice(start, end) for start, end in zip([0] + ends, ends)]


def product(rows, block):
    return lax.dot_general(
        rows, block, (((1,), (1,)), ((), ())), preferred_element_type=jnp.float32
    )


def prepare_kernel(queries, precond, rank, *refs):
    chunks, (held, scale, places, arrived) = refs[:CHUNKS], refs[CHUNKS:]
    rows, depth = queries.shape
    cuts = cuts_of(depth)
    loads = [pltpu.make_async_copy(rank, places, arrived.at[CHUNKS])]
    loads.append(pltpu.make_async_copy(precond, scale, arrived.at[CHUNKS + 1]))
    for n, cut in enumerate(cuts):
        loads.append(pltpu.make_async_copy(queries.at[:, cut], held.at[:, cut], arrived.at[n]))
    for load in loads:
        load.start()
    loads[0].wait()
    loads[1].wait()
    positions = lax.broadcasted_iota(jnp.int32, (rows, rows), 0)
    placing = (positions == places[...]).astype(jnp.bfloat16)
    for n, cut in enumerate(cuts):
        loads[2 + n].wait()
        pre = (held[:, cut].astype(jnp.float32) * scale[:, cut]).astype(jnp.bfloat16)
        chunks[n][...] = jnp.dot(placing, pre, preferred_element_type=jnp.float32).astype(
            jnp.bfloat16
        )


def prepare(queries, precond, rank):
    rows, depth = queries.shape
    shapes = [
        jax.ShapeDtypeStruct((rows, cut.stop - cut.start), jnp.bfloat16) for cut in cuts_of(depth)
    ]
    return pl.pallas_call(
        prepare_kernel,
        out_shape=shapes,
        in_specs=[far_spec()] * 3,
        out_specs=[whole_spec()] * CHUNKS,
        scratch_shapes=[
            pltpu.VMEM((rows, depth), jnp.bfloat16),
            pltpu.VMEM((1, depth), jnp.float32),
            pltpu.VMEM((1, rows), jnp.int32),
            pltpu.SemaphoreType.DMA((CHUNKS + 2,)),
        ],
        compiler_params=params(),
        cost_estimate=cost(2 * rows * rows * depth, 4 * rows * depth),
    )(in_hbm(queries), in_hbm(precond), in_hbm(rank))


def first_kernel(*refs):
    store, valid, blocks, (held, keep, send, own, count, arrived) = refs[0], refs[1], refs[2:-6], refs[-6:]
    rows, depth = store.shape
    half, tile = rows // 2, rows // TILES
    cuts = cuts_of(depth)
    me = lax.axis_index("dim")
    counted = pltpu.make_async_copy(valid, count, arrived.at[TILES])
    counted.start()
    loads, outs = [], []
    for n in range(TILES):
        out, where = (send, 1 - me) if n < TILES // 2 else (own, me)
        within = pl.ds(n % (TILES // 2) * tile, tile)
        place = pl.ds(pl.multiple_of(where * half + n % (TILES // 2) * tile, tile), tile)
        loads.append(pltpu.make_async_copy(store.at[place], held.at[place], arrived.at[n]))
        loads[n].start()
        outs.append((out, within, place))
    counted.wait()
    row_ids = lax.broadcasted_iota(jnp.int32, keep.shape, 0) + me * half
    keep[...] = (row_ids < count[0]).astype(jnp.float32)
    for n, (out, within, place) in enumerate(outs):
        loads[n].wait()
        total = None
        for cut, block in zip(cuts, blocks):
            part = product(held[place, cut], block[...])
            total = part if total is None else total + part
        out[within] = total


def first_scores(store, valid, blocks):
    (rows, depth), columns = store.shape, blocks[0].shape[0]
    shape = jax.ShapeDtypeStruct((rows // 2, columns), jnp.float32)
    return pl.pallas_call(
        first_kernel,
        out_shape=[jax.ShapeDtypeStruct(store.shape, store.dtype), shape, shape, shape],
        in_specs=[far_spec()] * 2 + [whole_spec()] * len(blocks),
        out_specs=[whole_spec()] * 4,
        scratch_shapes=[
            pltpu.SMEM((1,), jnp.int32),
            pltpu.SemaphoreType.DMA((TILES + 1,)),
        ],
        compiler_params=params(),
        cost_estimate=cost(2 * rows * columns * depth, 2 * (rows + columns) * depth),
    )(in_hbm(store), valid, *blocks)


def scores_kernel(pieces, fresh, *refs):
    count = len(fresh)
    store, outs = refs[0], refs[-2 * count:]
    carried = refs[-2 * count - 2 * (count - sum(fresh)):-2 * count]
    half = outs[0].shape[0]
    cuts = cuts_of(store.shape[1])
    me = lax.axis_index("dim")
    odd = lax.rem(lax.axis_index("ex"), 2) == 1
    sums = {}
    for side, where in enumerate((1 - me, me)):
        rows = pl.ds(pl.multiple_of(where * half, half), half)
        at = 0
        for i, new in enumerate(fresh):
            if not new:
                sums[i] = carried[at + side][...]
                at += 2
            else:
                sums[i] = None
        for n, targets in pieces:
            values = []
            for _, even_place, odd_place in targets:
                value = refs[1 + even_place][...]
                if odd_place != even_place:
                    value = jnp.where(odd, refs[1 + odd_place][...], value)
                values.append(value)
            columns = values[0].shape[0]
            stacked = values[0] if len(values) == 1 else jnp.concatenate(values, axis=0)
            part = product(store[rows, cuts[n]], stacked)
            for k, (i, _, _) in enumerate(targets):
                mine = part[:, k * columns:(k + 1) * columns]
                sums[i] = mine if sums[i] is None else sums[i] + mine
        for i in range(count):
            outs[2 * i + side][...] = sums[i]


def more_scores(store, pieces, carries):
    operands, placed = [], []

    def place(block):
        known = [i for i, operand in enumerate(operands) if operand is block]
        if not known:
            operands.append(block)
        return known[0] if known else len(operands) - 1

    (rows, depth), flops, traffic = store.shape, 0, 0
    for n, targets in pieces:
        kept = []
        for which, *blocks in targets:
            places = [place(block) for block in blocks]
            kept.append((which, places[0], places[-1]))
            flops += 2 * rows * blocks[0].size
        placed.append((n, tuple(kept)))
        traffic += 2 * rows * blocks[0].shape[1]
    columns = operands[0].shape[0]
    fresh = tuple(carry is None for carry in carries)
    operands = [store, *operands, *(half for carry in carries if carry for half in carry)]
    shape = jax.ShapeDtypeStruct((rows // 2, columns), jnp.float32)
    outs = pl.pallas_call(
        functools.partial(scores_kernel, tuple(placed), fresh),
        out_shape=[shape] * (2 * len(carries)),
        in_specs=[whole_spec()] * len(operands),
        out_specs=[whole_spec()] * (2 * len(carries)),
        compiler_params=params(),
        cost_estimate=cost(flops, traffic + 4 * rows * columns * len(carries)),
    )(*operands)
    return [(outs[2 * i], outs[2 * i + 1]) for i in range(len(carries))]


def finish_kernel(places, keep, *refs):
    out, summed, left = refs[-3:]
    half, columns = refs[0].shape
    inside = keep[...] > 0.5
    stores = []
    for n, place in enumerate(places):
        cut = slice(n * columns, (n + 1) * columns)
        summed[:, cut] = jnp.where(inside, refs[2 * n][...] + refs[2 * n + 1][...], 0.0)
        to = out.at[:, place * columns:(place + 1) * columns]
        stores.append(pltpu.make_async_copy(summed.at[:, cut], to, left.at[n]))
        stores[n].start()
    for store in stores:
        store.wait()


def finish(keep, pairs, places, steps, out=None):
    half, columns = pairs[0][0].shape
    operands = [ref for pair in pairs for ref in pair]
    given = [] if out is None else [in_hbm(out)]
    return pl.pallas_call(
        functools.partial(finish_kernel, places),
        out_shape=pltpu.HBM((half, columns * steps), jnp.float32),
        in_specs=[whole_spec()] * (1 + len(operands))
        + [far_spec()] * len(given),
        out_specs=far_spec(),
        scratch_shapes=[
            pltpu.VMEM((half, columns * len(places)), jnp.float32),
            pltpu.SemaphoreType.DMA((len(places),)),
        ],
        input_output_aliases={1 + len(operands): 0} if given else {},
        compiler_params=params(),
        cost_estimate=cost(half * columns * len(pairs), 12 * half * columns * len(pairs)),
    )(keep, *operands, *given)


def after(x, *earlier):
    return lax.optimization_barrier((x, *earlier))[0]


def shards(store, queries, precond, query_rank, valid_rows):
    size = lax.axis_size("ex")
    odd = lax.rem(lax.axis_index("ex"), 2) == 1
    one_ahead = [(i, (i + 1) % size) for i in range(size)]
    ahead = [(i, (i + 2) % size) for i in range(size)]
    even_ahead = ahead[::2]
    swap = [(i, i ^ 1) for i in range(size)]
    over_dim = [(0, 1), (1, 0)]

    def send(block, route, axis="ex"):
        return lax.ppermute(block, axis, route)

    def exchanged(total):
        theirs, ours = total
        return ours, send(theirs, over_dim, "dim")

    own = prepare(queries, precond[None, :], query_rank)
    two_back = [send(block, ahead) for block in own]
    early = send(own[0], swap)
    store, keep, *own_total = first_scores(store, valid_rows, own)
    own_pair = exchanged(own_total)

    scored = own_total[0]
    swapped = [send(after(two_back[0], scored), swap)]
    swapped += [send(jnp.where(odd, after(two_back[n], scored), own[n]), swap) for n in (1, 2)]
    shifted = [send(swapped[0], even_ahead)] + [send(swapped[n], ahead) for n in (1, 2)]
    direct = send(after(jnp.where(odd, two_back[3], own[3]), shifted[0]), one_ahead)
    swapped.append(send(after(two_back[3], shifted[0]), swap))

    two, one = more_scores(
        store,
        [
            (0, [(0, two_back[0]), (1, swapped[0], early)]),
            (1, [(0, two_back[1]), (1, swapped[1])]),
            (2, [(0, two_back[2]), (1, swapped[2])]),
            (3, [(0, two_back[3])]),
        ],
        [None, None],
    )
    two_pair = exchanged(two)
    [three] = more_scores(store, [(1, [(0, shifted[1])])], [None])
    [three] = more_scores(store, [(0, [(0, shifted[0], swapped[0])])], [three])
    one, three = more_scores(
        store, [(3, [(0, swapped[3], direct), (1, direct, swapped[3])])], [one, three]
    )
    one_pair = exchanged(one)
    out = finish(keep, [own_pair, one_pair, two_pair], (0, 1, 2), STEPS)
    [three] = more_scores(store, [(2, [(0, shifted[2])])], [three])
    return finish(keep, [exchanged(three)], (3,), STEPS, out)


def solution(mesh):
    return jax.shard_map(
        shards,
        mesh=mesh,
        in_specs=(
            P(("groups", "ex"), "dim"),
            P(("groups", "ex"), "dim"),
            P("dim"),
            P(("groups", "ex"), None),
            P(("groups", "ex")),
        ),
        out_specs=P(("groups", "ex", "dim"), None),
        check_vma=False,
    )
```

```python
import functools

import jax
import jax.numpy as jnp
from jax import lax
from jax.experimental import pallas as pl
from jax.experimental.pallas import tpu as pltpu
from jax.sharding import PartitionSpec as P

STEPS = 4
KINDS = "UUUT"
PARTS = (4, 4, 4, 4)
CHAIN = ((0,), (1,), (3,), (2,))
CHUNKS = len(PARTS)
VMEM_BYTES = 16 * 1024 * 1024


def params():
    return pltpu.CompilerParams(vmem_limit_bytes=VMEM_BYTES)


def whole_spec():
    return pl.BlockSpec(memory_space=pltpu.VMEM)


def far_spec():
    return pl.BlockSpec(memory_space=pltpu.HBM)


def in_hbm(x):
    return pltpu.with_memory_space_constraint(x, pltpu.HBM)


def cost(flops, traffic):
    return pl.CostEstimate(flops=flops, bytes_accessed=traffic, transcendentals=0)


def cuts_of(depth):
    ends = [depth * sum(PARTS[:n + 1]) // sum(PARTS) for n in range(CHUNKS)]
    return [slice(start, end) for start, end in zip([0] + ends, ends)]


def product(rows, block):
    return lax.dot_general(
        rows, block, (((1,), (1,)), ((), ())), preferred_element_type=jnp.float32
    )


def prepare_kernel(queries, precond, rank, *refs):
    chunks, (held, scale, places, arrived) = refs[:CHUNKS], refs[CHUNKS:]
    rows, depth = queries.shape
    cuts = cuts_of(depth)
    loads = [pltpu.make_async_copy(rank, places, arrived.at[CHUNKS])]
    loads.append(pltpu.make_async_copy(precond, scale, arrived.at[CHUNKS + 1]))
    for n, cut in enumerate(cuts):
        loads.append(pltpu.make_async_copy(queries.at[:, cut], held.at[:, cut], arrived.at[n]))
    for load in loads:
        load.start()
    loads[0].wait()
    loads[1].wait()
    positions = lax.broadcasted_iota(jnp.int32, (rows, rows), 0)
    placing = (positions == places[...]).astype(jnp.bfloat16)
    for n, cut in enumerate(cuts):
        loads[2 + n].wait()
        pre = (held[:, cut].astype(jnp.float32) * scale[:, cut]).astype(jnp.bfloat16)
        chunks[n][...] = jnp.dot(placing, pre, preferred_element_type=jnp.float32).astype(
            jnp.bfloat16
        )


def prepare(queries, precond, rank):
    rows, depth = queries.shape
    shapes = [
        jax.ShapeDtypeStruct((rows, cut.stop - cut.start), jnp.bfloat16) for cut in cuts_of(depth)
    ]
    return pl.pallas_call(
        prepare_kernel,
        out_shape=shapes,
        in_specs=[far_spec()] * 3,
        out_specs=[whole_spec()] * CHUNKS,
        scratch_shapes=[
            pltpu.VMEM((rows, depth), jnp.bfloat16),
            pltpu.VMEM((1, depth), jnp.float32),
            pltpu.VMEM((1, rows), jnp.int32),
            pltpu.SemaphoreType.DMA((CHUNKS + 2,)),
        ],
        compiler_params=params(),
        cost_estimate=cost(2 * rows * rows * depth, 4 * rows * depth),
    )(in_hbm(queries), in_hbm(precond), in_hbm(rank))


def scores_kernel(pieces, fresh, loading, *refs):
    count = len(fresh)
    odd = lax.rem(lax.axis_index("ex"), 2) == 1
    loads = []
    if loading:
        store, valid, *refs = refs
        *refs, limit, other, mine, arrived = refs
        stores = other, mine
        half = other.shape[0]
        me = lax.axis_index("dim")
        for side, where in enumerate((1 - me, me)):
            place = pl.ds(pl.multiple_of(where * half, half), half)
            loads.append(pltpu.make_async_copy(store.at[place], stores[side], arrived.at[side]))
            loads[side].start()
        limit[...] = jnp.full(limit.shape, valid[0], jnp.int32)
    else:
        other, mine, *refs = refs
        stores = other, mine
    outs = refs[-2 * count:]
    carried = refs[-2 * count - 2 * (count - sum(fresh)):-2 * count]
    cuts = cuts_of(other.shape[1])
    stacks = []
    for n, targets in pieces:
        values = []
        for _, even_place, odd_place in targets:
            value = refs[even_place][...]
            if odd_place != even_place:
                value = jnp.where(odd, refs[odd_place][...], value)
            values.append(value)
        stacked = values[0] if len(values) == 1 else jnp.concatenate(values, axis=0)
        stacks.append((n, [which for which, _, _ in targets], stacked))
    for side, store in enumerate(stores):
        if loading:
            loads[side].wait()
        sums, at = {}, 0
        for i, new in enumerate(fresh):
            sums[i] = None if new else carried[at + side][...]
            at += 0 if new else 2
        for n, whiches, stacked in stacks:
            part = product(store[:, cuts[n]], stacked)
            columns = stacked.shape[0] // len(whiches)
            for k, i in enumerate(whiches):
                here = part[:, k * columns:(k + 1) * columns]
                sums[i] = here if sums[i] is None else sums[i] + here
        for i in range(count):
            outs[2 * i + side][...] = sums[i]


def more_scores(stores, pieces, carries, valid=None):
    operands, placed = [], []

    def place(block):
        known = [i for i, operand in enumerate(operands) if operand is block]
        if not known:
            operands.append(block)
        return known[0] if known else len(operands) - 1

    loading = valid is not None
    half, depth = stores.shape[0] // 2 if loading else stores[0].shape[0], 0
    flops = 0
    for n, targets in pieces:
        kept = []
        for which, *blocks in targets:
            places = [place(block) for block in blocks]
            kept.append((which, places[0], places[-1]))
            flops += 4 * half * blocks[0].size
        placed.append((n, tuple(kept)))
    columns = operands[0].shape[0]
    fresh = tuple(carry is None for carry in carries)
    first = [in_hbm(stores), valid] if loading else list(stores)
    operands += [side for carry in carries if carry for side in carry]
    specs = [far_spec(), pl.BlockSpec(memory_space=pltpu.SMEM)] if loading else [whole_spec()] * 2
    total = jax.ShapeDtypeStruct((half, columns), jnp.float32)
    more = []
    if loading:
        held = jax.ShapeDtypeStruct((half, stores.shape[1]), stores.dtype)
        more = [jax.ShapeDtypeStruct((8, columns), jnp.int32), held, held]
    count = 2 * len(carries)
    outs = pl.pallas_call(
        functools.partial(scores_kernel, tuple(placed), fresh, loading),
        out_shape=[total] * count + more,
        in_specs=specs + [whole_spec()] * len(operands),
        out_specs=[whole_spec()] * (count + len(more)),
        scratch_shapes=[pltpu.SemaphoreType.DMA((2,))] if loading else [],
        compiler_params=params(),
        cost_estimate=cost(flops, 4 * half * columns * count),
    )(*first, *operands)
    totals = [(outs[2 * i], outs[2 * i + 1]) for i in range(len(carries))]
    return totals + ([outs[count], outs[count + 1:]] if loading else [])


def finish_kernel(places, limit, *refs):
    out, summed, left = refs[-3:]
    half, columns = refs[0].shape
    row_ids = lax.broadcasted_iota(jnp.int32, (half, columns), 0) + lax.axis_index("dim") * half
    inside = row_ids < limit[:1, :]
    stores = []
    for n, place in enumerate(places):
        cut = slice(n * columns, (n + 1) * columns)
        summed[:, cut] = jnp.where(inside, refs[2 * n][...] + refs[2 * n + 1][...], 0.0)
        to = out.at[:, place * columns:(place + 1) * columns]
        stores.append(pltpu.make_async_copy(summed.at[:, cut], to, left.at[n]))
        stores[n].start()
    for store in stores:
        store.wait()


def finish(limit, pairs, places, steps, out=None):
    half, columns = pairs[0][0].shape
    operands = [ref for pair in pairs for ref in pair]
    given = [] if out is None else [in_hbm(out)]
    return pl.pallas_call(
        functools.partial(finish_kernel, places),
        out_shape=pltpu.HBM((half, columns * steps), jnp.float32),
        in_specs=[whole_spec()] * (1 + len(operands))
        + [far_spec()] * len(given),
        out_specs=far_spec(),
        scratch_shapes=[
            pltpu.VMEM((half, columns * len(places)), jnp.float32),
            pltpu.SemaphoreType.DMA((len(places),)),
        ],
        input_output_aliases={1 + len(operands): 0} if given else {},
        compiler_params=params(),
        cost_estimate=cost(half * columns * len(pairs), 12 * half * columns * len(pairs)),
    )(limit, *operands, *given)


def after(x, *earlier):
    return lax.optimization_barrier((x, *earlier))[0]


def shards(store, queries, precond, query_rank, valid_rows):
    size = lax.axis_size("ex")
    odd = lax.rem(lax.axis_index("ex"), 2) == 1
    one_ahead = [(i, (i + 1) % size) for i in range(size)]
    ahead = [(i, (i + 2) % size) for i in range(size)]
    even_ahead = ahead[::2]
    swap = [(i, i ^ 1) for i in range(size)]
    over_dim = [(0, 1), (1, 0)]

    def send(block, route, axis="ex"):
        return lax.ppermute(block, axis, route)

    def exchanged(total):
        theirs, ours = total
        return ours, send(theirs, over_dim, "dim")

    def by_parity(at_even, at_odd):
        return jnp.where(odd, at_odd, at_even)

    own = prepare(queries, precond[None, :], query_rank)
    two_back = [send(block, ahead) for block in own]
    one_back, three_back = [], []
    for n, kind in enumerate(KINDS):
        arrived = two_back[n]
        if kind == "U":
            swapped = send(by_parity(own[n], arrived), swap)
            one_back.append((swapped,))
            three_back.append((send(swapped, ahead),))
        elif kind == "I":
            early, swapped = send(own[n], swap), send(arrived, swap)
            one_back.append((swapped, early))
            three_back.append((send(swapped, even_ahead), swapped))
        else:
            direct = send(by_parity(own[n], two_back[n]), one_ahead)
            swapped = send(two_back[n], swap)
            one_back.append((swapped, direct))
            three_back.append((direct, swapped))

    first, two, one, limit, stores = more_scores(
        store,
        [
            (n, [(0, own[n]), (1, two_back[n])] + ([] if kind == "T" else [(2, *one_back[n])]))
            for n, kind in enumerate(KINDS)
        ],
        [None, None, None],
        valid_rows,
    )
    own_pair = exchanged(first)
    two_pair = exchanged(two)
    three, left = None, KINDS.count("T")
    for group in CHAIN:
        if KINDS[group[0]] == "T":
            pieces = [(n, [(0, *one_back[n]), (1, *three_back[n])]) for n in group]
            one, three = more_scores(stores, pieces, [one, three])
            left -= len(group)
        else:
            [three] = more_scores(stores, [(n, [(0, *three_back[n])]) for n in group], [three])
        if left == 0:
            left, one_pair = -1, exchanged(one)
    out = finish(limit, [own_pair, one_pair, two_pair], (0, 1, 2), STEPS)
    return finish(limit, [exchanged(three)], (3,), STEPS, out)


def solution(mesh):
    return jax.shard_map(
        shards,
        mesh=mesh,
        in_specs=(
            P(("groups", "ex"), "dim"),
            P(("groups", "ex"), "dim"),
            P("dim"),
            P(("groups", "ex"), None),
            P(("groups", "ex")),
        ),
        out_specs=P(("groups", "ex", "dim"), None),
        check_vma=False,
    )
```

```python
import functools

import jax
import jax.numpy as jnp
from jax import lax
from jax.experimental import pallas as pl
from jax.experimental.pallas import tpu as pltpu
from jax.sharding import PartitionSpec as P

STEPS = 4
KINDS = "UUUT"
PARTS = (4, 4, 4, 4)
CHAIN = ("b2", "b1", "b3 o0", "t0")
ORDER = ("B0", "B1", "B2", "B3", "C2", "C1", "C0", "E2", "E1", "E0", "R3", "C3")
TIES = {"B3": "B2", "C3": "C0", "R3": "C2"}
CHUNKS = len(PARTS)
VMEM_BYTES = 16 * 1024 * 1024


def params():
    return pltpu.CompilerParams(vmem_limit_bytes=VMEM_BYTES)


def whole_spec():
    return pl.BlockSpec(memory_space=pltpu.VMEM)


def far_spec():
    return pl.BlockSpec(memory_space=pltpu.HBM)


def in_hbm(x):
    return pltpu.with_memory_space_constraint(x, pltpu.HBM)


def cost(flops, traffic):
    return pl.CostEstimate(flops=flops, bytes_accessed=traffic, transcendentals=0)


def cuts_of(depth):
    ends = [depth * sum(PARTS[:n + 1]) // sum(PARTS) for n in range(CHUNKS)]
    return [slice(start, end) for start, end in zip([0] + ends, ends)]


def product(rows, block):
    return lax.dot_general(
        rows, block, (((1,), (1,)), ((), ())), preferred_element_type=jnp.float32
    )


def prepare_kernel(queries, precond, rank, *refs):
    chunks, (held, scale, places, arrived) = refs[:CHUNKS], refs[CHUNKS:]
    rows, depth = queries.shape
    cuts = cuts_of(depth)
    loads = [pltpu.make_async_copy(rank, places, arrived.at[CHUNKS])]
    loads.append(pltpu.make_async_copy(precond, scale, arrived.at[CHUNKS + 1]))
    for n, cut in enumerate(cuts):
        loads.append(pltpu.make_async_copy(queries.at[:, cut], held.at[:, cut], arrived.at[n]))
    for load in loads:
        load.start()
    loads[0].wait()
    loads[1].wait()
    positions = lax.broadcasted_iota(jnp.int32, (rows, rows), 0)
    placing = (positions == places[...]).astype(jnp.bfloat16)
    for n, cut in enumerate(cuts):
        loads[2 + n].wait()
        pre = (held[:, cut].astype(jnp.float32) * scale[:, cut]).astype(jnp.bfloat16)
        chunks[n][...] = jnp.dot(placing, pre, preferred_element_type=jnp.float32).astype(
            jnp.bfloat16
        )


def prepare(queries, precond, rank):
    rows, depth = queries.shape
    shapes = [
        jax.ShapeDtypeStruct((rows, cut.stop - cut.start), jnp.bfloat16) for cut in cuts_of(depth)
    ]
    return pl.pallas_call(
        prepare_kernel,
        out_shape=shapes,
        in_specs=[far_spec()] * 3,
        out_specs=[whole_spec()] * CHUNKS,
        scratch_shapes=[
            pltpu.VMEM((rows, depth), jnp.bfloat16),
            pltpu.VMEM((1, depth), jnp.float32),
            pltpu.VMEM((1, rows), jnp.int32),
            pltpu.SemaphoreType.DMA((CHUNKS + 2,)),
        ],
        compiler_params=params(),
        cost_estimate=cost(2 * rows * rows * depth, 4 * rows * depth),
    )(in_hbm(queries), in_hbm(precond), in_hbm(rank))


def scores_kernel(pieces, fresh, loading, counted, *refs):
    count = len(fresh)
    if counted:
        valid, *refs, limit = refs
        limit[...] = jnp.full(limit.shape, valid[0], jnp.int32)
    odd = lax.rem(lax.axis_index("ex"), 2) == 1
    loads = []
    if loading:
        store, *refs = refs
        *refs, other, mine, arrived = refs
        stores = other, mine
        half = other.shape[0]
        me = lax.axis_index("dim")
        for side, where in enumerate((1 - me, me)):
            place = pl.ds(pl.multiple_of(where * half, half), half)
            loads.append(pltpu.make_async_copy(store.at[place], stores[side], arrived.at[side]))
            loads[side].start()
    else:
        other, mine, *refs = refs
        stores = other, mine
    outs = refs[-2 * count:]
    carried = refs[-2 * count - 2 * (count - sum(fresh)):-2 * count]
    cuts = cuts_of(other.shape[1])
    stacks = []
    for n, targets in pieces:
        values = []
        for _, even_place, odd_place in targets:
            value = refs[even_place][...]
            if odd_place != even_place:
                value = jnp.where(odd, refs[odd_place][...], value)
            values.append(value)
        stacked = values[0] if len(values) == 1 else jnp.concatenate(values, axis=0)
        stacks.append((n, [which for which, _, _ in targets], stacked))
    for side, store in enumerate(stores):
        if loading:
            loads[side].wait()
        sums, at = {}, 0
        for i, new in enumerate(fresh):
            sums[i] = None if new else carried[at + side][...]
            at += 0 if new else 2
        for n, whiches, stacked in stacks:
            part = product(store[:, cuts[n]], stacked)
            columns = stacked.shape[0] // len(whiches)
            for k, i in enumerate(whiches):
                here = part[:, k * columns:(k + 1) * columns]
                sums[i] = here if sums[i] is None else sums[i] + here
        for i in range(count):
            outs[2 * i + side][...] = sums[i]


def more_scores(stores, pieces, carries, valid=None):
    operands, placed = [], []

    def place(block):
        known = [i for i, operand in enumerate(operands) if operand is block]
        if not known:
            operands.append(block)
        return known[0] if known else len(operands) - 1

    loading = not isinstance(stores, tuple)
    half, depth = stores.shape[0] // 2 if loading else stores[0].shape[0], 0
    flops = 0
    for n, targets in pieces:
        kept = []
        for which, *blocks in targets:
            places = [place(block) for block in blocks]
            kept.append((which, places[0], places[-1]))
            flops += 4 * half * blocks[0].size
        placed.append((n, tuple(kept)))
    columns = operands[0].shape[0]
    fresh = tuple(carry is None for carry in carries)
    first = [in_hbm(stores)] if loading else list(stores)
    operands += [side for carry in carries if carry for side in carry]
    specs = [far_spec()] if loading else [whole_spec()] * 2
    total = jax.ShapeDtypeStruct((half, columns), jnp.float32)
    more = []
    if loading:
        held = jax.ShapeDtypeStruct((half, stores.shape[1]), stores.dtype)
        more = [held, held]
    if valid is not None:
        first, more = [valid] + first, more + [jax.ShapeDtypeStruct((8, columns), jnp.int32)]
        specs = [pl.BlockSpec(memory_space=pltpu.SMEM)] + specs
    count = 2 * len(carries)
    outs = pl.pallas_call(
        functools.partial(scores_kernel, tuple(placed), fresh, loading, valid is not None),
        out_shape=[total] * count + more,
        in_specs=specs + [whole_spec()] * len(operands),
        out_specs=[whole_spec()] * (count + len(more)),
        scratch_shapes=[pltpu.SemaphoreType.DMA((2,))] if loading else [],
        compiler_params=params(),
        cost_estimate=cost(flops, 4 * half * columns * count),
    )(*first, *operands)
    totals = [(outs[2 * i], outs[2 * i + 1]) for i in range(len(carries))]
    if valid is not None:
        return totals + [outs[-1]]
    return totals + ([tuple(outs[count:])] if loading else [])


def finish_kernel(places, limit, *refs):
    out, summed, left = refs[-3:]
    half, columns = refs[0].shape
    row_ids = lax.broadcasted_iota(jnp.int32, (half, columns), 0) + lax.axis_index("dim") * half
    inside = row_ids < limit[:1, :]
    stores = []
    for n, place in enumerate(places):
        cut = slice(n * columns, (n + 1) * columns)
        summed[:, cut] = jnp.where(inside, refs[2 * n][...] + refs[2 * n + 1][...], 0.0)
        to = out.at[:, place * columns:(place + 1) * columns]
        stores.append(pltpu.make_async_copy(summed.at[:, cut], to, left.at[n]))
        stores[n].start()
    for store in stores:
        store.wait()


def finish(limit, pairs, places, steps, out=None):
    half, columns = pairs[0][0].shape
    operands = [ref for pair in pairs for ref in pair]
    given = [] if out is None else [in_hbm(out)]
    return pl.pallas_call(
        functools.partial(finish_kernel, places),
        out_shape=pltpu.HBM((half, columns * steps), jnp.float32),
        in_specs=[whole_spec()] * (1 + len(operands))
        + [far_spec()] * len(given),
        out_specs=far_spec(),
        scratch_shapes=[
            pltpu.VMEM((half, columns * len(places)), jnp.float32),
            pltpu.SemaphoreType.DMA((len(places),)),
        ],
        input_output_aliases={1 + len(operands): 0} if given else {},
        compiler_params=params(),
        cost_estimate=cost(half * columns * len(pairs), 12 * half * columns * len(pairs)),
    )(limit, *operands, *given)


def after(x, *earlier):
    return lax.optimization_barrier((x, *earlier))[0]


def shards(store, queries, precond, query_rank, valid_rows):
    size = lax.axis_size("ex")
    odd = lax.rem(lax.axis_index("ex"), 2) == 1
    one_ahead = [(i, (i + 1) % size) for i in range(size)]
    ahead = [(i, (i + 2) % size) for i in range(size)]
    even_ahead = ahead[::2]
    swap = [(i, i ^ 1) for i in range(size)]
    over_dim = [(0, 1), (1, 0)]

    def send(block, route, axis="ex"):
        return lax.ppermute(block, axis, route)

    def exchanged(total):
        theirs, ours = total
        return ours, send(theirs, over_dim, "dim")

    def by_parity(at_even, at_odd):
        return jnp.where(odd, at_odd, at_even)

    own = prepare(queries, precond[None, :], query_rank)
    moved = {}

    def tied(name, block):
        return after(block, *(moved[key] for key in TIES.get(name, "").split()))

    def move(name, block, route):
        moved[name] = send(tied(name, block), route)
        return moved[name]

    one_back, three_back, two_back = {}, {}, {}
    for step in ORDER:
        kind, n = step[0], int(step[1:])
        if kind == "B":
            two_back[n] = move(step, own[n], ahead)
        elif kind == "A":
            move(step, own[n], swap)
        elif kind == "C":
            block = two_back[n] if KINDS[n] != "U" else by_parity(own[n], two_back[n])
            move(step, block, swap)
        elif kind == "E":
            move(step, moved[f"C{n}"], even_ahead if KINDS[n] == "I" else ahead)
        else:
            move(step, by_parity(own[n], two_back[n]), one_ahead)
    for n, kind in enumerate(KINDS):
        swapped = moved[f"C{n}"]
        if kind == "U":
            one_back[n], three_back[n] = (swapped,), (moved[f"E{n}"],)
        elif kind == "I":
            one_back[n], three_back[n] = (swapped, moved[f"A{n}"]), (moved[f"E{n}"], swapped)
        else:
            direct = moved[f"R{n}"]
            one_back[n], three_back[n] = (swapped, direct), (direct, swapped)

    first, two, stores = more_scores(
        store,
        [(n, [(0, own[n]), (1, two_back[n])]) for n in range(CHUNKS)],
        [None, None],
    )
    own_pair, two_pair = exchanged(first), exchanged(two)
    one = three = one_pair = None
    todo = set(range(CHUNKS))
    for group in CHAIN:
        pieces = []
        for item in group.split():
            n, parts = int(item[1:]), {"b": (0, 1), "o": (0,), "t": (1,)}[item[0]]
            blocks = one_back[n], three_back[n]
            pieces.append((n, [(part, *blocks[part]) for part in parts]))
            todo -= {n} if 0 in parts else set()
        if one_pair is None:
            if one is None:
                one, three, limit = more_scores(stores, pieces, [one, three], valid_rows)
            else:
                one, three = more_scores(stores, pieces, [one, three])
            one_pair = None if todo else exchanged(one)
        else:
            pieces = [(n, [(0, *blocks) for _, *blocks in targets]) for n, targets in pieces]
            [three] = more_scores(stores, pieces, [three])
    out = finish(limit, [own_pair, one_pair, two_pair], (0, 1, 2), STEPS)
    return finish(limit, [exchanged(three)], (3,), STEPS, out)


def solution(mesh):
    return jax.shard_map(
        shards,
        mesh=mesh,
        in_specs=(
            P(("groups", "ex"), "dim"),
            P(("groups", "ex"), "dim"),
            P("dim"),
            P(("groups", "ex"), None),
            P(("groups", "ex")),
        ),
        out_specs=P(("groups", "ex", "dim"), None),
        check_vma=False,
    )
```

```python
import functools

import jax
import jax.numpy as jnp
from jax import lax
from jax.experimental import pallas as pl
from jax.experimental.pallas import tpu as pltpu
from jax.sharding import PartitionSpec as P

STEPS = 4
KINDS = "UUT"
PARTS = (4, 5, 7)
CHAIN = ("b0", "b2 o1", "t1")
ORDER = ("B0", "B1", "B2", "C0", "C1", "E0", "E1", "R2", "C2")
TIES = {"B2": "B0", "C2": "E0"}
EARLY = "C0"
CHUNKS = len(PARTS)
VMEM_BYTES = 16 * 1024 * 1024


def params():
    return pltpu.CompilerParams(vmem_limit_bytes=VMEM_BYTES)


def whole_spec():
    return pl.BlockSpec(memory_space=pltpu.VMEM)


def far_spec():
    return pl.BlockSpec(memory_space=pltpu.HBM)


def in_hbm(x):
    return pltpu.with_memory_space_constraint(x, pltpu.HBM)


def cost(flops, traffic):
    return pl.CostEstimate(flops=flops, bytes_accessed=traffic, transcendentals=0)


def cuts_of(depth):
    ends = [depth * sum(PARTS[:n + 1]) // sum(PARTS) for n in range(CHUNKS)]
    return [slice(start, end) for start, end in zip([0] + ends, ends)]


def product(rows, block):
    return lax.dot_general(
        rows, block, (((1,), (1,)), ((), ())), preferred_element_type=jnp.float32
    )


def prepare_kernel(queries, precond, rank, *refs):
    chunks, (held, scale, places, arrived) = refs[:CHUNKS], refs[CHUNKS:]
    rows, depth = queries.shape
    cuts = cuts_of(depth)
    loads = [pltpu.make_async_copy(rank, places, arrived.at[CHUNKS])]
    loads.append(pltpu.make_async_copy(precond, scale, arrived.at[CHUNKS + 1]))
    for n, cut in enumerate(cuts):
        loads.append(pltpu.make_async_copy(queries.at[:, cut], held.at[:, cut], arrived.at[n]))
    for load in loads:
        load.start()
    loads[0].wait()
    loads[1].wait()
    positions = lax.broadcasted_iota(jnp.int32, (rows, rows), 0)
    placing = (positions == places[...]).astype(jnp.bfloat16)
    for n, cut in enumerate(cuts):
        loads[2 + n].wait()
        pre = (held[:, cut].astype(jnp.float32) * scale[:, cut]).astype(jnp.bfloat16)
        chunks[n][...] = jnp.dot(placing, pre, preferred_element_type=jnp.float32).astype(
            jnp.bfloat16
        )


def prepare(queries, precond, rank):
    rows, depth = queries.shape
    shapes = [
        jax.ShapeDtypeStruct((rows, cut.stop - cut.start), jnp.bfloat16) for cut in cuts_of(depth)
    ]
    return pl.pallas_call(
        prepare_kernel,
        out_shape=shapes,
        in_specs=[far_spec()] * 3,
        out_specs=[whole_spec()] * CHUNKS,
        scratch_shapes=[
            pltpu.VMEM((rows, depth), jnp.bfloat16),
            pltpu.VMEM((1, depth), jnp.float32),
            pltpu.VMEM((1, rows), jnp.int32),
            pltpu.SemaphoreType.DMA((CHUNKS + 2,)),
        ],
        compiler_params=params(),
        cost_estimate=cost(2 * rows * rows * depth, 4 * rows * depth),
    )(in_hbm(queries), in_hbm(precond), in_hbm(rank))


def scores_kernel(pieces, fresh, loading, counted, sides, *refs):
    count = len(fresh)
    if counted:
        valid, *refs, limit = refs
        limit[...] = jnp.full(limit.shape, valid[0], jnp.int32)
    odd = lax.rem(lax.axis_index("ex"), 2) == 1
    loads = []
    if loading:
        store, *refs = refs
        *refs, other, mine, arrived = refs
        stores = other, mine
        half = other.shape[0]
        me = lax.axis_index("dim")
        for side, where in enumerate((1 - me, me)):
            place = pl.ds(pl.multiple_of(where * half, half), half)
            loads.append(pltpu.make_async_copy(store.at[place], stores[side], arrived.at[side]))
            loads[side].start()
    else:
        other, mine, *refs = refs
        stores = other, mine
    count_out = len(sides) * count
    outs = refs[-count_out:]
    carried = refs[-count_out - len(sides) * (count - sum(fresh)):-count_out]
    cuts = cuts_of(other.shape[1])
    stacks = []
    for n, targets in pieces:
        values = []
        for _, even_place, odd_place in targets:
            value = refs[even_place][...]
            if odd_place != even_place:
                value = jnp.where(odd, refs[odd_place][...], value)
            values.append(value)
        stacked = values[0] if len(values) == 1 else jnp.concatenate(values, axis=0)
        stacks.append((n, [which for which, _, _ in targets], stacked))
    for at_side, side in enumerate(sides):
        store = stores[side]
        if loading:
            loads[side].wait()
        sums, at = {}, 0
        for i, new in enumerate(fresh):
            sums[i] = None if new else carried[at + at_side][...]
            at += 0 if new else len(sides)
        for n, whiches, stacked in stacks:
            part = product(store[:, cuts[n]], stacked)
            columns = stacked.shape[0] // len(whiches)
            for k, i in enumerate(whiches):
                here = part[:, k * columns:(k + 1) * columns]
                sums[i] = here if sums[i] is None else sums[i] + here
        for i in range(count):
            outs[len(sides) * i + at_side][...] = sums[i]


def more_scores(stores, pieces, carries, valid=None, sides=(0, 1)):
    operands, placed = [], []

    def place(block):
        known = [i for i, operand in enumerate(operands) if operand is block]
        if not known:
            operands.append(block)
        return known[0] if known else len(operands) - 1

    loading = not isinstance(stores, tuple)
    half, depth = stores.shape[0] // 2 if loading else stores[0].shape[0], 0
    flops = 0
    for n, targets in pieces:
        kept = []
        for which, *blocks in targets:
            places = [place(block) for block in blocks]
            kept.append((which, places[0], places[-1]))
            flops += 4 * half * blocks[0].size
        placed.append((n, tuple(kept)))
    columns = operands[0].shape[0]
    fresh = tuple(carry is None for carry in carries)
    first = [in_hbm(stores)] if loading else list(stores)
    operands += [carry[side] for carry in carries if carry for side in sides]
    specs = [far_spec()] if loading else [whole_spec()] * 2
    total = jax.ShapeDtypeStruct((half, columns), jnp.float32)
    more = []
    if loading:
        held = jax.ShapeDtypeStruct((half, stores.shape[1]), stores.dtype)
        more = [held, held]
    if valid is not None:
        first, more = [valid] + first, more + [jax.ShapeDtypeStruct((8, columns), jnp.int32)]
        specs = [pl.BlockSpec(memory_space=pltpu.SMEM)] + specs
    count = len(sides) * len(carries)
    outs = pl.pallas_call(
        functools.partial(scores_kernel, tuple(placed), fresh, loading, valid is not None, sides),
        out_shape=[total] * count + more,
        in_specs=specs + [whole_spec()] * len(operands),
        out_specs=[whole_spec()] * (count + len(more)),
        scratch_shapes=[pltpu.SemaphoreType.DMA((2,))] if loading else [],
        compiler_params=params(),
        cost_estimate=cost(flops, 4 * half * columns * count),
    )(*first, *operands)
    totals = [tuple(outs[i:i + len(sides)]) for i in range(0, count, len(sides))]
    if valid is not None:
        return totals + [outs[-1]]
    return totals + ([tuple(outs[count:])] if loading else [])


def finish_kernel(places, limit, *refs):
    out, summed, left = refs[-3:]
    half, columns = refs[0].shape
    row_ids = lax.broadcasted_iota(jnp.int32, (half, columns), 0) + lax.axis_index("dim") * half
    inside = row_ids < limit[:1, :]
    stores = []
    for n, place in enumerate(places):
        cut = slice(n * columns, (n + 1) * columns)
        summed[:, cut] = jnp.where(inside, refs[2 * n][...] + refs[2 * n + 1][...], 0.0)
        to = out.at[:, place * columns:(place + 1) * columns]
        stores.append(pltpu.make_async_copy(summed.at[:, cut], to, left.at[n]))
        stores[n].start()
    for store in stores:
        store.wait()


def finish(limit, pairs, places, steps, out=None):
    half, columns = pairs[0][0].shape
    operands = [ref for pair in pairs for ref in pair]
    given = [] if out is None else [in_hbm(out)]
    return pl.pallas_call(
        functools.partial(finish_kernel, places),
        out_shape=pltpu.HBM((half, columns * steps), jnp.float32),
        in_specs=[whole_spec()] * (1 + len(operands))
        + [far_spec()] * len(given),
        out_specs=far_spec(),
        scratch_shapes=[
            pltpu.VMEM((half, columns * len(places)), jnp.float32),
            pltpu.SemaphoreType.DMA((len(places),)),
        ],
        input_output_aliases={1 + len(operands): 0} if given else {},
        compiler_params=params(),
        cost_estimate=cost(half * columns * len(pairs), 12 * half * columns * len(pairs)),
    )(limit, *operands, *given)


def after(x, *earlier):
    return lax.optimization_barrier((x, *earlier))[0]


def shards(store, queries, precond, query_rank, valid_rows):
    size = lax.axis_size("ex")
    odd = lax.rem(lax.axis_index("ex"), 2) == 1
    one_ahead = [(i, (i + 1) % size) for i in range(size)]
    ahead = [(i, (i + 2) % size) for i in range(size)]
    even_ahead = ahead[::2]
    swap = [(i, i ^ 1) for i in range(size)]
    over_dim = [(0, 1), (1, 0)]

    def send(block, route, axis="ex"):
        return lax.ppermute(block, axis, route)

    def exchanged(total):
        theirs, ours = total
        return ours, send(theirs, over_dim, "dim")

    def by_parity(at_even, at_odd):
        return jnp.where(odd, at_odd, at_even)

    own = prepare(queries, precond[None, :], query_rank)
    first, stores = more_scores(store, [(n, [(0, own[n])]) for n in range(CHUNKS)], [None])
    own_pair = exchanged(first)
    moved = {}

    def tied(name, block):
        return after(block, *(moved[key] for key in TIES.get(name, "").split()))

    def move(name, block, route):
        moved[name] = send(tied(name, block), route)
        return moved[name]

    one_back, three_back, two_back = {}, {}, {}
    for step in ORDER:
        kind, n = step[0], int(step[1:])
        if kind == "B":
            two_back[n] = move(step, own[n], ahead)
        elif kind == "A":
            move(step, own[n], swap)
        elif kind == "C":
            block = two_back[n] if KINDS[n] != "U" else by_parity(own[n], two_back[n])
            if step == EARLY:
                block = after(block, first[1])
            move(step, block, swap)
        elif kind == "E":
            move(step, moved[f"C{n}"], even_ahead if KINDS[n] == "I" else ahead)
        else:
            move(step, by_parity(own[n], two_back[n]), one_ahead)
    for n, kind in enumerate(KINDS):
        swapped = moved[f"C{n}"]
        if kind == "U":
            one_back[n], three_back[n] = (swapped,), (moved[f"E{n}"],)
        elif kind == "I":
            one_back[n], three_back[n] = (swapped, moved[f"A{n}"]), (moved[f"E{n}"], swapped)
        else:
            direct = moved[f"R{n}"]
            one_back[n], three_back[n] = (swapped, direct), (direct, swapped)

    [two] = more_scores(stores, [(n, [(0, two_back[n])]) for n in range(CHUNKS)], [None])
    two_pair = exchanged(two)
    limited = after(valid_rows, two[1])
    one = three = one_pair = None
    todo = set(range(CHUNKS))
    for group in CHAIN:
        pieces = []
        for item in group.split():
            n, parts = int(item[1:]), {"b": (0, 1), "o": (0,), "t": (1,)}[item[0]]
            blocks = one_back[n], three_back[n]
            pieces.append((n, [(part, *blocks[part]) for part in parts]))
            todo -= {n} if 0 in parts else set()
        if one is None:
            one, three, limit = more_scores(stores, pieces, [one, three], limited)
        elif one_pair is None:
            one, three = more_scores(stores, pieces, [one, three])
        else:
            pieces = [(n, [(0, *blocks) for _, *blocks in targets]) for n, targets in pieces]
            [[theirs]] = more_scores(stores, pieces, [three], sides=(0,))
            [[ours]] = more_scores(stores, pieces, [three], sides=(1,))
            three = theirs, ours
        if one_pair is None and not todo:
            one_pair = exchanged(one)
    out = finish(limit, [own_pair, two_pair], (0, 2), STEPS)
    return finish(limit, [one_pair, exchanged(three)], (1, 3), STEPS, out)


def solution(mesh):
    return jax.shard_map(
        shards,
        mesh=mesh,
        in_specs=(
            P(("groups", "ex"), "dim"),
            P(("groups", "ex"), "dim"),
            P("dim"),
            P(("groups", "ex"), None),
            P(("groups", "ex")),
        ),
        out_specs=P(("groups", "ex", "dim"), None),
        check_vma=False,
    )
```

```python
import functools

import jax
import jax.numpy as jnp
from jax import lax
from jax.experimental import pallas as pl
from jax.experimental.pallas import tpu as pltpu
from jax.sharding import PartitionSpec as P

STEPS = 4
KINDS = "VV"
PARTS = (9, 7)
CHAIN = ("b0", "o1", "t1")
ORDER = ("B0", "A0", "B1", "A1", "Z0", "R0", "Z1", "R1")
TIES = {}
EARLY = "R0"
CHUNKS = len(PARTS)
VMEM_BYTES = 16 * 1024 * 1024


def params():
    return pltpu.CompilerParams(vmem_limit_bytes=VMEM_BYTES)


def whole_spec():
    return pl.BlockSpec(memory_space=pltpu.VMEM)


def far_spec():
    return pl.BlockSpec(memory_space=pltpu.HBM)


def in_hbm(x):
    return pltpu.with_memory_space_constraint(x, pltpu.HBM)


def cost(flops, traffic):
    return pl.CostEstimate(flops=flops, bytes_accessed=traffic, transcendentals=0)


def cuts_of(depth):
    ends = [depth * sum(PARTS[:n + 1]) // sum(PARTS) for n in range(CHUNKS)]
    return [slice(start, end) for start, end in zip([0] + ends, ends)]


def product(rows, block):
    return lax.dot_general(
        rows, block, (((1,), (1,)), ((), ())), preferred_element_type=jnp.float32
    )


def prepare_kernel(queries, precond, rank, *refs):
    chunks, (held, scale, places, arrived) = refs[:CHUNKS], refs[CHUNKS:]
    rows, depth = queries.shape
    cuts = cuts_of(depth)
    loads = [pltpu.make_async_copy(rank, places, arrived.at[CHUNKS])]
    loads.append(pltpu.make_async_copy(precond, scale, arrived.at[CHUNKS + 1]))
    for n, cut in enumerate(cuts):
        loads.append(pltpu.make_async_copy(queries.at[:, cut], held.at[:, cut], arrived.at[n]))
    for load in loads:
        load.start()
    loads[0].wait()
    loads[1].wait()
    positions = lax.broadcasted_iota(jnp.int32, (rows, rows), 0)
    placing = (positions == places[...]).astype(jnp.bfloat16)
    for n, cut in enumerate(cuts):
        loads[2 + n].wait()
        pre = (held[:, cut].astype(jnp.float32) * scale[:, cut]).astype(jnp.bfloat16)
        chunks[n][...] = jnp.dot(placing, pre, preferred_element_type=jnp.float32).astype(
            jnp.bfloat16
        )


def prepare(queries, precond, rank):
    rows, depth = queries.shape
    shapes = [
        jax.ShapeDtypeStruct((rows, cut.stop - cut.start), jnp.bfloat16) for cut in cuts_of(depth)
    ]
    return pl.pallas_call(
        prepare_kernel,
        out_shape=shapes,
        in_specs=[far_spec()] * 3,
        out_specs=[whole_spec()] * CHUNKS,
        scratch_shapes=[
            pltpu.VMEM((rows, depth), jnp.bfloat16),
            pltpu.VMEM((1, depth), jnp.float32),
            pltpu.VMEM((1, rows), jnp.int32),
            pltpu.SemaphoreType.DMA((CHUNKS + 2,)),
        ],
        compiler_params=params(),
        cost_estimate=cost(2 * rows * rows * depth, 4 * rows * depth),
    )(in_hbm(queries), in_hbm(precond), in_hbm(rank))


def scores_kernel(pieces, fresh, loading, counted, sides, *refs):
    count = len(fresh)
    if counted:
        valid, *refs, limit = refs
        limit[...] = jnp.full(limit.shape, valid[0], jnp.int32)
    odd = lax.rem(lax.axis_index("ex"), 2) == 1
    loads = []
    if loading:
        store, *refs = refs
        *refs, other, mine, arrived = refs
        stores = other, mine
        half = other.shape[0]
        me = lax.axis_index("dim")
        for side, where in enumerate((1 - me, me)):
            place = pl.ds(pl.multiple_of(where * half, half), half)
            loads.append(pltpu.make_async_copy(store.at[place], stores[side], arrived.at[side]))
            loads[side].start()
    else:
        other, mine, *refs = refs
        stores = other, mine
    count_out = len(sides) * count
    outs = refs[-count_out:]
    carried = refs[-count_out - len(sides) * (count - sum(fresh)):-count_out]
    cuts = cuts_of(other.shape[1])
    stacks = []
    for n, targets in pieces:
        values = []
        for _, even_place, odd_place in targets:
            value = refs[even_place][...]
            if odd_place != even_place:
                value = jnp.where(odd, refs[odd_place][...], value)
            values.append(value)
        stacked = values[0] if len(values) == 1 else jnp.concatenate(values, axis=0)
        stacks.append((n, [which for which, _, _ in targets], stacked))
    for at_side, side in enumerate(sides):
        store = stores[side]
        if loading:
            loads[side].wait()
        sums, at = {}, 0
        for i, new in enumerate(fresh):
            sums[i] = None if new else carried[at + at_side][...]
            at += 0 if new else len(sides)
        for n, whiches, stacked in stacks:
            part = product(store[:, cuts[n]], stacked)
            columns = stacked.shape[0] // len(whiches)
            for k, i in enumerate(whiches):
                here = part[:, k * columns:(k + 1) * columns]
                sums[i] = here if sums[i] is None else sums[i] + here
        for i in range(count):
            outs[len(sides) * i + at_side][...] = sums[i]


def more_scores(stores, pieces, carries, valid=None, sides=(0, 1)):
    operands, placed = [], []

    def place(block):
        known = [i for i, operand in enumerate(operands) if operand is block]
        if not known:
            operands.append(block)
        return known[0] if known else len(operands) - 1

    loading = not isinstance(stores, tuple)
    half, depth = stores.shape[0] // 2 if loading else stores[0].shape[0], 0
    flops = 0
    for n, targets in pieces:
        kept = []
        for which, *blocks in targets:
            places = [place(block) for block in blocks]
            kept.append((which, places[0], places[-1]))
            flops += 4 * half * blocks[0].size
        placed.append((n, tuple(kept)))
    columns = operands[0].shape[0]
    fresh = tuple(carry is None for carry in carries)
    first = [in_hbm(stores)] if loading else list(stores)
    operands += [carry[side] for carry in carries if carry for side in sides]
    specs = [far_spec()] if loading else [whole_spec()] * 2
    total = jax.ShapeDtypeStruct((half, columns), jnp.float32)
    more = []
    if loading:
        held = jax.ShapeDtypeStruct((half, stores.shape[1]), stores.dtype)
        more = [held, held]
    if valid is not None:
        first, more = [valid] + first, more + [jax.ShapeDtypeStruct((8, columns), jnp.int32)]
        specs = [pl.BlockSpec(memory_space=pltpu.SMEM)] + specs
    count = len(sides) * len(carries)
    outs = pl.pallas_call(
        functools.partial(scores_kernel, tuple(placed), fresh, loading, valid is not None, sides),
        out_shape=[total] * count + more,
        in_specs=specs + [whole_spec()] * len(operands),
        out_specs=[whole_spec()] * (count + len(more)),
        scratch_shapes=[pltpu.SemaphoreType.DMA((2,))] if loading else [],
        compiler_params=params(),
        cost_estimate=cost(flops, 4 * half * columns * count),
    )(*first, *operands)
    totals = [tuple(outs[i:i + len(sides)]) for i in range(0, count, len(sides))]
    if valid is not None:
        return totals + [outs[-1]]
    return totals + ([tuple(outs[count:])] if loading else [])


def finish_kernel(places, limit, *refs):
    out, summed, left = refs[-3:]
    half, columns = refs[0].shape
    row_ids = lax.broadcasted_iota(jnp.int32, (half, columns), 0) + lax.axis_index("dim") * half
    inside = row_ids < limit[:1, :]
    stores = []
    for n, place in enumerate(places):
        cut = slice(n * columns, (n + 1) * columns)
        summed[:, cut] = jnp.where(inside, refs[2 * n][...] + refs[2 * n + 1][...], 0.0)
        to = out.at[:, place * columns:(place + 1) * columns]
        stores.append(pltpu.make_async_copy(summed.at[:, cut], to, left.at[n]))
        stores[n].start()
    for store in stores:
        store.wait()


def finish(limit, pairs, places, steps, out=None):
    half, columns = pairs[0][0].shape
    operands = [ref for pair in pairs for ref in pair]
    given = [] if out is None else [in_hbm(out)]
    return pl.pallas_call(
        functools.partial(finish_kernel, places),
        out_shape=pltpu.HBM((half, columns * steps), jnp.float32),
        in_specs=[whole_spec()] * (1 + len(operands))
        + [far_spec()] * len(given),
        out_specs=far_spec(),
        scratch_shapes=[
            pltpu.VMEM((half, columns * len(places)), jnp.float32),
            pltpu.SemaphoreType.DMA((len(places),)),
        ],
        input_output_aliases={1 + len(operands): 0} if given else {},
        compiler_params=params(),
        cost_estimate=cost(half * columns * len(pairs), 12 * half * columns * len(pairs)),
    )(limit, *operands, *given)


def after(x, *earlier):
    return lax.optimization_barrier((x, *earlier))[0]


def shards(store, queries, precond, query_rank, valid_rows):
    size = lax.axis_size("ex")
    odd = lax.rem(lax.axis_index("ex"), 2) == 1
    one_ahead = [(i, (i + 1) % size) for i in range(size)]
    ahead = [(i, (i + 2) % size) for i in range(size)]
    even_ahead = ahead[::2]
    swap = [(i, i ^ 1) for i in range(size)]
    over_dim = [(0, 1), (1, 0)]

    def send(block, route, axis="ex"):
        return lax.ppermute(block, axis, route)

    def exchanged(total):
        theirs, ours = total
        return ours, send(theirs, over_dim, "dim")

    def by_parity(at_even, at_odd):
        return jnp.where(odd, at_odd, at_even)

    own = prepare(queries, precond[None, :], query_rank)
    first, stores = more_scores(store, [(n, [(0, own[n])]) for n in range(CHUNKS)], [None])
    own_pair = exchanged(first)
    moved = {}

    def tied(name, block):
        earlier = [first[1]] if name == EARLY else []
        return after(block, *earlier, *(moved[key] for key in TIES.get(name, "").split()))

    def move(name, block, route):
        moved[name] = send(tied(name, block), route)
        return moved[name]

    one_back, three_back, two_back = {}, {}, {}
    for step in ORDER:
        kind, n = step[0], int(step[1:])
        if kind == "B":
            two_back[n] = move(step, own[n], ahead)
        elif kind == "A":
            move(step, own[n], swap)
        elif kind == "C":
            block = two_back[n] if KINDS[n] != "U" else by_parity(own[n], two_back[n])
            move(step, block, swap)
        elif kind == "Z":
            move(step, moved[f"A{n}"], even_ahead)
        elif kind == "E":
            move(step, moved[f"C{n}"], even_ahead if KINDS[n] == "I" else ahead)
        else:
            block = two_back[n] if KINDS[n] == "V" else by_parity(own[n], two_back[n])
            move(step, block, one_ahead)
    for n, kind in enumerate(KINDS):
        if kind == "V":
            one_back[n], three_back[n] = (moved[f"Z{n}"], moved[f"A{n}"]), (moved[f"R{n}"],)
            continue
        swapped = moved[f"C{n}"]
        if kind == "U":
            one_back[n], three_back[n] = (swapped,), (moved[f"E{n}"],)
        elif kind == "I":
            one_back[n], three_back[n] = (swapped, moved[f"A{n}"]), (moved[f"E{n}"], swapped)
        else:
            direct = moved[f"R{n}"]
            one_back[n], three_back[n] = (swapped, direct), (direct, swapped)

    [two] = more_scores(stores, [(n, [(0, two_back[n])]) for n in range(CHUNKS)], [None])
    two_pair = exchanged(two)
    limited = after(valid_rows, two[1])
    one = three = one_pair = None
    todo = set(range(CHUNKS))
    for group in CHAIN:
        pieces = []
        for item in group.split():
            n, parts = int(item[1:]), {"b": (0, 1), "o": (0,), "t": (1,)}[item[0]]
            blocks = one_back[n], three_back[n]
            pieces.append((n, [(part, *blocks[part]) for part in parts]))
            todo -= {n} if 0 in parts else set()
        if one is None:
            one, three, limit = more_scores(stores, pieces, [one, three], limited)
        elif one_pair is None:
            one, three = more_scores(stores, pieces, [one, three])
        else:
            pieces = [(n, [(0, *blocks) for _, *blocks in targets]) for n, targets in pieces]
            [[theirs]] = more_scores(stores, pieces, [three], sides=(0,))
            [[ours]] = more_scores(stores, pieces, [three], sides=(1,))
            three = theirs, ours
        if one_pair is None and not todo:
            one_pair = exchanged(one)
    out = finish(limit, [own_pair, two_pair], (0, 2), STEPS)
    return finish(limit, [one_pair, exchanged(three)], (1, 3), STEPS, out)


def solution(mesh):
    return jax.shard_map(
        shards,
        mesh=mesh,
        in_specs=(
            P(("groups", "ex"), "dim"),
            P(("groups", "ex"), "dim"),
            P("dim"),
            P(("groups", "ex"), None),
            P(("groups", "ex")),
        ),
        out_specs=P(("groups", "ex", "dim"), None),
        check_vma=False,
    )
```

```python
import functools

import jax
import jax.numpy as jnp
from jax import lax
from jax.experimental import pallas as pl
from jax.experimental.pallas import tpu as pltpu
from jax.sharding import PartitionSpec as P

STEPS = 4
KINDS = "UUT"
PARTS = (4, 6, 6)
CHAIN = ("b0", "b2 o1", "t1")
ORDER = ("B0", "B1", "B2", "C0", "C1", "E0", "E1", "R2", "C2")
TIES = {"C2": "C1", "E1": "E0"}
EARLY = "none"
CHUNKS = len(PARTS)
VMEM_BYTES = 16 * 1024 * 1024


def params():
    return pltpu.CompilerParams(vmem_limit_bytes=VMEM_BYTES)


def whole_spec():
    return pl.BlockSpec(memory_space=pltpu.VMEM)


def far_spec():
    return pl.BlockSpec(memory_space=pltpu.HBM)


def in_hbm(x):
    return pltpu.with_memory_space_constraint(x, pltpu.HBM)


def cost(flops, traffic):
    return pl.CostEstimate(flops=flops, bytes_accessed=traffic, transcendentals=0)


def cuts_of(depth):
    ends = [depth * sum(PARTS[:n + 1]) // sum(PARTS) for n in range(CHUNKS)]
    return [slice(start, end) for start, end in zip([0] + ends, ends)]


def product(rows, block):
    return lax.dot_general(
        rows, block, (((1,), (1,)), ((), ())), preferred_element_type=jnp.float32
    )


def prepare_kernel(queries, precond, rank, *refs):
    chunks, (held, scale, places, arrived) = refs[:CHUNKS], refs[CHUNKS:]
    rows, depth = queries.shape
    cuts = cuts_of(depth)
    loads = [pltpu.make_async_copy(rank, places, arrived.at[CHUNKS])]
    loads.append(pltpu.make_async_copy(precond, scale, arrived.at[CHUNKS + 1]))
    for n, cut in enumerate(cuts):
        loads.append(pltpu.make_async_copy(queries.at[:, cut], held.at[:, cut], arrived.at[n]))
    for load in loads:
        load.start()
    loads[0].wait()
    loads[1].wait()
    positions = lax.broadcasted_iota(jnp.int32, (rows, rows), 0)
    placing = (positions == places[...]).astype(jnp.bfloat16)
    for n, cut in enumerate(cuts):
        loads[2 + n].wait()
        pre = (held[:, cut].astype(jnp.float32) * scale[:, cut]).astype(jnp.bfloat16)
        chunks[n][...] = jnp.dot(placing, pre, preferred_element_type=jnp.float32).astype(
            jnp.bfloat16
        )


def prepare(queries, precond, rank):
    rows, depth = queries.shape
    shapes = [
        jax.ShapeDtypeStruct((rows, cut.stop - cut.start), jnp.bfloat16) for cut in cuts_of(depth)
    ]
    return pl.pallas_call(
        prepare_kernel,
        out_shape=shapes,
        in_specs=[far_spec()] * 3,
        out_specs=[whole_spec()] * CHUNKS,
        scratch_shapes=[
            pltpu.VMEM((rows, depth), jnp.bfloat16),
            pltpu.VMEM((1, depth), jnp.float32),
            pltpu.VMEM((1, rows), jnp.int32),
            pltpu.SemaphoreType.DMA((CHUNKS + 2,)),
        ],
        compiler_params=params(),
        cost_estimate=cost(2 * rows * rows * depth, 4 * rows * depth),
    )(in_hbm(queries), in_hbm(precond), in_hbm(rank))


def scores_kernel(pieces, fresh, loading, counted, sides, *refs):
    count = len(fresh)
    if counted:
        valid, *refs, limit = refs
        limit[...] = jnp.full(limit.shape, valid[0], jnp.int32)
    odd = lax.rem(lax.axis_index("ex"), 2) == 1
    loads = []
    if loading:
        store, *refs = refs
        *refs, other, mine, arrived = refs
        stores = other, mine
        half = other.shape[0]
        me = lax.axis_index("dim")
        for side, where in enumerate((1 - me, me)):
            place = pl.ds(pl.multiple_of(where * half, half), half)
            loads.append(pltpu.make_async_copy(store.at[place], stores[side], arrived.at[side]))
            loads[side].start()
    else:
        other, mine, *refs = refs
        stores = other, mine
    count_out = len(sides) * count
    outs = refs[-count_out:]
    carried = refs[-count_out - len(sides) * (count - sum(fresh)):-count_out]
    cuts = cuts_of(other.shape[1])
    stacks = []
    for n, targets in pieces:
        values = []
        for _, even_place, odd_place in targets:
            value = refs[even_place][...]
            if odd_place != even_place:
                value = jnp.where(odd, refs[odd_place][...], value)
            values.append(value)
        stacked = values[0] if len(values) == 1 else jnp.concatenate(values, axis=0)
        stacks.append((n, [which for which, _, _ in targets], stacked))
    for at_side, side in enumerate(sides):
        store = stores[side]
        if loading:
            loads[side].wait()
        sums, at = {}, 0
        for i, new in enumerate(fresh):
            sums[i] = None if new else carried[at + at_side][...]
            at += 0 if new else len(sides)
        for n, whiches, stacked in stacks:
            part = product(store[:, cuts[n]], stacked)
            columns = stacked.shape[0] // len(whiches)
            for k, i in enumerate(whiches):
                here = part[:, k * columns:(k + 1) * columns]
                sums[i] = here if sums[i] is None else sums[i] + here
        for i in range(count):
            outs[len(sides) * i + at_side][...] = sums[i]


def more_scores(stores, pieces, carries, valid=None, sides=(0, 1)):
    operands, placed = [], []

    def place(block):
        known = [i for i, operand in enumerate(operands) if operand is block]
        if not known:
            operands.append(block)
        return known[0] if known else len(operands) - 1

    loading = not isinstance(stores, tuple)
    half, depth = stores.shape[0] // 2 if loading else stores[0].shape[0], 0
    flops = 0
    for n, targets in pieces:
        kept = []
        for which, *blocks in targets:
            places = [place(block) for block in blocks]
            kept.append((which, places[0], places[-1]))
            flops += 4 * half * blocks[0].size
        placed.append((n, tuple(kept)))
    columns = operands[0].shape[0]
    fresh = tuple(carry is None for carry in carries)
    first = [in_hbm(stores)] if loading else list(stores)
    operands += [carry[side] for carry in carries if carry for side in sides]
    specs = [far_spec()] if loading else [whole_spec()] * 2
    total = jax.ShapeDtypeStruct((half, columns), jnp.float32)
    more = []
    if loading:
        held = jax.ShapeDtypeStruct((half, stores.shape[1]), stores.dtype)
        more = [held, held]
    if valid is not None:
        first, more = [valid] + first, more + [jax.ShapeDtypeStruct((8, columns), jnp.int32)]
        specs = [pl.BlockSpec(memory_space=pltpu.SMEM)] + specs
    count = len(sides) * len(carries)
    outs = pl.pallas_call(
        functools.partial(scores_kernel, tuple(placed), fresh, loading, valid is not None, sides),
        out_shape=[total] * count + more,
        in_specs=specs + [whole_spec()] * len(operands),
        out_specs=[whole_spec()] * (count + len(more)),
        scratch_shapes=[pltpu.SemaphoreType.DMA((2,))] if loading else [],
        compiler_params=params(),
        cost_estimate=cost(flops, 4 * half * columns * count),
    )(*first, *operands)
    totals = [tuple(outs[i:i + len(sides)]) for i in range(0, count, len(sides))]
    if valid is not None:
        return totals + [outs[-1]]
    return totals + ([tuple(outs[count:])] if loading else [])


def finish_kernel(places, limit, *refs):
    out, summed, left = refs[-3:]
    half, columns = refs[0].shape
    row_ids = lax.broadcasted_iota(jnp.int32, (half, columns), 0) + lax.axis_index("dim") * half
    inside = row_ids < limit[:1, :]
    stores = []
    for n, place in enumerate(places):
        cut = slice(n * columns, (n + 1) * columns)
        summed[:, cut] = jnp.where(inside, refs[2 * n][...] + refs[2 * n + 1][...], 0.0)
        to = out.at[:, place * columns:(place + 1) * columns]
        stores.append(pltpu.make_async_copy(summed.at[:, cut], to, left.at[n]))
        stores[n].start()
    for store in stores:
        store.wait()


def finish(limit, pairs, places, steps, out=None):
    half, columns = pairs[0][0].shape
    operands = [ref for pair in pairs for ref in pair]
    given = [] if out is None else [in_hbm(out)]
    return pl.pallas_call(
        functools.partial(finish_kernel, places),
        out_shape=pltpu.HBM((half, columns * steps), jnp.float32),
        in_specs=[whole_spec()] * (1 + len(operands))
        + [far_spec()] * len(given),
        out_specs=far_spec(),
        scratch_shapes=[
            pltpu.VMEM((half, columns * len(places)), jnp.float32),
            pltpu.SemaphoreType.DMA((len(places),)),
        ],
        input_output_aliases={1 + len(operands): 0} if given else {},
        compiler_params=params(),
        cost_estimate=cost(half * columns * len(pairs), 12 * half * columns * len(pairs)),
    )(limit, *operands, *given)


def after(x, *earlier):
    return lax.optimization_barrier((x, *earlier))[0]


def shards(store, queries, precond, query_rank, valid_rows):
    size = lax.axis_size("ex")
    odd = lax.rem(lax.axis_index("ex"), 2) == 1
    one_ahead = [(i, (i + 1) % size) for i in range(size)]
    ahead = [(i, (i + 2) % size) for i in range(size)]
    even_ahead = ahead[::2]
    swap = [(i, i ^ 1) for i in range(size)]
    over_dim = [(0, 1), (1, 0)]

    def send(block, route, axis="ex"):
        return lax.ppermute(block, axis, route)

    def exchanged(total):
        theirs, ours = total
        return ours, send(theirs, over_dim, "dim")

    def by_parity(at_even, at_odd):
        return jnp.where(odd, at_odd, at_even)

    own = prepare(queries, precond[None, :], query_rank)
    first, stores = more_scores(store, [(n, [(0, own[n])]) for n in range(CHUNKS)], [None])
    own_pair = exchanged(first)
    moved = {}

    def tied(name, block):
        earlier = [first[1]] if name == EARLY else []
        return after(block, *earlier, *(moved[key] for key in TIES.get(name, "").split()))

    def move(name, block, route):
        moved[name] = send(tied(name, block), route)
        return moved[name]

    one_back, three_back, two_back = {}, {}, {}
    for step in ORDER:
        kind, n = step[0], int(step[1:])
        if kind == "B":
            two_back[n] = move(step, own[n], ahead)
        elif kind == "A":
            move(step, own[n], swap)
        elif kind == "C":
            block = two_back[n] if KINDS[n] != "U" else by_parity(own[n], two_back[n])
            move(step, block, swap)
        elif kind == "Z":
            move(step, moved[f"A{n}"], even_ahead)
        elif kind == "E":
            move(step, moved[f"C{n}"], even_ahead if KINDS[n] == "I" else ahead)
        else:
            block = two_back[n] if KINDS[n] == "V" else by_parity(own[n], two_back[n])
            move(step, block, one_ahead)
    for n, kind in enumerate(KINDS):
        if kind == "V":
            one_back[n], three_back[n] = (moved[f"Z{n}"], moved[f"A{n}"]), (moved[f"R{n}"],)
            continue
        swapped = moved[f"C{n}"]
        if kind == "U":
            one_back[n], three_back[n] = (swapped,), (moved[f"E{n}"],)
        elif kind == "I":
            one_back[n], three_back[n] = (swapped, moved[f"A{n}"]), (moved[f"E{n}"], swapped)
        else:
            direct = moved[f"R{n}"]
            one_back[n], three_back[n] = (swapped, direct), (direct, swapped)

    [two] = more_scores(stores, [(n, [(0, two_back[n])]) for n in range(CHUNKS)], [None])
    two_pair = exchanged(two)
    limited = after(valid_rows, two[1])
    one = three = one_pair = None
    todo = set(range(CHUNKS))
    for group in CHAIN:
        pieces = []
        for item in group.split():
            n, parts = int(item[1:]), {"b": (0, 1), "o": (0,), "t": (1,)}[item[0]]
            blocks = one_back[n], three_back[n]
            pieces.append((n, [(part, *blocks[part]) for part in parts]))
            todo -= {n} if 0 in parts else set()
        if one is None:
            one, three, limit = more_scores(stores, pieces, [one, three], limited)
        elif one_pair is None:
            one, three = more_scores(stores, pieces, [one, three])
        else:
            pieces = [(n, [(0, *blocks) for _, *blocks in targets]) for n, targets in pieces]
            [[theirs]] = more_scores(stores, pieces, [three], sides=(0,))
            [[ours]] = more_scores(stores, pieces, [three], sides=(1,))
            three = theirs, ours
        if one_pair is None and not todo:
            one_pair = exchanged(one)
    out = finish(limit, [own_pair, two_pair], (0, 2), STEPS)
    return finish(limit, [one_pair, exchanged(three)], (1, 3), STEPS, out)


def solution(mesh):
    return jax.shard_map(
        shards,
        mesh=mesh,
        in_specs=(
            P(("groups", "ex"), "dim"),
            P(("groups", "ex"), "dim"),
            P("dim"),
            P(("groups", "ex"), None),
            P(("groups", "ex")),
        ),
        out_specs=P(("groups", "ex", "dim"), None),
        check_vma=False,
    )
```

```python
import functools

import jax
import jax.numpy as jnp
from jax import lax
from jax.experimental import pallas as pl
from jax.experimental.pallas import tpu as pltpu
from jax.sharding import PartitionSpec as P

STEPS = 4
KINDS = "UUT"
PARTS = (4, 6, 6)
CHAIN = ("b0", "b2 o1", "t1")
ORDER = ("B0", "B1", "B2", "C0", "C1", "E0", "E1", "R2", "C2")
TIES = {"C2": "C1", "E1": "E0"}
EARLY = "C0"
CHUNKS = len(PARTS)
VMEM_BYTES = 16 * 1024 * 1024


def params():
    return pltpu.CompilerParams(vmem_limit_bytes=VMEM_BYTES)


def whole_spec():
    return pl.BlockSpec(memory_space=pltpu.VMEM)


def far_spec():
    return pl.BlockSpec(memory_space=pltpu.HBM)


def in_hbm(x):
    return pltpu.with_memory_space_constraint(x, pltpu.HBM)


def cost(flops, traffic):
    return pl.CostEstimate(flops=flops, bytes_accessed=traffic, transcendentals=0)


def cuts_of(depth):
    ends = [depth * sum(PARTS[:n + 1]) // sum(PARTS) for n in range(CHUNKS)]
    return [slice(start, end) for start, end in zip([0] + ends, ends)]


def product(rows, block):
    return lax.dot_general(
        rows, block, (((1,), (1,)), ((), ())), preferred_element_type=jnp.float32
    )


def prepare_kernel(queries, precond, rank, *refs):
    chunks, (held, scale, places, arrived) = refs[:CHUNKS], refs[CHUNKS:]
    rows, depth = queries.shape
    cuts = cuts_of(depth)
    loads = [pltpu.make_async_copy(rank, places, arrived.at[CHUNKS])]
    loads.append(pltpu.make_async_copy(precond, scale, arrived.at[CHUNKS + 1]))
    for n, cut in enumerate(cuts):
        loads.append(pltpu.make_async_copy(queries.at[:, cut], held.at[:, cut], arrived.at[n]))
    for load in loads:
        load.start()
    loads[0].wait()
    loads[1].wait()
    positions = lax.broadcasted_iota(jnp.int32, (rows, rows), 0)
    placing = (positions == places[...]).astype(jnp.bfloat16)
    for n, cut in enumerate(cuts):
        loads[2 + n].wait()
        pre = (held[:, cut].astype(jnp.float32) * scale[:, cut]).astype(jnp.bfloat16)
        chunks[n][...] = jnp.dot(placing, pre, preferred_element_type=jnp.float32).astype(
            jnp.bfloat16
        )


def prepare(queries, precond, rank):
    rows, depth = queries.shape
    shapes = [
        jax.ShapeDtypeStruct((rows, cut.stop - cut.start), jnp.bfloat16) for cut in cuts_of(depth)
    ]
    return pl.pallas_call(
        prepare_kernel,
        out_shape=shapes,
        in_specs=[far_spec()] * 3,
        out_specs=[whole_spec()] * CHUNKS,
        scratch_shapes=[
            pltpu.VMEM((rows, depth), jnp.bfloat16),
            pltpu.VMEM((1, depth), jnp.float32),
            pltpu.VMEM((1, rows), jnp.int32),
            pltpu.SemaphoreType.DMA((CHUNKS + 2,)),
        ],
        compiler_params=params(),
        cost_estimate=cost(2 * rows * rows * depth, 4 * rows * depth),
    )(in_hbm(queries), in_hbm(precond), in_hbm(rank))


def scores_kernel(pieces, fresh, loading, counted, sides, *refs):
    count = len(fresh)
    if counted:
        valid, *refs, limit = refs
        limit[...] = jnp.full(limit.shape, valid[0], jnp.int32)
    odd = lax.rem(lax.axis_index("ex"), 2) == 1
    loads = []
    if loading:
        store, *refs = refs
        *refs, other, mine, arrived = refs
        stores = other, mine
        half = other.shape[0]
        me = lax.axis_index("dim")
        for side, where in enumerate((1 - me, me)):
            place = pl.ds(pl.multiple_of(where * half, half), half)
            loads.append(pltpu.make_async_copy(store.at[place], stores[side], arrived.at[side]))
            loads[side].start()
    else:
        other, mine, *refs = refs
        stores = other, mine
    count_out = len(sides) * count
    outs = refs[-count_out:]
    carried = refs[-count_out - len(sides) * (count - sum(fresh)):-count_out]
    cuts = cuts_of(other.shape[1])
    stacks = []
    for n, targets in pieces:
        values = []
        for _, even_place, odd_place in targets:
            value = refs[even_place][...]
            if odd_place != even_place:
                value = jnp.where(odd, refs[odd_place][...], value)
            values.append(value)
        stacked = values[0] if len(values) == 1 else jnp.concatenate(values, axis=0)
        stacks.append((n, [which for which, _, _ in targets], stacked))
    for at_side, side in enumerate(sides):
        store = stores[side]
        if loading:
            loads[side].wait()
        sums, at = {}, 0
        for i, new in enumerate(fresh):
            sums[i] = None if new else carried[at + at_side][...]
            at += 0 if new else len(sides)
        for n, whiches, stacked in stacks:
            part = product(store[:, cuts[n]], stacked)
            columns = stacked.shape[0] // len(whiches)
            for k, i in enumerate(whiches):
                here = part[:, k * columns:(k + 1) * columns]
                sums[i] = here if sums[i] is None else sums[i] + here
        for i in range(count):
            outs[len(sides) * i + at_side][...] = sums[i]


def more_scores(stores, pieces, carries, valid=None, sides=(0, 1)):
    operands, placed = [], []

    def place(block):
        known = [i for i, operand in enumerate(operands) if operand is block]
        if not known:
            operands.append(block)
        return known[0] if known else len(operands) - 1

    loading = not isinstance(stores, tuple)
    half, depth = stores.shape[0] // 2 if loading else stores[0].shape[0], 0
    flops = 0
    for n, targets in pieces:
        kept = []
        for which, *blocks in targets:
            places = [place(block) for block in blocks]
            kept.append((which, places[0], places[-1]))
            flops += 4 * half * blocks[0].size
        placed.append((n, tuple(kept)))
    columns = operands[0].shape[0]
    fresh = tuple(carry is None for carry in carries)
    first = [in_hbm(stores)] if loading else list(stores)
    operands += [carry[side] for carry in carries if carry for side in sides]
    specs = [far_spec()] if loading else [whole_spec()] * 2
    total = jax.ShapeDtypeStruct((half, columns), jnp.float32)
    more = []
    if loading:
        held = jax.ShapeDtypeStruct((half, stores.shape[1]), stores.dtype)
        more = [held, held]
    if valid is not None:
        first, more = [valid] + first, more + [jax.ShapeDtypeStruct((8, columns), jnp.int32)]
        specs = [pl.BlockSpec(memory_space=pltpu.SMEM)] + specs
    count = len(sides) * len(carries)
    outs = pl.pallas_call(
        functools.partial(scores_kernel, tuple(placed), fresh, loading, valid is not None, sides),
        out_shape=[total] * count + more,
        in_specs=specs + [whole_spec()] * len(operands),
        out_specs=[whole_spec()] * (count + len(more)),
        scratch_shapes=[pltpu.SemaphoreType.DMA((2,))] if loading else [],
        compiler_params=params(),
        cost_estimate=cost(flops, 4 * half * columns * count),
    )(*first, *operands)
    totals = [tuple(outs[i:i + len(sides)]) for i in range(0, count, len(sides))]
    if valid is not None:
        return totals + [outs[-1]]
    return totals + ([tuple(outs[count:])] if loading else [])


def finish_kernel(places, limit, *refs):
    out, summed, left = refs[-3:]
    half, columns = refs[0].shape
    row_ids = lax.broadcasted_iota(jnp.int32, (half, columns), 0) + lax.axis_index("dim") * half
    inside = row_ids < limit[:1, :]
    stores = []
    for n, place in enumerate(places):
        cut = slice(n * columns, (n + 1) * columns)
        summed[:, cut] = jnp.where(inside, refs[2 * n][...] + refs[2 * n + 1][...], 0.0)
        to = out.at[:, place * columns:(place + 1) * columns]
        stores.append(pltpu.make_async_copy(summed.at[:, cut], to, left.at[n]))
        stores[n].start()
    for store in stores:
        store.wait()


def finish(limit, pairs, places, steps, out=None):
    half, columns = pairs[0][0].shape
    operands = [ref for pair in pairs for ref in pair]
    given = [] if out is None else [in_hbm(out)]
    return pl.pallas_call(
        functools.partial(finish_kernel, places),
        out_shape=pltpu.HBM((half, columns * steps), jnp.float32),
        in_specs=[whole_spec()] * (1 + len(operands))
        + [far_spec()] * len(given),
        out_specs=far_spec(),
        scratch_shapes=[
            pltpu.VMEM((half, columns * len(places)), jnp.float32),
            pltpu.SemaphoreType.DMA((len(places),)),
        ],
        input_output_aliases={1 + len(operands): 0} if given else {},
        compiler_params=params(),
        cost_estimate=cost(half * columns * len(pairs), 12 * half * columns * len(pairs)),
    )(limit, *operands, *given)


def after(x, *earlier):
    return lax.optimization_barrier((x, *earlier))[0]


def shards(store, queries, precond, query_rank, valid_rows):
    size = lax.axis_size("ex")
    odd = lax.rem(lax.axis_index("ex"), 2) == 1
    one_ahead = [(i, (i + 1) % size) for i in range(size)]
    ahead = [(i, (i + 2) % size) for i in range(size)]
    even_ahead = ahead[::2]
    swap = [(i, i ^ 1) for i in range(size)]
    over_dim = [(0, 1), (1, 0)]

    def send(block, route, axis="ex"):
        return lax.ppermute(block, axis, route)

    def exchanged(total):
        theirs, ours = total
        return ours, send(theirs, over_dim, "dim")

    def by_parity(at_even, at_odd):
        return jnp.where(odd, at_odd, at_even)

    own = prepare(queries, precond[None, :], query_rank)
    first, stores = more_scores(store, [(n, [(0, own[n])]) for n in range(CHUNKS)], [None])
    own_pair = exchanged(first)
    moved = {}

    def tied(name, block):
        earlier = [first[1]] if name == EARLY else []
        return after(block, *earlier, *(moved[key] for key in TIES.get(name, "").split()))

    def move(name, block, route):
        moved[name] = send(tied(name, block), route)
        return moved[name]

    one_back, three_back, two_back = {}, {}, {}
    for step in ORDER:
        kind, n = step[0], int(step[1:])
        if kind == "B":
            two_back[n] = move(step, own[n], ahead)
        elif kind == "A":
            move(step, own[n], swap)
        elif kind == "C":
            block = two_back[n] if KINDS[n] != "U" else by_parity(own[n], two_back[n])
            move(step, block, swap)
        elif kind == "Z":
            move(step, moved[f"A{n}"], even_ahead)
        elif kind == "E":
            move(step, moved[f"C{n}"], even_ahead if KINDS[n] == "I" else ahead)
        else:
            block = two_back[n] if KINDS[n] == "V" else by_parity(own[n], two_back[n])
            move(step, block, one_ahead)
    for n, kind in enumerate(KINDS):
        if kind == "V":
            one_back[n], three_back[n] = (moved[f"Z{n}"], moved[f"A{n}"]), (moved[f"R{n}"],)
            continue
        swapped = moved[f"C{n}"]
        if kind == "U":
            one_back[n], three_back[n] = (swapped,), (moved[f"E{n}"],)
        elif kind == "I":
            one_back[n], three_back[n] = (swapped, moved[f"A{n}"]), (moved[f"E{n}"], swapped)
        else:
            direct = moved[f"R{n}"]
            one_back[n], three_back[n] = (swapped, direct), (direct, swapped)

    [two] = more_scores(stores, [(n, [(0, two_back[n])]) for n in range(CHUNKS)], [None])
    two_pair = exchanged(two)
    limited = after(valid_rows, two[1])
    one = three = one_pair = None
    todo = set(range(CHUNKS))
    for group in CHAIN:
        pieces = []
        for item in group.split():
            n, parts = int(item[1:]), {"b": (0, 1), "o": (0,), "t": (1,)}[item[0]]
            blocks = one_back[n], three_back[n]
            pieces.append((n, [(part, *blocks[part]) for part in parts]))
            todo -= {n} if 0 in parts else set()
        if one is None:
            one, three, limit = more_scores(stores, pieces, [one, three], limited)
        elif one_pair is None:
            one, three = more_scores(stores, pieces, [one, three])
        else:
            pieces = [(n, [(0, *blocks) for _, *blocks in targets]) for n, targets in pieces]
            [[theirs]] = more_scores(stores, pieces, [three], sides=(0,))
            [[ours]] = more_scores(stores, pieces, [three], sides=(1,))
            three = theirs, ours
        if one_pair is None and not todo:
            one_pair = exchanged(one)
    out = finish(limit, [own_pair, two_pair], (0, 2), STEPS)
    return finish(limit, [one_pair, exchanged(three)], (1, 3), STEPS, out)


def solution(mesh):
    return jax.shard_map(
        shards,
        mesh=mesh,
        in_specs=(
            P(("groups", "ex"), "dim"),
            P(("groups", "ex"), "dim"),
            P("dim"),
            P(("groups", "ex"), None),
            P(("groups", "ex")),
        ),
        out_specs=P(("groups", "ex", "dim"), None),
        check_vma=False,
    )
```

```python
import functools

import jax
import jax.numpy as jnp
from jax import lax
from jax.experimental import pallas as pl
from jax.experimental.pallas import tpu as pltpu
from jax.sharding import PartitionSpec as P

STEPS = 4
KINDS = "UUT"
PARTS = (4, 6, 6)
CHAIN = ("b0", "o1", "b2", "t1")
ORDER = ("B0", "B1", "B2", "C0", "C1", "E0", "E1", "R2", "C2")
TIES = {"C2": "C0", "E1": "E0"}
EARLY = "C0"
OUT = "none"
CHUNKS = len(PARTS)
VMEM_BYTES = 16 * 1024 * 1024


def params():
    return pltpu.CompilerParams(vmem_limit_bytes=VMEM_BYTES)


def whole_spec():
    return pl.BlockSpec(memory_space=pltpu.VMEM)


def far_spec():
    return pl.BlockSpec(memory_space=pltpu.HBM)


def in_hbm(x):
    return pltpu.with_memory_space_constraint(x, pltpu.HBM)


def cost(flops, traffic):
    return pl.CostEstimate(flops=flops, bytes_accessed=traffic, transcendentals=0)


def cuts_of(depth):
    ends = [depth * sum(PARTS[:n + 1]) // sum(PARTS) for n in range(CHUNKS)]
    return [slice(start, end) for start, end in zip([0] + ends, ends)]


def product(rows, block):
    return lax.dot_general(
        rows, block, (((1,), (1,)), ((), ())), preferred_element_type=jnp.float32
    )


def prepare_kernel(queries, precond, rank, *refs):
    chunks, (held, scale, places, arrived) = refs[:CHUNKS], refs[CHUNKS:]
    rows, depth = queries.shape
    cuts = cuts_of(depth)
    loads = [pltpu.make_async_copy(rank, places, arrived.at[CHUNKS])]
    loads.append(pltpu.make_async_copy(precond, scale, arrived.at[CHUNKS + 1]))
    for n, cut in enumerate(cuts):
        loads.append(pltpu.make_async_copy(queries.at[:, cut], held.at[:, cut], arrived.at[n]))
    for load in loads:
        load.start()
    loads[0].wait()
    loads[1].wait()
    positions = lax.broadcasted_iota(jnp.int32, (rows, rows), 0)
    placing = (positions == places[...]).astype(jnp.bfloat16)
    for n, cut in enumerate(cuts):
        loads[2 + n].wait()
        pre = (held[:, cut].astype(jnp.float32) * scale[:, cut]).astype(jnp.bfloat16)
        chunks[n][...] = jnp.dot(placing, pre, preferred_element_type=jnp.float32).astype(
            jnp.bfloat16
        )


def prepare(queries, precond, rank):
    rows, depth = queries.shape
    shapes = [
        jax.ShapeDtypeStruct((rows, cut.stop - cut.start), jnp.bfloat16) for cut in cuts_of(depth)
    ]
    return pl.pallas_call(
        prepare_kernel,
        out_shape=shapes,
        in_specs=[far_spec()] * 3,
        out_specs=[whole_spec()] * CHUNKS,
        scratch_shapes=[
            pltpu.VMEM((rows, depth), jnp.bfloat16),
            pltpu.VMEM((1, depth), jnp.float32),
            pltpu.VMEM((1, rows), jnp.int32),
            pltpu.SemaphoreType.DMA((CHUNKS + 2,)),
        ],
        compiler_params=params(),
        cost_estimate=cost(2 * rows * rows * depth, 4 * rows * depth),
    )(in_hbm(queries), in_hbm(precond), in_hbm(rank))


def scores_kernel(pieces, fresh, loading, counted, sides, *refs):
    count = len(fresh)
    if counted:
        valid, *refs, limit = refs
        limit[...] = jnp.full(limit.shape, valid[0], jnp.int32)
    odd = lax.rem(lax.axis_index("ex"), 2) == 1
    loads = []
    if loading:
        store, *refs = refs
        *refs, other, mine, arrived = refs
        stores = other, mine
        half = other.shape[0]
        me = lax.axis_index("dim")
        for side, where in enumerate((1 - me, me)):
            place = pl.ds(pl.multiple_of(where * half, half), half)
            loads.append(pltpu.make_async_copy(store.at[place], stores[side], arrived.at[side]))
            loads[side].start()
    else:
        other, mine, *refs = refs
        stores = other, mine
    count_out = len(sides) * count
    outs = refs[-count_out:]
    carried = refs[-count_out - len(sides) * (count - sum(fresh)):-count_out]
    cuts = cuts_of(other.shape[1])
    stacks = []
    for n, targets in pieces:
        values = []
        for _, even_place, odd_place in targets:
            value = refs[even_place][...]
            if odd_place != even_place:
                value = jnp.where(odd, refs[odd_place][...], value)
            values.append(value)
        stacked = values[0] if len(values) == 1 else jnp.concatenate(values, axis=0)
        stacks.append((n, [which for which, _, _ in targets], stacked))
    for at_side, side in enumerate(sides):
        store = stores[side]
        if loading:
            loads[side].wait()
        sums, at = {}, 0
        for i, new in enumerate(fresh):
            sums[i] = None if new else carried[at + at_side][...]
            at += 0 if new else len(sides)
        for n, whiches, stacked in stacks:
            part = product(store[:, cuts[n]], stacked)
            columns = stacked.shape[0] // len(whiches)
            for k, i in enumerate(whiches):
                here = part[:, k * columns:(k + 1) * columns]
                sums[i] = here if sums[i] is None else sums[i] + here
        for i in range(count):
            outs[len(sides) * i + at_side][...] = sums[i]


def more_scores(stores, pieces, carries, valid=None, sides=(0, 1)):
    operands, placed = [], []

    def place(block):
        known = [i for i, operand in enumerate(operands) if operand is block]
        if not known:
            operands.append(block)
        return known[0] if known else len(operands) - 1

    loading = not isinstance(stores, tuple)
    half, depth = stores.shape[0] // 2 if loading else stores[0].shape[0], 0
    flops = 0
    for n, targets in pieces:
        kept = []
        for which, *blocks in targets:
            places = [place(block) for block in blocks]
            kept.append((which, places[0], places[-1]))
            flops += 4 * half * blocks[0].size
        placed.append((n, tuple(kept)))
    columns = operands[0].shape[0]
    fresh = tuple(carry is None for carry in carries)
    first = [in_hbm(stores)] if loading else list(stores)
    operands += [carry[side] for carry in carries if carry for side in sides]
    specs = [far_spec()] if loading else [whole_spec()] * 2
    total = jax.ShapeDtypeStruct((half, columns), jnp.float32)
    more = []
    if loading:
        held = jax.ShapeDtypeStruct((half, stores.shape[1]), stores.dtype)
        more = [held, held]
    if valid is not None:
        first, more = [valid] + first, more + [jax.ShapeDtypeStruct((8, columns), jnp.int32)]
        specs = [pl.BlockSpec(memory_space=pltpu.SMEM)] + specs
    count = len(sides) * len(carries)
    outs = pl.pallas_call(
        functools.partial(scores_kernel, tuple(placed), fresh, loading, valid is not None, sides),
        out_shape=[total] * count + more,
        in_specs=specs + [whole_spec()] * len(operands),
        out_specs=[whole_spec()] * (count + len(more)),
        scratch_shapes=[pltpu.SemaphoreType.DMA((2,))] if loading else [],
        compiler_params=params(),
        cost_estimate=cost(flops, 4 * half * columns * count),
    )(*first, *operands)
    totals = [tuple(outs[i:i + len(sides)]) for i in range(0, count, len(sides))]
    if valid is not None:
        return totals + [outs[-1]]
    return totals + ([tuple(outs[count:])] if loading else [])


def finish_kernel(places, limit, *refs):
    out, summed, left = refs[-3:]
    half, columns = refs[0].shape
    row_ids = lax.broadcasted_iota(jnp.int32, (half, columns), 0) + lax.axis_index("dim") * half
    inside = row_ids < limit[:1, :]
    stores = []
    for n, place in enumerate(places):
        cut = slice(n * columns, (n + 1) * columns)
        summed[:, cut] = jnp.where(inside, refs[2 * n][...] + refs[2 * n + 1][...], 0.0)
        to = out.at[:, place * columns:(place + 1) * columns]
        stores.append(pltpu.make_async_copy(summed.at[:, cut], to, left.at[n]))
        stores[n].start()
    for store in stores:
        store.wait()


def finish(limit, pairs, places, steps, out=None):
    half, columns = pairs[0][0].shape
    operands = [ref for pair in pairs for ref in pair]
    given = [] if out is None else [in_hbm(out)]
    return pl.pallas_call(
        functools.partial(finish_kernel, places),
        out_shape=pltpu.HBM((half, columns * steps), jnp.float32),
        in_specs=[whole_spec()] * (1 + len(operands))
        + [far_spec()] * len(given),
        out_specs=far_spec(),
        scratch_shapes=[
            pltpu.VMEM((half, columns * len(places)), jnp.float32),
            pltpu.SemaphoreType.DMA((len(places),)),
        ],
        input_output_aliases={1 + len(operands): 0} if given else {},
        compiler_params=params(),
        cost_estimate=cost(half * columns * len(pairs), 12 * half * columns * len(pairs)),
    )(limit, *operands, *given)


def after(x, *earlier):
    return lax.optimization_barrier((x, *earlier))[0]


def shards(store, queries, precond, query_rank, valid_rows):
    size = lax.axis_size("ex")
    odd = lax.rem(lax.axis_index("ex"), 2) == 1
    one_ahead = [(i, (i + 1) % size) for i in range(size)]
    ahead = [(i, (i + 2) % size) for i in range(size)]
    even_ahead = ahead[::2]
    swap = [(i, i ^ 1) for i in range(size)]
    over_dim = [(0, 1), (1, 0)]

    def send(block, route, axis="ex"):
        return lax.ppermute(block, axis, route)

    def exchanged(total):
        theirs, ours = total
        return ours, send(theirs, over_dim, "dim")

    def by_parity(at_even, at_odd):
        return jnp.where(odd, at_odd, at_even)

    own = prepare(queries, precond[None, :], query_rank)
    first, stores = more_scores(store, [(n, [(0, own[n])]) for n in range(CHUNKS)], [None])
    own_pair = exchanged(first)
    moved = {}

    def tied(name, block):
        earlier = [first[1]] if name == EARLY else []
        return after(block, *earlier, *(moved[key] for key in TIES.get(name, "").split()))

    def move(name, block, route):
        moved[name] = send(tied(name, block), route)
        return moved[name]

    one_back, three_back, two_back = {}, {}, {}
    for step in ORDER:
        kind, n = step[0], int(step[1:])
        if kind == "B":
            two_back[n] = move(step, own[n], ahead)
        elif kind == "A":
            move(step, own[n], swap)
        elif kind == "C":
            block = two_back[n] if KINDS[n] != "U" else by_parity(own[n], two_back[n])
            move(step, block, swap)
        elif kind == "Z":
            move(step, moved[f"A{n}"], even_ahead)
        elif kind == "E":
            move(step, moved[f"C{n}"], even_ahead if KINDS[n] == "I" else ahead)
        else:
            block = two_back[n] if KINDS[n] == "V" else by_parity(own[n], two_back[n])
            move(step, block, one_ahead)
    for n, kind in enumerate(KINDS):
        if kind == "V":
            one_back[n], three_back[n] = (moved[f"Z{n}"], moved[f"A{n}"]), (moved[f"R{n}"],)
            continue
        swapped = moved[f"C{n}"]
        if kind == "U":
            one_back[n], three_back[n] = (swapped,), (moved[f"E{n}"],)
        elif kind == "I":
            one_back[n], three_back[n] = (swapped, moved[f"A{n}"]), (moved[f"E{n}"], swapped)
        else:
            direct = moved[f"R{n}"]
            one_back[n], three_back[n] = (swapped, direct), (direct, swapped)

    [two] = more_scores(stores, [(n, [(0, two_back[n])]) for n in range(CHUNKS)], [None])
    two_pair = exchanged(two)
    limited = after(valid_rows, two[1])
    one = three = one_pair = None
    todo, out = set(range(CHUNKS)), None
    for group in CHAIN:
        pieces = []
        if group == OUT:
            out = finish(limit, [own_pair, two_pair], (0, 2), STEPS)
            one = after(one[0], out), one[1]
        for item in group.split():
            n, parts = int(item[1:]), {"b": (0, 1), "o": (0,), "t": (1,)}[item[0]]
            blocks = one_back[n], three_back[n]
            pieces.append((n, [(part, *blocks[part]) for part in parts]))
            todo -= {n} if 0 in parts else set()
        if one is None:
            one, three, limit = more_scores(stores, pieces, [one, three], limited)
        elif one_pair is None:
            one, three = more_scores(stores, pieces, [one, three])
        else:
            pieces = [(n, [(0, *blocks) for _, *blocks in targets]) for n, targets in pieces]
            [[theirs]] = more_scores(stores, pieces, [three], sides=(0,))
            [[ours]] = more_scores(stores, pieces, [three], sides=(1,))
            three = theirs, ours
        if one_pair is None and not todo:
            one_pair = exchanged(one)
    if out is None:
        out = finish(limit, [own_pair, two_pair], (0, 2), STEPS)
    return finish(limit, [one_pair, exchanged(three)], (1, 3), STEPS, out)


def solution(mesh):
    return jax.shard_map(
        shards,
        mesh=mesh,
        in_specs=(
            P(("groups", "ex"), "dim"),
            P(("groups", "ex"), "dim"),
            P("dim"),
            P(("groups", "ex"), None),
            P(("groups", "ex")),
        ),
        out_specs=P(("groups", "ex", "dim"), None),
        check_vma=False,
    )
```

```python
import functools

import jax
import jax.numpy as jnp
from jax import lax
from jax.experimental import pallas as pl
from jax.experimental.pallas import tpu as pltpu
from jax.sharding import PartitionSpec as P

STEPS = 4
KINDS = "UUT"
PARTS = (5, 5, 6)
CHAIN = ("b0", "o1", "b2", "t1")
ORDER = ("B0", "B1", "B2", "C0", "C1", "E0", "E1", "R2", "C2")
TIES = {"C2": "C0"}
EARLY = "C0"
OUT = "none"
CHUNKS = len(PARTS)
VMEM_BYTES = 16 * 1024 * 1024


def params():
    return pltpu.CompilerParams(vmem_limit_bytes=VMEM_BYTES)


def whole_spec():
    return pl.BlockSpec(memory_space=pltpu.VMEM)


def far_spec():
    return pl.BlockSpec(memory_space=pltpu.HBM)


def in_hbm(x):
    return pltpu.with_memory_space_constraint(x, pltpu.HBM)


def cost(flops, traffic):
    return pl.CostEstimate(flops=flops, bytes_accessed=traffic, transcendentals=0)


def cuts_of(depth):
    ends = [depth * sum(PARTS[:n + 1]) // sum(PARTS) for n in range(CHUNKS)]
    return [slice(start, end) for start, end in zip([0] + ends, ends)]


def product(rows, block):
    return lax.dot_general(
        rows, block, (((1,), (1,)), ((), ())), preferred_element_type=jnp.float32
    )


def prepare_kernel(queries, precond, rank, *refs):
    chunks, (held, scale, places, arrived) = refs[:CHUNKS], refs[CHUNKS:]
    rows, depth = queries.shape
    cuts = cuts_of(depth)
    loads = [pltpu.make_async_copy(rank, places, arrived.at[CHUNKS])]
    loads.append(pltpu.make_async_copy(precond, scale, arrived.at[CHUNKS + 1]))
    for n, cut in enumerate(cuts):
        loads.append(pltpu.make_async_copy(queries.at[:, cut], held.at[:, cut], arrived.at[n]))
    for load in loads:
        load.start()
    loads[0].wait()
    loads[1].wait()
    positions = lax.broadcasted_iota(jnp.int32, (rows, rows), 0)
    placing = (positions == places[...]).astype(jnp.bfloat16)
    for n, cut in enumerate(cuts):
        loads[2 + n].wait()
        pre = (held[:, cut].astype(jnp.float32) * scale[:, cut]).astype(jnp.bfloat16)
        chunks[n][...] = jnp.dot(placing, pre, preferred_element_type=jnp.float32).astype(
            jnp.bfloat16
        )


def prepare(queries, precond, rank):
    rows, depth = queries.shape
    shapes = [
        jax.ShapeDtypeStruct((rows, cut.stop - cut.start), jnp.bfloat16) for cut in cuts_of(depth)
    ]
    return pl.pallas_call(
        prepare_kernel,
        out_shape=shapes,
        in_specs=[far_spec()] * 3,
        out_specs=[whole_spec()] * CHUNKS,
        scratch_shapes=[
            pltpu.VMEM((rows, depth), jnp.bfloat16),
            pltpu.VMEM((1, depth), jnp.float32),
            pltpu.VMEM((1, rows), jnp.int32),
            pltpu.SemaphoreType.DMA((CHUNKS + 2,)),
        ],
        compiler_params=params(),
        cost_estimate=cost(2 * rows * rows * depth, 4 * rows * depth),
    )(in_hbm(queries), in_hbm(precond), in_hbm(rank))


def scores_kernel(pieces, fresh, loading, counted, sides, *refs):
    count = len(fresh)
    if counted:
        valid, *refs, limit = refs
        limit[...] = jnp.full(limit.shape, valid[0], jnp.int32)
    odd = lax.rem(lax.axis_index("ex"), 2) == 1
    loads = []
    if loading:
        store, *refs = refs
        *refs, other, mine, arrived = refs
        stores = other, mine
        half = other.shape[0]
        me = lax.axis_index("dim")
        for side, where in enumerate((1 - me, me)):
            place = pl.ds(pl.multiple_of(where * half, half), half)
            loads.append(pltpu.make_async_copy(store.at[place], stores[side], arrived.at[side]))
            loads[side].start()
    else:
        other, mine, *refs = refs
        stores = other, mine
    count_out = len(sides) * count
    outs = refs[-count_out:]
    carried = refs[-count_out - len(sides) * (count - sum(fresh)):-count_out]
    cuts = cuts_of(other.shape[1])
    stacks = []
    for n, targets in pieces:
        values = []
        for _, even_place, odd_place in targets:
            value = refs[even_place][...]
            if odd_place != even_place:
                value = jnp.where(odd, refs[odd_place][...], value)
            values.append(value)
        stacked = values[0] if len(values) == 1 else jnp.concatenate(values, axis=0)
        stacks.append((n, [which for which, _, _ in targets], stacked))
    for at_side, side in enumerate(sides):
        store = stores[side]
        if loading:
            loads[side].wait()
        sums, at = {}, 0
        for i, new in enumerate(fresh):
            sums[i] = None if new else carried[at + at_side][...]
            at += 0 if new else len(sides)
        for n, whiches, stacked in stacks:
            part = product(store[:, cuts[n]], stacked)
            columns = stacked.shape[0] // len(whiches)
            for k, i in enumerate(whiches):
                here = part[:, k * columns:(k + 1) * columns]
                sums[i] = here if sums[i] is None else sums[i] + here
        for i in range(count):
            outs[len(sides) * i + at_side][...] = sums[i]


def more_scores(stores, pieces, carries, valid=None, sides=(0, 1)):
    operands, placed = [], []

    def place(block):
        known = [i for i, operand in enumerate(operands) if operand is block]
        if not known:
            operands.append(block)
        return known[0] if known else len(operands) - 1

    loading = not isinstance(stores, tuple)
    half, depth = stores.shape[0] // 2 if loading else stores[0].shape[0], 0
    flops = 0
    for n, targets in pieces:
        kept = []
        for which, *blocks in targets:
            places = [place(block) for block in blocks]
            kept.append((which, places[0], places[-1]))
            flops += 4 * half * blocks[0].size
        placed.append((n, tuple(kept)))
    columns = operands[0].shape[0]
    fresh = tuple(carry is None for carry in carries)
    first = [in_hbm(stores)] if loading else list(stores)
    operands += [carry[side] for carry in carries if carry for side in sides]
    specs = [far_spec()] if loading else [whole_spec()] * 2
    total = jax.ShapeDtypeStruct((half, columns), jnp.float32)
    more = []
    if loading:
        held = jax.ShapeDtypeStruct((half, stores.shape[1]), stores.dtype)
        more = [held, held]
    if valid is not None:
        first, more = [valid] + first, more + [jax.ShapeDtypeStruct((8, columns), jnp.int32)]
        specs = [pl.BlockSpec(memory_space=pltpu.SMEM)] + specs
    count = len(sides) * len(carries)
    outs = pl.pallas_call(
        functools.partial(scores_kernel, tuple(placed), fresh, loading, valid is not None, sides),
        out_shape=[total] * count + more,
        in_specs=specs + [whole_spec()] * len(operands),
        out_specs=[whole_spec()] * (count + len(more)),
        scratch_shapes=[pltpu.SemaphoreType.DMA((2,))] if loading else [],
        compiler_params=params(),
        cost_estimate=cost(flops, 4 * half * columns * count),
    )(*first, *operands)
    totals = [tuple(outs[i:i + len(sides)]) for i in range(0, count, len(sides))]
    if valid is not None:
        return totals + [outs[-1]]
    return totals + ([tuple(outs[count:])] if loading else [])


def finish_kernel(places, limit, *refs):
    out, summed, left = refs[-3:]
    half, columns = refs[0].shape
    row_ids = lax.broadcasted_iota(jnp.int32, (half, columns), 0) + lax.axis_index("dim") * half
    inside = row_ids < limit[:1, :]
    stores = []
    for n, place in enumerate(places):
        cut = slice(n * columns, (n + 1) * columns)
        summed[:, cut] = jnp.where(inside, refs[2 * n][...] + refs[2 * n + 1][...], 0.0)
        to = out.at[:, place * columns:(place + 1) * columns]
        stores.append(pltpu.make_async_copy(summed.at[:, cut], to, left.at[n]))
        stores[n].start()
    for store in stores:
        store.wait()


def finish(limit, pairs, places, steps, out=None):
    half, columns = pairs[0][0].shape
    operands = [ref for pair in pairs for ref in pair]
    given = [] if out is None else [in_hbm(out)]
    return pl.pallas_call(
        functools.partial(finish_kernel, places),
        out_shape=pltpu.HBM((half, columns * steps), jnp.float32),
        in_specs=[whole_spec()] * (1 + len(operands))
        + [far_spec()] * len(given),
        out_specs=far_spec(),
        scratch_shapes=[
            pltpu.VMEM((half, columns * len(places)), jnp.float32),
            pltpu.SemaphoreType.DMA((len(places),)),
        ],
        input_output_aliases={1 + len(operands): 0} if given else {},
        compiler_params=params(),
        cost_estimate=cost(half * columns * len(pairs), 12 * half * columns * len(pairs)),
    )(limit, *operands, *given)


def after(x, *earlier):
    return lax.optimization_barrier((x, *earlier))[0]


def shards(store, queries, precond, query_rank, valid_rows):
    size = lax.axis_size("ex")
    odd = lax.rem(lax.axis_index("ex"), 2) == 1
    one_ahead = [(i, (i + 1) % size) for i in range(size)]
    ahead = [(i, (i + 2) % size) for i in range(size)]
    even_ahead = ahead[::2]
    swap = [(i, i ^ 1) for i in range(size)]
    over_dim = [(0, 1), (1, 0)]

    def send(block, route, axis="ex"):
        return lax.ppermute(block, axis, route)

    def exchanged(total):
        theirs, ours = total
        return ours, send(theirs, over_dim, "dim")

    def by_parity(at_even, at_odd):
        return jnp.where(odd, at_odd, at_even)

    own = prepare(queries, precond[None, :], query_rank)
    first, stores = more_scores(store, [(n, [(0, own[n])]) for n in range(CHUNKS)], [None])
    own_pair = exchanged(first)
    moved = {}

    def tied(name, block):
        earlier = [first[1]] if name == EARLY else []
        return after(block, *earlier, *(moved[key] for key in TIES.get(name, "").split()))

    def move(name, block, route):
        moved[name] = send(tied(name, block), route)
        return moved[name]

    one_back, three_back, two_back = {}, {}, {}
    for step in ORDER:
        kind, n = step[0], int(step[1:])
        if kind == "B":
            two_back[n] = move(step, own[n], ahead)
        elif kind == "A":
            move(step, own[n], swap)
        elif kind == "C":
            block = two_back[n] if KINDS[n] != "U" else by_parity(own[n], two_back[n])
            move(step, block, swap)
        elif kind == "Z":
            move(step, moved[f"A{n}"], even_ahead)
        elif kind == "E":
            move(step, moved[f"C{n}"], even_ahead if KINDS[n] == "I" else ahead)
        else:
            block = two_back[n] if KINDS[n] == "V" else by_parity(own[n], two_back[n])
            move(step, block, one_ahead)
    for n, kind in enumerate(KINDS):
        if kind == "V":
            one_back[n], three_back[n] = (moved[f"Z{n}"], moved[f"A{n}"]), (moved[f"R{n}"],)
            continue
        swapped = moved[f"C{n}"]
        if kind == "U":
            one_back[n], three_back[n] = (swapped,), (moved[f"E{n}"],)
        elif kind == "I":
            one_back[n], three_back[n] = (swapped, moved[f"A{n}"]), (moved[f"E{n}"], swapped)
        else:
            direct = moved[f"R{n}"]
            one_back[n], three_back[n] = (swapped, direct), (direct, swapped)

    [two] = more_scores(stores, [(n, [(0, two_back[n])]) for n in range(CHUNKS)], [None])
    two_pair = exchanged(two)
    limited = after(valid_rows, two[1])
    one = three = one_pair = None
    todo, out = set(range(CHUNKS)), None
    for group in CHAIN:
        pieces = []
        if group == OUT:
            out = finish(limit, [own_pair, two_pair], (0, 2), STEPS)
            one = after(one[0], out), one[1]
        for item in group.split():
            n, parts = int(item[1:]), {"b": (0, 1), "o": (0,), "t": (1,)}[item[0]]
            blocks = one_back[n], three_back[n]
            pieces.append((n, [(part, *blocks[part]) for part in parts]))
            todo -= {n} if 0 in parts else set()
        if one is None:
            one, three, limit = more_scores(stores, pieces, [one, three], limited)
        elif one_pair is None:
            one, three = more_scores(stores, pieces, [one, three])
        else:
            pieces = [(n, [(0, *blocks) for _, *blocks in targets]) for n, targets in pieces]
            [[theirs]] = more_scores(stores, pieces, [three], sides=(0,))
            [[ours]] = more_scores(stores, pieces, [three], sides=(1,))
            three = theirs, ours
        if one_pair is None and not todo:
            one_pair = exchanged(one)
    if out is None:
        out = finish(limit, [own_pair, two_pair], (0, 2), STEPS)
    return finish(limit, [one_pair, exchanged(three)], (1, 3), STEPS, out)


def solution(mesh):
    return jax.shard_map(
        shards,
        mesh=mesh,
        in_specs=(
            P(("groups", "ex"), "dim"),
            P(("groups", "ex"), "dim"),
            P("dim"),
            P(("groups", "ex"), None),
            P(("groups", "ex")),
        ),
        out_specs=P(("groups", "ex", "dim"), None),
        check_vma=False,
    )
```

```python
import functools

import jax
import jax.numpy as jnp
from jax import lax
from jax.experimental import pallas as pl
from jax.experimental.pallas import tpu as pltpu
from jax.sharding import PartitionSpec as P

STEPS = 4
KINDS = "UUT"
PARTS = (4, 6, 6)
CHAIN = ("b0", "o1", "b2", "t1")
ORDER = ("B0", "B1", "B2", "C0", "C1", "E0", "E1", "R2", "C2")
TIES = {"C2": "C0"}
EARLY = "C0"
OUT = "none"
WEIGHT = 2
CHUNKS = len(PARTS)
VMEM_BYTES = 16 * 1024 * 1024


def params():
    return pltpu.CompilerParams(vmem_limit_bytes=VMEM_BYTES)


def whole_spec():
    return pl.BlockSpec(memory_space=pltpu.VMEM)


def far_spec():
    return pl.BlockSpec(memory_space=pltpu.HBM)


def in_hbm(x):
    return pltpu.with_memory_space_constraint(x, pltpu.HBM)


def cost(flops, traffic):
    return pl.CostEstimate(flops=flops, bytes_accessed=traffic, transcendentals=0)


def cuts_of(depth):
    ends = [depth * sum(PARTS[:n + 1]) // sum(PARTS) for n in range(CHUNKS)]
    return [slice(start, end) for start, end in zip([0] + ends, ends)]


def product(rows, block):
    return lax.dot_general(
        rows, block, (((1,), (1,)), ((), ())), preferred_element_type=jnp.float32
    )


def prepare_kernel(queries, precond, rank, *refs):
    chunks, (held, scale, places, arrived) = refs[:CHUNKS], refs[CHUNKS:]
    rows, depth = queries.shape
    cuts = cuts_of(depth)
    loads = [pltpu.make_async_copy(rank, places, arrived.at[CHUNKS])]
    loads.append(pltpu.make_async_copy(precond, scale, arrived.at[CHUNKS + 1]))
    for n, cut in enumerate(cuts):
        loads.append(pltpu.make_async_copy(queries.at[:, cut], held.at[:, cut], arrived.at[n]))
    for load in loads:
        load.start()
    loads[0].wait()
    loads[1].wait()
    positions = lax.broadcasted_iota(jnp.int32, (rows, rows), 0)
    placing = (positions == places[...]).astype(jnp.bfloat16)
    for n, cut in enumerate(cuts):
        loads[2 + n].wait()
        pre = (held[:, cut].astype(jnp.float32) * scale[:, cut]).astype(jnp.bfloat16)
        chunks[n][...] = jnp.dot(placing, pre, preferred_element_type=jnp.float32).astype(
            jnp.bfloat16
        )


def prepare(queries, precond, rank):
    rows, depth = queries.shape
    shapes = [
        jax.ShapeDtypeStruct((rows, cut.stop - cut.start), jnp.bfloat16) for cut in cuts_of(depth)
    ]
    return pl.pallas_call(
        prepare_kernel,
        out_shape=shapes,
        in_specs=[far_spec()] * 3,
        out_specs=[whole_spec()] * CHUNKS,
        scratch_shapes=[
            pltpu.VMEM((rows, depth), jnp.bfloat16),
            pltpu.VMEM((1, depth), jnp.float32),
            pltpu.VMEM((1, rows), jnp.int32),
            pltpu.SemaphoreType.DMA((CHUNKS + 2,)),
        ],
        compiler_params=params(),
        cost_estimate=cost(2 * rows * rows * depth, 4 * rows * depth),
    )(in_hbm(queries), in_hbm(precond), in_hbm(rank))


def scores_kernel(pieces, fresh, loading, counted, sides, *refs):
    count = len(fresh)
    if counted:
        valid, *refs, limit = refs
        limit[...] = jnp.full(limit.shape, valid[0], jnp.int32)
    odd = lax.rem(lax.axis_index("ex"), 2) == 1
    loads = []
    if loading:
        store, *refs = refs
        *refs, other, mine, arrived = refs
        stores = other, mine
        half = other.shape[0]
        me = lax.axis_index("dim")
        for side, where in enumerate((1 - me, me)):
            place = pl.ds(pl.multiple_of(where * half, half), half)
            loads.append(pltpu.make_async_copy(store.at[place], stores[side], arrived.at[side]))
            loads[side].start()
    else:
        other, mine, *refs = refs
        stores = other, mine
    count_out = len(sides) * count
    outs = refs[-count_out:]
    carried = refs[-count_out - len(sides) * (count - sum(fresh)):-count_out]
    cuts = cuts_of(other.shape[1])
    stacks = []
    for n, targets in pieces:
        values = []
        for _, even_place, odd_place in targets:
            value = refs[even_place][...]
            if odd_place != even_place:
                value = jnp.where(odd, refs[odd_place][...], value)
            values.append(value)
        stacked = values[0] if len(values) == 1 else jnp.concatenate(values, axis=0)
        stacks.append((n, [which for which, _, _ in targets], stacked))
    for at_side, side in enumerate(sides):
        store = stores[side]
        if loading:
            loads[side].wait()
        sums, at = {}, 0
        for i, new in enumerate(fresh):
            sums[i] = None if new else carried[at + at_side][...]
            at += 0 if new else len(sides)
        for n, whiches, stacked in stacks:
            part = product(store[:, cuts[n]], stacked)
            columns = stacked.shape[0] // len(whiches)
            for k, i in enumerate(whiches):
                here = part[:, k * columns:(k + 1) * columns]
                sums[i] = here if sums[i] is None else sums[i] + here
        for i in range(count):
            outs[len(sides) * i + at_side][...] = sums[i]


def more_scores(stores, pieces, carries, valid=None, sides=(0, 1), weight=1):
    operands, placed = [], []

    def place(block):
        known = [i for i, operand in enumerate(operands) if operand is block]
        if not known:
            operands.append(block)
        return known[0] if known else len(operands) - 1

    loading = not isinstance(stores, tuple)
    half, depth = stores.shape[0] // 2 if loading else stores[0].shape[0], 0
    flops = 0
    for n, targets in pieces:
        kept = []
        for which, *blocks in targets:
            places = [place(block) for block in blocks]
            kept.append((which, places[0], places[-1]))
            flops += 4 * half * blocks[0].size
        placed.append((n, tuple(kept)))
    columns = operands[0].shape[0]
    fresh = tuple(carry is None for carry in carries)
    first = [in_hbm(stores)] if loading else list(stores)
    operands += [carry[side] for carry in carries if carry for side in sides]
    specs = [far_spec()] if loading else [whole_spec()] * 2
    total = jax.ShapeDtypeStruct((half, columns), jnp.float32)
    more = []
    if loading:
        held = jax.ShapeDtypeStruct((half, stores.shape[1]), stores.dtype)
        more = [held, held]
    if valid is not None:
        first, more = [valid] + first, more + [jax.ShapeDtypeStruct((8, columns), jnp.int32)]
        specs = [pl.BlockSpec(memory_space=pltpu.SMEM)] + specs
    count = len(sides) * len(carries)
    outs = pl.pallas_call(
        functools.partial(scores_kernel, tuple(placed), fresh, loading, valid is not None, sides),
        out_shape=[total] * count + more,
        in_specs=specs + [whole_spec()] * len(operands),
        out_specs=[whole_spec()] * (count + len(more)),
        scratch_shapes=[pltpu.SemaphoreType.DMA((2,))] if loading else [],
        compiler_params=params(),
        cost_estimate=cost(weight * flops, weight * 4 * half * columns * count),
    )(*first, *operands)
    totals = [tuple(outs[i:i + len(sides)]) for i in range(0, count, len(sides))]
    if valid is not None:
        return totals + [outs[-1]]
    return totals + ([tuple(outs[count:])] if loading else [])


def finish_kernel(places, limit, *refs):
    out, summed, left = refs[-3:]
    half, columns = refs[0].shape
    row_ids = lax.broadcasted_iota(jnp.int32, (half, columns), 0) + lax.axis_index("dim") * half
    inside = row_ids < limit[:1, :]
    stores = []
    for n, place in enumerate(places):
        cut = slice(n * columns, (n + 1) * columns)
        summed[:, cut] = jnp.where(inside, refs[2 * n][...] + refs[2 * n + 1][...], 0.0)
        to = out.at[:, place * columns:(place + 1) * columns]
        stores.append(pltpu.make_async_copy(summed.at[:, cut], to, left.at[n]))
        stores[n].start()
    for store in stores:
        store.wait()


def finish(limit, pairs, places, steps, out=None):
    half, columns = pairs[0][0].shape
    operands = [ref for pair in pairs for ref in pair]
    given = [] if out is None else [in_hbm(out)]
    return pl.pallas_call(
        functools.partial(finish_kernel, places),
        out_shape=pltpu.HBM((half, columns * steps), jnp.float32),
        in_specs=[whole_spec()] * (1 + len(operands))
        + [far_spec()] * len(given),
        out_specs=far_spec(),
        scratch_shapes=[
            pltpu.VMEM((half, columns * len(places)), jnp.float32),
            pltpu.SemaphoreType.DMA((len(places),)),
        ],
        input_output_aliases={1 + len(operands): 0} if given else {},
        compiler_params=params(),
        cost_estimate=cost(half * columns * len(pairs), 12 * half * columns * len(pairs)),
    )(limit, *operands, *given)


def after(x, *earlier):
    return lax.optimization_barrier((x, *earlier))[0]


def shards(store, queries, precond, query_rank, valid_rows):
    size = lax.axis_size("ex")
    odd = lax.rem(lax.axis_index("ex"), 2) == 1
    one_ahead = [(i, (i + 1) % size) for i in range(size)]
    ahead = [(i, (i + 2) % size) for i in range(size)]
    even_ahead = ahead[::2]
    swap = [(i, i ^ 1) for i in range(size)]
    over_dim = [(0, 1), (1, 0)]

    def send(block, route, axis="ex"):
        return lax.ppermute(block, axis, route)

    def exchanged(total):
        theirs, ours = total
        return ours, send(theirs, over_dim, "dim")

    def by_parity(at_even, at_odd):
        return jnp.where(odd, at_odd, at_even)

    own = prepare(queries, precond[None, :], query_rank)
    first, stores = more_scores(store, [(n, [(0, own[n])]) for n in range(CHUNKS)], [None])
    own_pair = exchanged(first)
    moved = {}

    def tied(name, block):
        earlier = [first[1]] if name == EARLY else []
        return after(block, *earlier, *(moved[key] for key in TIES.get(name, "").split()))

    def move(name, block, route):
        moved[name] = send(tied(name, block), route)
        return moved[name]

    one_back, three_back, two_back = {}, {}, {}
    for step in ORDER:
        kind, n = step[0], int(step[1:])
        if kind == "B":
            two_back[n] = move(step, own[n], ahead)
        elif kind == "A":
            move(step, own[n], swap)
        elif kind == "C":
            block = two_back[n] if KINDS[n] != "U" else by_parity(own[n], two_back[n])
            move(step, block, swap)
        elif kind == "Z":
            move(step, moved[f"A{n}"], even_ahead)
        elif kind == "E":
            move(step, moved[f"C{n}"], even_ahead if KINDS[n] == "I" else ahead)
        else:
            block = two_back[n] if KINDS[n] == "V" else by_parity(own[n], two_back[n])
            move(step, block, one_ahead)
    for n, kind in enumerate(KINDS):
        if kind == "V":
            one_back[n], three_back[n] = (moved[f"Z{n}"], moved[f"A{n}"]), (moved[f"R{n}"],)
            continue
        swapped = moved[f"C{n}"]
        if kind == "U":
            one_back[n], three_back[n] = (swapped,), (moved[f"E{n}"],)
        elif kind == "I":
            one_back[n], three_back[n] = (swapped, moved[f"A{n}"]), (moved[f"E{n}"], swapped)
        else:
            direct = moved[f"R{n}"]
            one_back[n], three_back[n] = (swapped, direct), (direct, swapped)

    [two] = more_scores(stores, [(n, [(0, two_back[n])]) for n in range(CHUNKS)], [None])
    two_pair = exchanged(two)
    limited = after(valid_rows, two[1])
    one = three = one_pair = None
    todo, out = set(range(CHUNKS)), None
    for group in CHAIN:
        pieces = []
        if group == OUT:
            out = finish(limit, [own_pair, two_pair], (0, 2), STEPS)
            one = after(one[0], out), one[1]
        for item in group.split():
            n, parts = int(item[1:]), {"b": (0, 1), "o": (0,), "t": (1,)}[item[0]]
            blocks = one_back[n], three_back[n]
            pieces.append((n, [(part, *blocks[part]) for part in parts]))
            todo -= {n} if 0 in parts else set()
        if one is None:
            one, three, limit = more_scores(
                stores, pieces, [one, three], limited, weight=WEIGHT
            )
        elif one_pair is None:
            one, three = more_scores(stores, pieces, [one, three], weight=WEIGHT)
        else:
            pieces = [(n, [(0, *blocks) for _, *blocks in targets]) for n, targets in pieces]
            [[theirs]] = more_scores(stores, pieces, [three], sides=(0,))
            [[ours]] = more_scores(stores, pieces, [three], sides=(1,))
            three = theirs, ours
        if one_pair is None and not todo:
            one_pair = exchanged(one)
    if out is None:
        out = finish(limit, [own_pair, two_pair], (0, 2), STEPS)
    return finish(limit, [one_pair, exchanged(three)], (1, 3), STEPS, out)


def solution(mesh):
    return jax.shard_map(
        shards,
        mesh=mesh,
        in_specs=(
            P(("groups", "ex"), "dim"),
            P(("groups", "ex"), "dim"),
            P("dim"),
            P(("groups", "ex"), None),
            P(("groups", "ex")),
        ),
        out_specs=P(("groups", "ex", "dim"), None),
        check_vma=False,
    )
```

```python
import functools

import jax
import jax.numpy as jnp
from jax import lax
from jax.experimental import pallas as pl
from jax.experimental.pallas import tpu as pltpu
from jax.sharding import PartitionSpec as P

STEPS = 4
KINDS = "UTU"
PARTS = (4, 6, 6)
CHAIN = ("b0", "o2", "b1", "t2")
ORDER = ("B0", "B2", "B1", "C0", "C2", "E0", "E2", "R1", "C1")
TIES = {"C1": "C0"}
EARLY = "C0"
WEIGHT = 2
CHUNKS = len(PARTS)
VMEM_BYTES = 16 * 1024 * 1024


def params():
    return pltpu.CompilerParams(vmem_limit_bytes=VMEM_BYTES)


def whole_spec():
    return pl.BlockSpec(memory_space=pltpu.VMEM)


def far_spec():
    return pl.BlockSpec(memory_space=pltpu.HBM)


def in_hbm(x):
    return pltpu.with_memory_space_constraint(x, pltpu.HBM)


def cost(flops, traffic):
    return pl.CostEstimate(flops=flops, bytes_accessed=traffic, transcendentals=0)


def cuts_of(depth):
    ends = [depth * sum(PARTS[:n + 1]) // sum(PARTS) for n in range(CHUNKS)]
    return [slice(start, end) for start, end in zip([0] + ends, ends)]


def product(rows, block):
    return lax.dot_general(
        rows, block, (((1,), (1,)), ((), ())), preferred_element_type=jnp.float32
    )


def prepare_kernel(queries, precond, rank, *refs):
    chunks, (held, scale, places, arrived) = refs[:CHUNKS], refs[CHUNKS:]
    rows, depth = queries.shape
    cuts = cuts_of(depth)
    loads = [pltpu.make_async_copy(rank, places, arrived.at[CHUNKS])]
    loads.append(pltpu.make_async_copy(precond, scale, arrived.at[CHUNKS + 1]))
    for n, cut in enumerate(cuts):
        loads.append(pltpu.make_async_copy(queries.at[:, cut], held.at[:, cut], arrived.at[n]))
    for load in loads:
        load.start()
    loads[0].wait()
    loads[1].wait()
    positions = lax.broadcasted_iota(jnp.int32, (rows, rows), 0)
    placing = (positions == places[...]).astype(jnp.bfloat16)
    for n, cut in enumerate(cuts):
        loads[2 + n].wait()
        pre = (held[:, cut].astype(jnp.float32) * scale[:, cut]).astype(jnp.bfloat16)
        chunks[n][...] = jnp.dot(placing, pre, preferred_element_type=jnp.float32).astype(
            jnp.bfloat16
        )


def prepare(queries, precond, rank):
    rows, depth = queries.shape
    shapes = [
        jax.ShapeDtypeStruct((rows, cut.stop - cut.start), jnp.bfloat16) for cut in cuts_of(depth)
    ]
    return pl.pallas_call(
        prepare_kernel,
        out_shape=shapes,
        in_specs=[far_spec()] * 3,
        out_specs=[whole_spec()] * CHUNKS,
        scratch_shapes=[
            pltpu.VMEM((rows, depth), jnp.bfloat16),
            pltpu.VMEM((1, depth), jnp.float32),
            pltpu.VMEM((1, rows), jnp.int32),
            pltpu.SemaphoreType.DMA((CHUNKS + 2,)),
        ],
        compiler_params=params(),
        cost_estimate=cost(2 * rows * rows * depth, 4 * rows * depth),
    )(in_hbm(queries), in_hbm(precond), in_hbm(rank))


def scores_kernel(pieces, fresh, loading, counted, sides, *refs):
    count = len(fresh)
    if counted:
        valid, *refs, limit = refs
        limit[...] = jnp.full(limit.shape, valid[0], jnp.int32)
    odd = lax.rem(lax.axis_index("ex"), 2) == 1
    loads = []
    if loading:
        store, *refs = refs
        *refs, other, mine, arrived = refs
        stores = other, mine
        half = other.shape[0]
        me = lax.axis_index("dim")
        for side, where in enumerate((1 - me, me)):
            place = pl.ds(pl.multiple_of(where * half, half), half)
            loads.append(pltpu.make_async_copy(store.at[place], stores[side], arrived.at[side]))
            loads[side].start()
    else:
        other, mine, *refs = refs
        stores = other, mine
    count_out = len(sides) * count
    outs = refs[-count_out:]
    carried = refs[-count_out - len(sides) * (count - sum(fresh)):-count_out]
    cuts = cuts_of(other.shape[1])
    stacks = []
    for n, targets in pieces:
        values = []
        for _, even_place, odd_place in targets:
            value = refs[even_place][...]
            if odd_place != even_place:
                value = jnp.where(odd, refs[odd_place][...], value)
            values.append(value)
        stacked = values[0] if len(values) == 1 else jnp.concatenate(values, axis=0)
        stacks.append((n, [which for which, _, _ in targets], stacked))
    for at_side, side in enumerate(sides):
        store = stores[side]
        if loading:
            loads[side].wait()
        sums, at = {}, 0
        for i, new in enumerate(fresh):
            sums[i] = None if new else carried[at + at_side][...]
            at += 0 if new else len(sides)
        for n, whiches, stacked in stacks:
            part = product(store[:, cuts[n]], stacked)
            columns = stacked.shape[0] // len(whiches)
            for k, i in enumerate(whiches):
                here = part[:, k * columns:(k + 1) * columns]
                sums[i] = here if sums[i] is None else sums[i] + here
        for i in range(count):
            outs[len(sides) * i + at_side][...] = sums[i]


def more_scores(stores, pieces, carries, valid=None, sides=(0, 1), weight=1):
    operands, placed = [], []

    def place(block):
        known = [i for i, operand in enumerate(operands) if operand is block]
        if not known:
            operands.append(block)
        return known[0] if known else len(operands) - 1

    loading = not isinstance(stores, tuple)
    half, depth = stores.shape[0] // 2 if loading else stores[0].shape[0], 0
    flops = 0
    for n, targets in pieces:
        kept = []
        for which, *blocks in targets:
            places = [place(block) for block in blocks]
            kept.append((which, places[0], places[-1]))
            flops += 4 * half * blocks[0].size
        placed.append((n, tuple(kept)))
    columns = operands[0].shape[0]
    fresh = tuple(carry is None for carry in carries)
    first = [in_hbm(stores)] if loading else list(stores)
    operands += [carry[side] for carry in carries if carry for side in sides]
    specs = [far_spec()] if loading else [whole_spec()] * 2
    total = jax.ShapeDtypeStruct((half, columns), jnp.float32)
    more = []
    if loading:
        held = jax.ShapeDtypeStruct((half, stores.shape[1]), stores.dtype)
        more = [held, held]
    if valid is not None:
        first, more = [valid] + first, more + [jax.ShapeDtypeStruct((8, columns), jnp.int32)]
        specs = [pl.BlockSpec(memory_space=pltpu.SMEM)] + specs
    count = len(sides) * len(carries)
    outs = pl.pallas_call(
        functools.partial(scores_kernel, tuple(placed), fresh, loading, valid is not None, sides),
        out_shape=[total] * count + more,
        in_specs=specs + [whole_spec()] * len(operands),
        out_specs=[whole_spec()] * (count + len(more)),
        scratch_shapes=[pltpu.SemaphoreType.DMA((2,))] if loading else [],
        compiler_params=params(),
        cost_estimate=cost(weight * flops, weight * 4 * half * columns * count),
    )(*first, *operands)
    totals = [tuple(outs[i:i + len(sides)]) for i in range(0, count, len(sides))]
    if valid is not None:
        return totals + [outs[-1]]
    return totals + ([tuple(outs[count:])] if loading else [])


def finish_kernel(places, limit, *refs):
    out, summed, left = refs[-3:]
    half, columns = refs[0].shape
    row_ids = lax.broadcasted_iota(jnp.int32, (half, columns), 0) + lax.axis_index("dim") * half
    inside = row_ids < limit[:1, :]
    stores = []
    for n, place in enumerate(places):
        cut = slice(n * columns, (n + 1) * columns)
        summed[:, cut] = jnp.where(inside, refs[2 * n][...] + refs[2 * n + 1][...], 0.0)
        to = out.at[:, place * columns:(place + 1) * columns]
        stores.append(pltpu.make_async_copy(summed.at[:, cut], to, left.at[n]))
        stores[n].start()
    for store in stores:
        store.wait()


def finish(limit, pairs, places, steps, out=None):
    half, columns = pairs[0][0].shape
    operands = [ref for pair in pairs for ref in pair]
    given = [] if out is None else [in_hbm(out)]
    return pl.pallas_call(
        functools.partial(finish_kernel, places),
        out_shape=pltpu.HBM((half, columns * steps), jnp.float32),
        in_specs=[whole_spec()] * (1 + len(operands))
        + [far_spec()] * len(given),
        out_specs=far_spec(),
        scratch_shapes=[
            pltpu.VMEM((half, columns * len(places)), jnp.float32),
            pltpu.SemaphoreType.DMA((len(places),)),
        ],
        input_output_aliases={1 + len(operands): 0} if given else {},
        compiler_params=params(),
        cost_estimate=cost(half * columns * len(pairs), 12 * half * columns * len(pairs)),
    )(limit, *operands, *given)


def after(x, *earlier):
    return lax.optimization_barrier((x, *earlier))[0]


def shards(store, queries, precond, query_rank, valid_rows):
    size = lax.axis_size("ex")
    odd = lax.rem(lax.axis_index("ex"), 2) == 1
    one_ahead = [(i, (i + 1) % size) for i in range(size)]
    ahead = [(i, (i + 2) % size) for i in range(size)]
    even_ahead = ahead[::2]
    swap = [(i, i ^ 1) for i in range(size)]
    over_dim = [(0, 1), (1, 0)]

    def send(block, route, axis="ex"):
        return lax.ppermute(block, axis, route)

    def exchanged(total):
        theirs, ours = total
        return ours, send(theirs, over_dim, "dim")

    def by_parity(at_even, at_odd):
        return jnp.where(odd, at_odd, at_even)

    own = prepare(queries, precond[None, :], query_rank)
    first, stores = more_scores(store, [(n, [(0, own[n])]) for n in range(CHUNKS)], [None])
    own_pair = exchanged(first)
    moved = {}

    def tied(name, block):
        earlier = [first[1]] if name == EARLY else []
        return after(block, *earlier, *(moved[key] for key in TIES.get(name, "").split()))

    def move(name, block, route):
        moved[name] = send(tied(name, block), route)
        return moved[name]

    one_back, three_back, two_back = {}, {}, {}
    for step in ORDER:
        kind, n = step[0], int(step[1:])
        if kind == "B":
            two_back[n] = move(step, own[n], ahead)
        elif kind == "A":
            move(step, own[n], swap)
        elif kind == "C":
            block = two_back[n] if KINDS[n] != "U" else by_parity(own[n], two_back[n])
            move(step, block, swap)
        elif kind == "Z":
            move(step, moved[f"A{n}"], even_ahead)
        elif kind == "E":
            move(step, moved[f"C{n}"], even_ahead if KINDS[n] == "I" else ahead)
        else:
            block = two_back[n] if KINDS[n] == "V" else by_parity(own[n], two_back[n])
            move(step, block, one_ahead)
    for n, kind in enumerate(KINDS):
        if kind == "V":
            one_back[n], three_back[n] = (moved[f"Z{n}"], moved[f"A{n}"]), (moved[f"R{n}"],)
            continue
        swapped = moved[f"C{n}"]
        if kind == "U":
            one_back[n], three_back[n] = (swapped,), (moved[f"E{n}"],)
        elif kind == "I":
            one_back[n], three_back[n] = (swapped, moved[f"A{n}"]), (moved[f"E{n}"], swapped)
        else:
            direct = moved[f"R{n}"]
            one_back[n], three_back[n] = (swapped, direct), (direct, swapped)

    [two] = more_scores(stores, [(n, [(0, two_back[n])]) for n in range(CHUNKS)], [None])
    two_pair = exchanged(two)
    limited = after(valid_rows, two[1])
    one = three = None
    def pieces_of(group):
        pieces = []
        for item in group.split():
            n, parts = int(item[1:]), {"b": (0, 1), "o": (0,), "t": (1,)}[item[0]]
            blocks = one_back[n], three_back[n]
            pieces.append((n, [(part, *blocks[part]) for part in parts]))
        return pieces

    for group in CHAIN[:-2]:
        if one is None:
            one, three, limit = more_scores(
                stores, pieces_of(group), [one, three], limited, weight=WEIGHT
            )
        else:
            one, three = more_scores(stores, pieces_of(group), [one, three], weight=WEIGHT)
    out = finish(limit, [own_pair], (0,), STEPS)
    one = after(one[0], out), one[1]
    late, last = pieces_of(CHAIN[-2]), pieces_of(CHAIN[-1])
    [one_theirs], [three_theirs] = more_scores(stores, late, [one, three], sides=(0,))
    one_came = send(one_theirs, over_dim, "dim")
    only = [(n, [(0, *blocks) for _, *blocks in targets]) for n, targets in last]
    [[three_theirs]] = more_scores(stores, only, [(three_theirs, None)], sides=(0,))
    three_came = send(three_theirs, over_dim, "dim")
    [one_ours], [three_ours] = more_scores(stores, late + last, [one, three], sides=(1,))
    return finish(limit, [(one_ours, one_came), two_pair, (three_ours, three_came)], (1, 2, 3), STEPS, out)


def solution(mesh):
    return jax.shard_map(
        shards,
        mesh=mesh,
        in_specs=(
            P(("groups", "ex"), "dim"),
            P(("groups", "ex"), "dim"),
            P("dim"),
            P(("groups", "ex"), None),
            P(("groups", "ex")),
        ),
        out_specs=P(("groups", "ex", "dim"), None),
        check_vma=False,
    )
```

```python
import functools

import jax
import jax.numpy as jnp
from jax import lax
from jax.experimental import pallas as pl
from jax.experimental.pallas import tpu as pltpu
from jax.sharding import PartitionSpec as P

STEPS = 4
KINDS = "UUT"
PARTS = (4, 6, 6)
CHAIN = ("b0", "o1", "b2", "t1")
ORDER = ("B0", "B1", "B2", "C0", "C1", "E0", "E1", "R2", "C2")
TIES = {"C2": "C0"}
EARLY = "C0"
WEIGHT = 2
CHUNKS = len(PARTS)
VMEM_BYTES = 16 * 1024 * 1024


def params():
    return pltpu.CompilerParams(vmem_limit_bytes=VMEM_BYTES)


def whole_spec():
    return pl.BlockSpec(memory_space=pltpu.VMEM)


def far_spec():
    return pl.BlockSpec(memory_space=pltpu.HBM)


def in_hbm(x):
    return pltpu.with_memory_space_constraint(x, pltpu.HBM)


def cost(flops, traffic):
    return pl.CostEstimate(flops=flops, bytes_accessed=traffic, transcendentals=0)


def cuts_of(depth):
    ends = [depth * sum(PARTS[:n + 1]) // sum(PARTS) for n in range(CHUNKS)]
    return [slice(start, end) for start, end in zip([0] + ends, ends)]


def product(rows, block):
    return lax.dot_general(
        rows, block, (((1,), (1,)), ((), ())), preferred_element_type=jnp.float32
    )


def prepare_kernel(queries, precond, rank, *refs):
    chunks, (held, scale, places, arrived) = refs[:CHUNKS], refs[CHUNKS:]
    rows, depth = queries.shape
    cuts = cuts_of(depth)
    loads = [pltpu.make_async_copy(rank, places, arrived.at[CHUNKS])]
    loads.append(pltpu.make_async_copy(precond, scale, arrived.at[CHUNKS + 1]))
    for n, cut in enumerate(cuts):
        loads.append(pltpu.make_async_copy(queries.at[:, cut], held.at[:, cut], arrived.at[n]))
    for load in loads:
        load.start()
    loads[0].wait()
    loads[1].wait()
    positions = lax.broadcasted_iota(jnp.int32, (rows, rows), 0)
    placing = (positions == places[...]).astype(jnp.bfloat16)
    for n, cut in enumerate(cuts):
        loads[2 + n].wait()
        pre = (held[:, cut].astype(jnp.float32) * scale[:, cut]).astype(jnp.bfloat16)
        chunks[n][...] = jnp.dot(placing, pre, preferred_element_type=jnp.float32).astype(
            jnp.bfloat16
        )


def prepare(queries, precond, rank):
    rows, depth = queries.shape
    shapes = [
        jax.ShapeDtypeStruct((rows, cut.stop - cut.start), jnp.bfloat16) for cut in cuts_of(depth)
    ]
    return pl.pallas_call(
        prepare_kernel,
        out_shape=shapes,
        in_specs=[far_spec()] * 3,
        out_specs=[whole_spec()] * CHUNKS,
        scratch_shapes=[
            pltpu.VMEM((rows, depth), jnp.bfloat16),
            pltpu.VMEM((1, depth), jnp.float32),
            pltpu.VMEM((1, rows), jnp.int32),
            pltpu.SemaphoreType.DMA((CHUNKS + 2,)),
        ],
        compiler_params=params(),
        cost_estimate=cost(2 * rows * rows * depth, 4 * rows * depth),
    )(in_hbm(queries), in_hbm(precond), in_hbm(rank))


def scores_kernel(pieces, fresh, loading, counted, sides, *refs):
    count = len(fresh)
    if counted:
        valid, *refs, limit = refs
        limit[...] = jnp.full(limit.shape, valid[0], jnp.int32)
    odd = lax.rem(lax.axis_index("ex"), 2) == 1
    loads = []
    if loading:
        store, *refs = refs
        *refs, other, mine, arrived = refs
        stores = other, mine
        half = other.shape[0]
        me = lax.axis_index("dim")
        for side, where in enumerate((1 - me, me)):
            place = pl.ds(pl.multiple_of(where * half, half), half)
            loads.append(pltpu.make_async_copy(store.at[place], stores[side], arrived.at[side]))
            loads[side].start()
    else:
        other, mine, *refs = refs
        stores = other, mine
    count_out = len(sides) * count
    outs = refs[-count_out:]
    carried = refs[-count_out - len(sides) * (count - sum(fresh)):-count_out]
    cuts = cuts_of(other.shape[1])
    stacks = []
    for n, targets in pieces:
        values = []
        for _, even_place, odd_place in targets:
            value = refs[even_place][...]
            if odd_place != even_place:
                value = jnp.where(odd, refs[odd_place][...], value)
            values.append(value)
        stacked = values[0] if len(values) == 1 else jnp.concatenate(values, axis=0)
        stacks.append((n, [which for which, _, _ in targets], stacked))
    for at_side, side in enumerate(sides):
        store = stores[side]
        if loading:
            loads[side].wait()
        sums, at = {}, 0
        for i, new in enumerate(fresh):
            sums[i] = None if new else carried[at + at_side][...]
            at += 0 if new else len(sides)
        for n, whiches, stacked in stacks:
            part = product(store[:, cuts[n]], stacked)
            columns = stacked.shape[0] // len(whiches)
            for k, i in enumerate(whiches):
                here = part[:, k * columns:(k + 1) * columns]
                sums[i] = here if sums[i] is None else sums[i] + here
        for i in range(count):
            outs[len(sides) * i + at_side][...] = sums[i]


def more_scores(stores, pieces, carries, valid=None, sides=(0, 1), weight=1):
    operands, placed = [], []

    def place(block):
        known = [i for i, operand in enumerate(operands) if operand is block]
        if not known:
            operands.append(block)
        return known[0] if known else len(operands) - 1

    loading = not isinstance(stores, tuple)
    half, depth = stores.shape[0] // 2 if loading else stores[0].shape[0], 0
    flops = 0
    for n, targets in pieces:
        kept = []
        for which, *blocks in targets:
            places = [place(block) for block in blocks]
            kept.append((which, places[0], places[-1]))
            flops += 4 * half * blocks[0].size
        placed.append((n, tuple(kept)))
    columns = operands[0].shape[0]
    fresh = tuple(carry is None for carry in carries)
    first = [in_hbm(stores)] if loading else list(stores)
    operands += [carry[side] for carry in carries if carry for side in sides]
    specs = [far_spec()] if loading else [whole_spec()] * 2
    total = jax.ShapeDtypeStruct((half, columns), jnp.float32)
    more = []
    if loading:
        held = jax.ShapeDtypeStruct((half, stores.shape[1]), stores.dtype)
        more = [held, held]
    if valid is not None:
        first, more = [valid] + first, more + [jax.ShapeDtypeStruct((8, columns), jnp.int32)]
        specs = [pl.BlockSpec(memory_space=pltpu.SMEM)] + specs
    count = len(sides) * len(carries)
    outs = pl.pallas_call(
        functools.partial(scores_kernel, tuple(placed), fresh, loading, valid is not None, sides),
        out_shape=[total] * count + more,
        in_specs=specs + [whole_spec()] * len(operands),
        out_specs=[whole_spec()] * (count + len(more)),
        scratch_shapes=[pltpu.SemaphoreType.DMA((2,))] if loading else [],
        compiler_params=params(),
        cost_estimate=cost(weight * flops, weight * 4 * half * columns * count),
    )(*first, *operands)
    totals = [tuple(outs[i:i + len(sides)]) for i in range(0, count, len(sides))]
    if valid is not None:
        return totals + [outs[-1]]
    return totals + ([tuple(outs[count:])] if loading else [])


def finish_kernel(places, limit, *refs):
    out, summed, left = refs[-3:]
    half, columns = refs[0].shape
    row_ids = lax.broadcasted_iota(jnp.int32, (half, columns), 0) + lax.axis_index("dim") * half
    inside = row_ids < limit[:1, :]
    stores = []
    for n, place in enumerate(places):
        cut = slice(n * columns, (n + 1) * columns)
        summed[:, cut] = jnp.where(inside, refs[2 * n][...] + refs[2 * n + 1][...], 0.0)
        to = out.at[:, place * columns:(place + 1) * columns]
        stores.append(pltpu.make_async_copy(summed.at[:, cut], to, left.at[n]))
        stores[n].start()
    for store in stores:
        store.wait()


def finish(limit, pairs, places, steps, out=None):
    half, columns = pairs[0][0].shape
    operands = [ref for pair in pairs for ref in pair]
    given = [] if out is None else [in_hbm(out)]
    return pl.pallas_call(
        functools.partial(finish_kernel, places),
        out_shape=pltpu.HBM((half, columns * steps), jnp.float32),
        in_specs=[whole_spec()] * (1 + len(operands))
        + [far_spec()] * len(given),
        out_specs=far_spec(),
        scratch_shapes=[
            pltpu.VMEM((half, columns * len(places)), jnp.float32),
            pltpu.SemaphoreType.DMA((len(places),)),
        ],
        input_output_aliases={1 + len(operands): 0} if given else {},
        compiler_params=params(),
        cost_estimate=cost(half * columns * len(pairs), 12 * half * columns * len(pairs)),
    )(limit, *operands, *given)


def after(x, *earlier):
    return lax.optimization_barrier((x, *earlier))[0]


def shards(store, queries, precond, query_rank, valid_rows):
    size = lax.axis_size("ex")
    odd = lax.rem(lax.axis_index("ex"), 2) == 1
    one_ahead = [(i, (i + 1) % size) for i in range(size)]
    ahead = [(i, (i + 2) % size) for i in range(size)]
    even_ahead = ahead[::2]
    swap = [(i, i ^ 1) for i in range(size)]
    over_dim = [(0, 1), (1, 0)]

    def send(block, route, axis="ex"):
        return lax.ppermute(block, axis, route)

    def exchanged(total):
        theirs, ours = total
        return ours, send(theirs, over_dim, "dim")

    def by_parity(at_even, at_odd):
        return jnp.where(odd, at_odd, at_even)

    own = prepare(queries, precond[None, :], query_rank)
    first, stores = more_scores(store, [(n, [(0, own[n])]) for n in range(CHUNKS)], [None])
    own_pair = exchanged(first)
    moved = {}

    def tied(name, block):
        earlier = [first[1]] if name == EARLY else []
        return after(block, *earlier, *(moved[key] for key in TIES.get(name, "").split()))

    def move(name, block, route):
        moved[name] = send(tied(name, block), route)
        return moved[name]

    one_back, three_back, two_back = {}, {}, {}
    for step in ORDER:
        kind, n = step[0], int(step[1:])
        if kind == "B":
            two_back[n] = move(step, own[n], ahead)
        elif kind == "A":
            move(step, own[n], swap)
        elif kind == "C":
            block = two_back[n] if KINDS[n] != "U" else by_parity(own[n], two_back[n])
            move(step, block, swap)
        elif kind == "Z":
            move(step, moved[f"A{n}"], even_ahead)
        elif kind == "E":
            move(step, moved[f"C{n}"], even_ahead if KINDS[n] == "I" else ahead)
        else:
            block = two_back[n] if KINDS[n] == "V" else by_parity(own[n], two_back[n])
            move(step, block, one_ahead)
    for n, kind in enumerate(KINDS):
        if kind == "V":
            one_back[n], three_back[n] = (moved[f"Z{n}"], moved[f"A{n}"]), (moved[f"R{n}"],)
            continue
        swapped = moved[f"C{n}"]
        if kind == "U":
            one_back[n], three_back[n] = (swapped,), (moved[f"E{n}"],)
        elif kind == "I":
            one_back[n], three_back[n] = (swapped, moved[f"A{n}"]), (moved[f"E{n}"], swapped)
        else:
            direct = moved[f"R{n}"]
            one_back[n], three_back[n] = (swapped, direct), (direct, swapped)

    [two] = more_scores(stores, [(n, [(0, two_back[n])]) for n in range(CHUNKS)], [None])
    two_pair = exchanged(two)
    limited = after(valid_rows, two[1])
    one = three = None
    def pieces_of(group):
        pieces = []
        for item in group.split():
            n, parts = int(item[1:]), {"b": (0, 1), "o": (0,), "t": (1,)}[item[0]]
            blocks = one_back[n], three_back[n]
            pieces.append((n, [(part, *blocks[part]) for part in parts]))
        return pieces

    for group in CHAIN[:-2]:
        if one is None:
            one, three, limit = more_scores(
                stores, pieces_of(group), [one, three], limited, weight=WEIGHT
            )
        else:
            one, three = more_scores(stores, pieces_of(group), [one, three], weight=WEIGHT)
    late, last = pieces_of(CHAIN[-2]), pieces_of(CHAIN[-1])
    [one_theirs], [three_theirs] = more_scores(stores, late, [one, three], sides=(0,))
    one_came = send(one_theirs, over_dim, "dim")
    only = [(n, [(0, *blocks) for _, *blocks in targets]) for n, targets in last]
    [[three_theirs]] = more_scores(stores, only, [(three_theirs, None)], sides=(0,))
    three_came = send(three_theirs, over_dim, "dim")
    [one_ours], [three_ours] = more_scores(stores, late, [one, three], sides=(1,))
    [[three_ours]] = more_scores(stores, only, [(None, three_ours)], sides=(1,))
    pairs = [own_pair, (one_ours, one_came), two_pair, (three_ours, three_came)]
    return finish(limit, pairs, (0, 1, 2, 3), STEPS)


def solution(mesh):
    return jax.shard_map(
        shards,
        mesh=mesh,
        in_specs=(
            P(("groups", "ex"), "dim"),
            P(("groups", "ex"), "dim"),
            P("dim"),
            P(("groups", "ex"), None),
            P(("groups", "ex")),
        ),
        out_specs=P(("groups", "ex", "dim"), None),
        check_vma=False,
    )
```

```python
import functools

import jax
import jax.numpy as jnp
from jax import lax
from jax.experimental import pallas as pl
from jax.experimental.pallas import tpu as pltpu
from jax.sharding import PartitionSpec as P

STEPS = 4
KINDS = "UUT"
PARTS = (4, 6, 6)
CHAIN = ("b0", "o1", "b2", "t1")
ORDER = ("B0", "B1", "B2", "C0", "C1", "E0", "E1", "R2", "C2")
TIES = {"C2": "C0"}
EARLY = "C0"
OUT = "none"
WEIGHT = 2
CHUNKS = len(PARTS)
VMEM_BYTES = 16 * 1024 * 1024


def params():
    return pltpu.CompilerParams(vmem_limit_bytes=VMEM_BYTES)


def whole_spec():
    return pl.BlockSpec(memory_space=pltpu.VMEM)


def far_spec():
    return pl.BlockSpec(memory_space=pltpu.HBM)


def in_hbm(x):
    return pltpu.with_memory_space_constraint(x, pltpu.HBM)


def cost(flops, traffic):
    return pl.CostEstimate(flops=flops, bytes_accessed=traffic, transcendentals=0)


def cuts_of(depth):
    ends = [depth * sum(PARTS[:n + 1]) // sum(PARTS) for n in range(CHUNKS)]
    return [slice(start, end) for start, end in zip([0] + ends, ends)]


def product(rows, block):
    return lax.dot_general(
        rows, block, (((1,), (1,)), ((), ())), preferred_element_type=jnp.float32
    )


def ordered_chunk(raw, scale, rank, cut):
    rows = raw.shape[0]
    positions = lax.broadcasted_iota(jnp.int32, (rows, rows), 0)
    placing = (positions == rank[...]).astype(jnp.bfloat16)
    pre = (raw[:, cut].astype(jnp.float32) * scale[:, cut]).astype(jnp.bfloat16)
    return jnp.dot(placing, pre, preferred_element_type=jnp.float32).astype(jnp.bfloat16)


def prepare_first_kernel(queries, precond, rank, chunk, raw, scale, places, arrived):
    depth = queries.shape[1]
    cut, rest = slice(0, chunk.shape[1]), slice(chunk.shape[1], depth)
    loads = [
        pltpu.make_async_copy(rank, places, arrived.at[0]),
        pltpu.make_async_copy(precond, scale, arrived.at[1]),
        pltpu.make_async_copy(queries.at[:, cut], raw.at[:, cut], arrived.at[2]),
        pltpu.make_async_copy(queries.at[:, rest], raw.at[:, rest], arrived.at[3]),
    ]
    for load in loads:
        load.start()
    for load in loads[:3]:
        load.wait()
    chunk[...] = ordered_chunk(raw, scale, places, cut)
    loads[3].wait()


def prepare_rest_kernel(cuts, raw, scale, places, *chunks):
    for cut, chunk in zip(cuts, chunks):
        chunk[...] = ordered_chunk(raw, scale, places, cut)


def prepare(queries, precond, rank):
    rows, depth = queries.shape
    cuts = cuts_of(depth)
    shapes = [
        jax.ShapeDtypeStruct((rows, cut.stop - cut.start), jnp.bfloat16) for cut in cuts
    ]
    held = [jax.ShapeDtypeStruct(x.shape, x.dtype) for x in (queries, precond, rank)]
    chunk, *held = pl.pallas_call(
        prepare_first_kernel,
        out_shape=[shapes[0], *held],
        in_specs=[far_spec()] * 3,
        out_specs=[whole_spec()] * 4,
        scratch_shapes=[pltpu.SemaphoreType.DMA((4,))],
        compiler_params=params(),
        cost_estimate=cost(2 * rows * rows * cuts[0].stop, 2 * rows * depth),
    )(in_hbm(queries), in_hbm(precond), in_hbm(rank))
    rest = pl.pallas_call(
        functools.partial(prepare_rest_kernel, cuts[1:]),
        out_shape=shapes[1:],
        in_specs=[whole_spec()] * 3,
        out_specs=[whole_spec()] * (CHUNKS - 1),
        compiler_params=params(),
        cost_estimate=cost(2 * rows * rows * depth, 2 * rows * depth),
    )(*held)
    return [chunk, *rest]


def load_kernel(store, other, mine, arrived):
    half = other.shape[0]
    me = lax.axis_index("dim")
    loads = []
    for n, (where, to) in enumerate(((1 - me, other), (me, mine))):
        place = pl.ds(pl.multiple_of(where * half, half), half)
        loads.append(pltpu.make_async_copy(store.at[place], to, arrived.at[n]))
        loads[n].start()
    for load in loads:
        load.wait()


def loaded(store):
    half = jax.ShapeDtypeStruct((store.shape[0] // 2, store.shape[1]), store.dtype)
    return pl.pallas_call(
        load_kernel,
        out_shape=[half] * 2,
        in_specs=[far_spec()],
        out_specs=[whole_spec()] * 2,
        scratch_shapes=[pltpu.SemaphoreType.DMA((2,))],
        compiler_params=params(),
        cost_estimate=cost(0, 2 * store.size),
    )(in_hbm(store))


def scores_kernel(pieces, fresh, loading, counted, sides, *refs):
    count = len(fresh)
    if counted:
        valid, *refs, limit = refs
        limit[...] = jnp.full(limit.shape, valid[0], jnp.int32)
    odd = lax.rem(lax.axis_index("ex"), 2) == 1
    loads = []
    if loading:
        store, *refs = refs
        *refs, other, mine, arrived = refs
        stores = other, mine
        half = other.shape[0]
        me = lax.axis_index("dim")
        for side, where in enumerate((1 - me, me)):
            place = pl.ds(pl.multiple_of(where * half, half), half)
            loads.append(pltpu.make_async_copy(store.at[place], stores[side], arrived.at[side]))
            loads[side].start()
    else:
        other, mine, *refs = refs
        stores = other, mine
    count_out = len(sides) * count
    outs = refs[-count_out:]
    carried = refs[-count_out - len(sides) * (count - sum(fresh)):-count_out]
    cuts = cuts_of(other.shape[1])
    stacks = []
    for n, targets in pieces:
        values = []
        for _, even_place, odd_place in targets:
            value = refs[even_place][...]
            if odd_place != even_place:
                value = jnp.where(odd, refs[odd_place][...], value)
            values.append(value)
        stacked = values[0] if len(values) == 1 else jnp.concatenate(values, axis=0)
        stacks.append((n, [which for which, _, _ in targets], stacked))
    for at_side, side in enumerate(sides):
        store = stores[side]
        if loading:
            loads[side].wait()
        sums, at = {}, 0
        for i, new in enumerate(fresh):
            sums[i] = None if new else carried[at + at_side][...]
            at += 0 if new else len(sides)
        for n, whiches, stacked in stacks:
            part = product(store[:, cuts[n]], stacked)
            columns = stacked.shape[0] // len(whiches)
            for k, i in enumerate(whiches):
                here = part[:, k * columns:(k + 1) * columns]
                sums[i] = here if sums[i] is None else sums[i] + here
        for i in range(count):
            outs[len(sides) * i + at_side][...] = sums[i]


def more_scores(stores, pieces, carries, valid=None, sides=(0, 1), weight=1):
    operands, placed = [], []

    def place(block):
        known = [i for i, operand in enumerate(operands) if operand is block]
        if not known:
            operands.append(block)
        return known[0] if known else len(operands) - 1

    loading = not isinstance(stores, tuple)
    half, depth = stores.shape[0] // 2 if loading else stores[0].shape[0], 0
    flops = 0
    for n, targets in pieces:
        kept = []
        for which, *blocks in targets:
            places = [place(block) for block in blocks]
            kept.append((which, places[0], places[-1]))
            flops += 4 * half * blocks[0].size
        placed.append((n, tuple(kept)))
    columns = operands[0].shape[0]
    fresh = tuple(carry is None for carry in carries)
    first = [in_hbm(stores)] if loading else list(stores)
    operands += [carry[side] for carry in carries if carry for side in sides]
    specs = [far_spec()] if loading else [whole_spec()] * 2
    total = jax.ShapeDtypeStruct((half, columns), jnp.float32)
    more = []
    if loading:
        held = jax.ShapeDtypeStruct((half, stores.shape[1]), stores.dtype)
        more = [held, held]
    if valid is not None:
        first, more = [valid] + first, more + [jax.ShapeDtypeStruct((8, columns), jnp.int32)]
        specs = [pl.BlockSpec(memory_space=pltpu.SMEM)] + specs
    count = len(sides) * len(carries)
    outs = pl.pallas_call(
        functools.partial(scores_kernel, tuple(placed), fresh, loading, valid is not None, sides),
        out_shape=[total] * count + more,
        in_specs=specs + [whole_spec()] * len(operands),
        out_specs=[whole_spec()] * (count + len(more)),
        scratch_shapes=[pltpu.SemaphoreType.DMA((2,))] if loading else [],
        compiler_params=params(),
        cost_estimate=cost(weight * flops, weight * 4 * half * columns * count),
    )(*first, *operands)
    totals = [tuple(outs[i:i + len(sides)]) for i in range(0, count, len(sides))]
    if valid is not None:
        return totals + [outs[-1]]
    return totals + ([tuple(outs[count:])] if loading else [])


def finish_kernel(places, limit, *refs):
    out, summed, left = refs[-3:]
    half, columns = refs[0].shape
    row_ids = lax.broadcasted_iota(jnp.int32, (half, columns), 0) + lax.axis_index("dim") * half
    inside = row_ids < limit[:1, :]
    stores = []
    for n, place in enumerate(places):
        cut = slice(n * columns, (n + 1) * columns)
        summed[:, cut] = jnp.where(inside, refs[2 * n][...] + refs[2 * n + 1][...], 0.0)
        to = out.at[:, place * columns:(place + 1) * columns]
        stores.append(pltpu.make_async_copy(summed.at[:, cut], to, left.at[n]))
        stores[n].start()
    for store in stores:
        store.wait()


def finish(limit, pairs, places, steps, out=None):
    half, columns = pairs[0][0].shape
    operands = [ref for pair in pairs for ref in pair]
    given = [] if out is None else [in_hbm(out)]
    return pl.pallas_call(
        functools.partial(finish_kernel, places),
        out_shape=pltpu.HBM((half, columns * steps), jnp.float32),
        in_specs=[whole_spec()] * (1 + len(operands))
        + [far_spec()] * len(given),
        out_specs=far_spec(),
        scratch_shapes=[
            pltpu.VMEM((half, columns * len(places)), jnp.float32),
            pltpu.SemaphoreType.DMA((len(places),)),
        ],
        input_output_aliases={1 + len(operands): 0} if given else {},
        compiler_params=params(),
        cost_estimate=cost(half * columns * len(pairs), 12 * half * columns * len(pairs)),
    )(limit, *operands, *given)


def after(x, *earlier):
    return lax.optimization_barrier((x, *earlier))[0]


def shards(store, queries, precond, query_rank, valid_rows):
    size = lax.axis_size("ex")
    odd = lax.rem(lax.axis_index("ex"), 2) == 1
    one_ahead = [(i, (i + 1) % size) for i in range(size)]
    ahead = [(i, (i + 2) % size) for i in range(size)]
    even_ahead = ahead[::2]
    swap = [(i, i ^ 1) for i in range(size)]
    over_dim = [(0, 1), (1, 0)]

    def send(block, route, axis="ex"):
        return lax.ppermute(block, axis, route)

    def exchanged(total):
        theirs, ours = total
        return ours, send(theirs, over_dim, "dim")

    def by_parity(at_even, at_odd):
        return jnp.where(odd, at_odd, at_even)

    own = prepare(queries, precond[None, :], query_rank)
    stores = tuple(loaded(store))
    moved = {}

    def tied(name, block):
        earlier = [stores[1]] if name == EARLY else []
        return after(block, *earlier, *(moved[key] for key in TIES.get(name, "").split()))

    def move(name, block, route):
        moved[name] = send(tied(name, block), route)
        return moved[name]

    one_back, three_back, two_back = {}, {}, {}
    for step in ORDER:
        kind, n = step[0], int(step[1:])
        if kind == "B":
            two_back[n] = move(step, own[n], ahead)
        elif kind == "A":
            move(step, own[n], swap)
        elif kind == "C":
            block = two_back[n] if KINDS[n] != "U" else by_parity(own[n], two_back[n])
            move(step, block, swap)
        elif kind == "Z":
            move(step, moved[f"A{n}"], even_ahead)
        elif kind == "E":
            move(step, moved[f"C{n}"], even_ahead if KINDS[n] == "I" else ahead)
        else:
            block = two_back[n] if KINDS[n] == "V" else by_parity(own[n], two_back[n])
            move(step, block, one_ahead)
    for n, kind in enumerate(KINDS):
        if kind == "V":
            one_back[n], three_back[n] = (moved[f"Z{n}"], moved[f"A{n}"]), (moved[f"R{n}"],)
            continue
        swapped = moved[f"C{n}"]
        if kind == "U":
            one_back[n], three_back[n] = (swapped,), (moved[f"E{n}"],)
        elif kind == "I":
            one_back[n], three_back[n] = (swapped, moved[f"A{n}"]), (moved[f"E{n}"], swapped)
        else:
            direct = moved[f"R{n}"]
            one_back[n], three_back[n] = (swapped, direct), (direct, swapped)

    first, two = more_scores(
        stores, [(n, [(0, own[n]), (1, two_back[n])]) for n in range(CHUNKS)], [None, None]
    )
    own_pair, two_pair = exchanged(first), exchanged(two)
    limited = after(valid_rows, two[1])
    one = three = one_pair = None
    todo, out = set(range(CHUNKS)), None
    for group in CHAIN:
        pieces = []
        if group == OUT:
            out = finish(limit, [own_pair, two_pair], (0, 2), STEPS)
            one = after(one[0], out), one[1]
        for item in group.split():
            n, parts = int(item[1:]), {"b": (0, 1), "o": (0,), "t": (1,)}[item[0]]
            blocks = one_back[n], three_back[n]
            pieces.append((n, [(part, *blocks[part]) for part in parts]))
            todo -= {n} if 0 in parts else set()
        if one is None:
            one, three, limit = more_scores(
                stores, pieces, [one, three], limited, weight=WEIGHT
            )
        elif one_pair is None:
            one, three = more_scores(stores, pieces, [one, three], weight=WEIGHT)
        else:
            pieces = [(n, [(0, *blocks) for _, *blocks in targets]) for n, targets in pieces]
            [[theirs]] = more_scores(stores, pieces, [three], sides=(0,))
            [[ours]] = more_scores(stores, pieces, [three], sides=(1,))
            three = theirs, ours
        if one_pair is None and not todo:
            one_pair = exchanged(one)
    if out is None:
        out = finish(limit, [own_pair, two_pair], (0, 2), STEPS)
    return finish(limit, [one_pair, exchanged(three)], (1, 3), STEPS, out)


def solution(mesh):
    return jax.shard_map(
        shards,
        mesh=mesh,
        in_specs=(
            P(("groups", "ex"), "dim"),
            P(("groups", "ex"), "dim"),
            P("dim"),
            P(("groups", "ex"), None),
            P(("groups", "ex")),
        ),
        out_specs=P(("groups", "ex", "dim"), None),
        check_vma=False,
    )
```

```python
import functools

import jax
import jax.numpy as jnp
from jax import lax
from jax.experimental import pallas as pl
from jax.experimental.pallas import tpu as pltpu
from jax.sharding import PartitionSpec as P

STEPS = 4
KINDS = "UUT"
PARTS = (4, 6, 6)
CHAIN = ("b0", "o1", "b2", "t1")
ORDER = ("B0", "B1", "B2", "C0", "C1", "E0", "E1", "R2", "C2")
TIES = {"C2": "C0"}
EARLY = "C0"
WEIGHT = 2
CHUNKS = len(PARTS)
VMEM_BYTES = 16 * 1024 * 1024


def params():
    return pltpu.CompilerParams(vmem_limit_bytes=VMEM_BYTES)


def whole_spec():
    return pl.BlockSpec(memory_space=pltpu.VMEM)


def far_spec():
    return pl.BlockSpec(memory_space=pltpu.HBM)


def in_hbm(x):
    return pltpu.with_memory_space_constraint(x, pltpu.HBM)


def cost(flops, traffic):
    return pl.CostEstimate(flops=flops, bytes_accessed=traffic, transcendentals=0)


def cuts_of(depth):
    ends = [depth * sum(PARTS[:n + 1]) // sum(PARTS) for n in range(CHUNKS)]
    return [slice(start, end) for start, end in zip([0] + ends, ends)]


def product(rows, block):
    return lax.dot_general(
        rows, block, (((1,), (1,)), ((), ())), preferred_element_type=jnp.float32
    )


def prepare_kernel(queries, precond, rank, *refs):
    chunks, (own, held, scale, places, arrived) = refs[:CHUNKS], refs[CHUNKS:]
    rows, depth = queries.shape
    cuts = cuts_of(depth)
    loads = [pltpu.make_async_copy(rank, places, arrived.at[CHUNKS])]
    loads.append(pltpu.make_async_copy(precond, scale, arrived.at[CHUNKS + 1]))
    for n, cut in enumerate(cuts):
        loads.append(pltpu.make_async_copy(queries.at[:, cut], held.at[:, cut], arrived.at[n]))
    for load in loads:
        load.start()
    loads[0].wait()
    loads[1].wait()
    positions = lax.broadcasted_iota(jnp.int32, (rows, rows), 0)
    placing = (positions == places[...]).astype(jnp.bfloat16)
    for n, cut in enumerate(cuts):
        loads[2 + n].wait()
        pre = (held[:, cut].astype(jnp.float32) * scale[:, cut]).astype(jnp.bfloat16)
        ordered = jnp.dot(placing, pre, preferred_element_type=jnp.float32).astype(jnp.bfloat16)
        chunks[n][...] = ordered
        own[:, cut] = ordered


def prepare(queries, precond, rank):
    rows, depth = queries.shape
    shapes = [
        jax.ShapeDtypeStruct((rows, cut.stop - cut.start), jnp.bfloat16) for cut in cuts_of(depth)
    ]
    return pl.pallas_call(
        prepare_kernel,
        out_shape=shapes + [jax.ShapeDtypeStruct((rows, depth), jnp.bfloat16)],
        in_specs=[far_spec()] * 3,
        out_specs=[whole_spec()] * (CHUNKS + 1),
        scratch_shapes=[
            pltpu.VMEM((rows, depth), jnp.bfloat16),
            pltpu.VMEM((1, depth), jnp.float32),
            pltpu.VMEM((1, rows), jnp.int32),
            pltpu.SemaphoreType.DMA((CHUNKS + 2,)),
        ],
        compiler_params=params(),
        cost_estimate=cost(2 * rows * rows * depth, 4 * rows * depth),
    )(in_hbm(queries), in_hbm(precond), in_hbm(rank))


def scores_kernel(pieces, fresh, loading, counted, sides, *refs):
    count = len(fresh)
    if counted:
        valid, *refs, limit = refs
        limit[...] = jnp.full(limit.shape, valid[0], jnp.int32)
    odd = lax.rem(lax.axis_index("ex"), 2) == 1
    loads = []
    if loading:
        store, *refs = refs
        *refs, other, mine, arrived = refs
        stores = other, mine
        half = other.shape[0]
        me = lax.axis_index("dim")
        for side, where in enumerate((1 - me, me)):
            place = pl.ds(pl.multiple_of(where * half, half), half)
            loads.append(pltpu.make_async_copy(store.at[place], stores[side], arrived.at[side]))
            loads[side].start()
    else:
        other, mine, *refs = refs
        stores = other, mine
    count_out = len(sides) * count
    outs = refs[-count_out:]
    carried = refs[-count_out - len(sides) * (count - sum(fresh)):-count_out]
    cuts = cuts_of(other.shape[1]) + [slice(0, other.shape[1])]
    stacks = []
    for n, targets in pieces:
        values = []
        for _, even_place, odd_place in targets:
            value = refs[even_place][...]
            if odd_place != even_place:
                value = jnp.where(odd, refs[odd_place][...], value)
            values.append(value)
        stacked = values[0] if len(values) == 1 else jnp.concatenate(values, axis=0)
        stacks.append((n, [which for which, _, _ in targets], stacked))
    for at_side, side in enumerate(sides):
        store = stores[side]
        if loading:
            loads[side].wait()
        sums, at = {}, 0
        for i, new in enumerate(fresh):
            sums[i] = None if new else carried[at + at_side][...]
            at += 0 if new else len(sides)
        for n, whiches, stacked in stacks:
            part = product(store[:, cuts[n]], stacked)
            columns = stacked.shape[0] // len(whiches)
            for k, i in enumerate(whiches):
                here = part[:, k * columns:(k + 1) * columns]
                sums[i] = here if sums[i] is None else sums[i] + here
        for i in range(count):
            outs[len(sides) * i + at_side][...] = sums[i]


def more_scores(stores, pieces, carries, valid=None, sides=(0, 1), weight=1):
    operands, placed = [], []

    def place(block):
        known = [i for i, operand in enumerate(operands) if operand is block]
        if not known:
            operands.append(block)
        return known[0] if known else len(operands) - 1

    loading = not isinstance(stores, tuple)
    half, depth = stores.shape[0] // 2 if loading else stores[0].shape[0], 0
    flops = 0
    for n, targets in pieces:
        kept = []
        for which, *blocks in targets:
            places = [place(block) for block in blocks]
            kept.append((which, places[0], places[-1]))
            flops += 4 * half * blocks[0].size
        placed.append((n, tuple(kept)))
    columns = operands[0].shape[0]
    fresh = tuple(carry is None for carry in carries)
    first = [in_hbm(stores)] if loading else list(stores)
    operands += [carry[side] for carry in carries if carry for side in sides]
    specs = [far_spec()] if loading else [whole_spec()] * 2
    total = jax.ShapeDtypeStruct((half, columns), jnp.float32)
    more = []
    if loading:
        held = jax.ShapeDtypeStruct((half, stores.shape[1]), stores.dtype)
        more = [held, held]
    if valid is not None:
        first, more = [valid] + first, more + [jax.ShapeDtypeStruct((8, columns), jnp.int32)]
        specs = [pl.BlockSpec(memory_space=pltpu.SMEM)] + specs
    count = len(sides) * len(carries)
    outs = pl.pallas_call(
        functools.partial(scores_kernel, tuple(placed), fresh, loading, valid is not None, sides),
        out_shape=[total] * count + more,
        in_specs=specs + [whole_spec()] * len(operands),
        out_specs=[whole_spec()] * (count + len(more)),
        scratch_shapes=[pltpu.SemaphoreType.DMA((2,))] if loading else [],
        compiler_params=params(),
        cost_estimate=cost(weight * flops, weight * 4 * half * columns * count),
    )(*first, *operands)
    totals = [tuple(outs[i:i + len(sides)]) for i in range(0, count, len(sides))]
    if valid is not None:
        return totals + [outs[-1]]
    return totals + ([tuple(outs[count:])] if loading else [])


def finish_kernel(places, limit, *refs):
    out, summed, left = refs[-3:]
    half, columns = refs[0].shape
    row_ids = lax.broadcasted_iota(jnp.int32, (half, columns), 0) + lax.axis_index("dim") * half
    inside = row_ids < limit[:1, :]
    stores = []
    for n, place in enumerate(places):
        cut = slice(n * columns, (n + 1) * columns)
        summed[:, cut] = jnp.where(inside, refs[2 * n][...] + refs[2 * n + 1][...], 0.0)
        to = out.at[:, place * columns:(place + 1) * columns]
        stores.append(pltpu.make_async_copy(summed.at[:, cut], to, left.at[n]))
        stores[n].start()
    for store in stores:
        store.wait()


def finish(limit, pairs, places, steps, out=None):
    half, columns = pairs[0][0].shape
    operands = [ref for pair in pairs for ref in pair]
    given = [] if out is None else [in_hbm(out)]
    return pl.pallas_call(
        functools.partial(finish_kernel, places),
        out_shape=pltpu.HBM((half, columns * steps), jnp.float32),
        in_specs=[whole_spec()] * (1 + len(operands))
        + [far_spec()] * len(given),
        out_specs=far_spec(),
        scratch_shapes=[
            pltpu.VMEM((half, columns * len(places)), jnp.float32),
            pltpu.SemaphoreType.DMA((len(places),)),
        ],
        input_output_aliases={1 + len(operands): 0} if given else {},
        compiler_params=params(),
        cost_estimate=cost(half * columns * len(pairs), 12 * half * columns * len(pairs)),
    )(limit, *operands, *given)


def after(x, *earlier):
    return lax.optimization_barrier((x, *earlier))[0]


def shards(store, queries, precond, query_rank, valid_rows):
    size = lax.axis_size("ex")
    odd = lax.rem(lax.axis_index("ex"), 2) == 1
    one_ahead = [(i, (i + 1) % size) for i in range(size)]
    ahead = [(i, (i + 2) % size) for i in range(size)]
    even_ahead = ahead[::2]
    swap = [(i, i ^ 1) for i in range(size)]
    over_dim = [(0, 1), (1, 0)]

    def send(block, route, axis="ex"):
        return lax.ppermute(block, axis, route)

    def exchanged(total):
        theirs, ours = total
        return ours, send(theirs, over_dim, "dim")

    def by_parity(at_even, at_odd):
        return jnp.where(odd, at_odd, at_even)

    *own, undivided = prepare(queries, precond[None, :], query_rank)
    first, stores = more_scores(store, [(CHUNKS, [(0, undivided)])], [None])
    own_pair = exchanged(first)
    moved = {}

    def tied(name, block):
        earlier = [first[1]] if name == EARLY else []
        return after(block, *earlier, *(moved[key] for key in TIES.get(name, "").split()))

    def move(name, block, route):
        moved[name] = send(tied(name, block), route)
        return moved[name]

    one_back, three_back, two_back = {}, {}, {}
    for step in ORDER:
        kind, n = step[0], int(step[1:])
        if kind == "B":
            two_back[n] = move(step, own[n], ahead)
        elif kind == "A":
            move(step, own[n], swap)
        elif kind == "C":
            block = two_back[n] if KINDS[n] != "U" else by_parity(own[n], two_back[n])
            move(step, block, swap)
        elif kind == "Z":
            move(step, moved[f"A{n}"], even_ahead)
        elif kind == "E":
            move(step, moved[f"C{n}"], even_ahead if KINDS[n] == "I" else ahead)
        else:
            block = two_back[n] if KINDS[n] == "V" else by_parity(own[n], two_back[n])
            move(step, block, one_ahead)
    for n, kind in enumerate(KINDS):
        if kind == "V":
            one_back[n], three_back[n] = (moved[f"Z{n}"], moved[f"A{n}"]), (moved[f"R{n}"],)
            continue
        swapped = moved[f"C{n}"]
        if kind == "U":
            one_back[n], three_back[n] = (swapped,), (moved[f"E{n}"],)
        elif kind == "I":
            one_back[n], three_back[n] = (swapped, moved[f"A{n}"]), (moved[f"E{n}"], swapped)
        else:
            direct = moved[f"R{n}"]
            one_back[n], three_back[n] = (swapped, direct), (direct, swapped)

    [two] = more_scores(stores, [(n, [(0, two_back[n])]) for n in range(CHUNKS)], [None])
    two_pair = exchanged(two)
    limited = after(valid_rows, two[1])
    one = three = one_pair = None
    todo = set(range(CHUNKS))
    for group in CHAIN:
        pieces = []
        for item in group.split():
            n, parts = int(item[1:]), {"b": (0, 1), "o": (0,), "t": (1,)}[item[0]]
            blocks = one_back[n], three_back[n]
            pieces.append((n, [(part, *blocks[part]) for part in parts]))
            todo -= {n} if 0 in parts else set()
        if one is None:
            one, three, limit = more_scores(
                stores, pieces, [one, three], limited, weight=WEIGHT
            )
        elif one_pair is None:
            one, three = more_scores(stores, pieces, [one, three], weight=WEIGHT)
        else:
            pieces = [(n, [(0, *blocks) for _, *blocks in targets]) for n, targets in pieces]
            [[theirs]] = more_scores(stores, pieces, [three], sides=(0,))
            [[ours]] = more_scores(stores, pieces, [three], sides=(1,))
            three = theirs, ours
        if one_pair is None and not todo:
            one_pair = exchanged(one)
    out = finish(limit, [own_pair, two_pair], (0, 2), STEPS)
    return finish(limit, [one_pair, exchanged(three)], (1, 3), STEPS, out)


def solution(mesh):
    return jax.shard_map(
        shards,
        mesh=mesh,
        in_specs=(
            P(("groups", "ex"), "dim"),
            P(("groups", "ex"), "dim"),
            P("dim"),
            P(("groups", "ex"), None),
            P(("groups", "ex")),
        ),
        out_specs=P(("groups", "ex", "dim"), None),
        check_vma=False,
    )
```

```python
import functools

import jax
import jax.numpy as jnp
from jax import lax
from jax.experimental import pallas as pl
from jax.experimental.pallas import tpu as pltpu
from jax.sharding import PartitionSpec as P

STEPS = 4
KINDS = "UUT"
PARTS = (4, 7, 5)
CHAIN = ("b0", "o1", "b2", "t1")
ORDER = ("B0", "B1", "B2", "C0", "C1", "E0", "E1", "R2", "C2")
TIES = {"C2": "C0"}
EARLY = "C0"
WEIGHT = 3
CHUNKS = len(PARTS)
VMEM_BYTES = 16 * 1024 * 1024


def params():
    return pltpu.CompilerParams(vmem_limit_bytes=VMEM_BYTES)


def whole_spec():
    return pl.BlockSpec(memory_space=pltpu.VMEM)


def far_spec():
    return pl.BlockSpec(memory_space=pltpu.HBM)


def in_hbm(x):
    return pltpu.with_memory_space_constraint(x, pltpu.HBM)


def cost(flops, traffic):
    return pl.CostEstimate(flops=flops, bytes_accessed=traffic, transcendentals=0)


def cuts_of(depth):
    ends = [depth * sum(PARTS[:n + 1]) // sum(PARTS) for n in range(CHUNKS)]
    return [slice(start, end) for start, end in zip([0] + ends, ends)]


def product(rows, block):
    return lax.dot_general(
        rows, block, (((1,), (1,)), ((), ())), preferred_element_type=jnp.float32
    )


def prepare_kernel(queries, precond, rank, *refs):
    chunks, (own, held, scale, places, arrived) = refs[:CHUNKS], refs[CHUNKS:]
    rows, depth = queries.shape
    cuts = cuts_of(depth)
    loads = [pltpu.make_async_copy(rank, places, arrived.at[CHUNKS])]
    loads.append(pltpu.make_async_copy(precond, scale, arrived.at[CHUNKS + 1]))
    for n, cut in enumerate(cuts):
        loads.append(pltpu.make_async_copy(queries.at[:, cut], held.at[:, cut], arrived.at[n]))
    for load in loads:
        load.start()
    loads[0].wait()
    loads[1].wait()
    positions = lax.broadcasted_iota(jnp.int32, (rows, rows), 0)
    placing = (positions == places[...]).astype(jnp.bfloat16)
    for n, cut in enumerate(cuts):
        loads[2 + n].wait()
        pre = (held[:, cut].astype(jnp.float32) * scale[:, cut]).astype(jnp.bfloat16)
        ordered = jnp.dot(placing, pre, preferred_element_type=jnp.float32).astype(jnp.bfloat16)
        chunks[n][...] = ordered
        own[:, cut] = ordered


def prepare(queries, precond, rank):
    rows, depth = queries.shape
    shapes = [
        jax.ShapeDtypeStruct((rows, cut.stop - cut.start), jnp.bfloat16) for cut in cuts_of(depth)
    ]
    return pl.pallas_call(
        prepare_kernel,
        out_shape=shapes + [jax.ShapeDtypeStruct((rows, depth), jnp.bfloat16)],
        in_specs=[far_spec()] * 3,
        out_specs=[whole_spec()] * (CHUNKS + 1),
        scratch_shapes=[
            pltpu.VMEM((rows, depth), jnp.bfloat16),
            pltpu.VMEM((1, depth), jnp.float32),
            pltpu.VMEM((1, rows), jnp.int32),
            pltpu.SemaphoreType.DMA((CHUNKS + 2,)),
        ],
        compiler_params=params(),
        cost_estimate=cost(2 * rows * rows * depth, 4 * rows * depth),
    )(in_hbm(queries), in_hbm(precond), in_hbm(rank))


def scores_kernel(pieces, fresh, loading, counted, sides, *refs):
    count = len(fresh)
    if counted:
        valid, *refs, limit = refs
        limit[...] = jnp.full(limit.shape, valid[0], jnp.int32)
    odd = lax.rem(lax.axis_index("ex"), 2) == 1
    loads = []
    if loading:
        store, *refs = refs
        *refs, other, mine, arrived = refs
        stores = other, mine
        half = other.shape[0]
        me = lax.axis_index("dim")
        for side, where in enumerate((1 - me, me)):
            place = pl.ds(pl.multiple_of(where * half, half), half)
            loads.append(pltpu.make_async_copy(store.at[place], stores[side], arrived.at[side]))
            loads[side].start()
    else:
        other, mine, *refs = refs
        stores = other, mine
    count_out = len(sides) * count
    outs = refs[-count_out:]
    carried = refs[-count_out - len(sides) * (count - sum(fresh)):-count_out]
    cuts = cuts_of(other.shape[1]) + [slice(0, other.shape[1])]
    stacks = []
    for n, targets in pieces:
        values = []
        for _, even_place, odd_place in targets:
            value = refs[even_place][...]
            if odd_place != even_place:
                value = jnp.where(odd, refs[odd_place][...], value)
            values.append(value)
        stacked = values[0] if len(values) == 1 else jnp.concatenate(values, axis=0)
        stacks.append((n, [which for which, _, _ in targets], stacked))
    for at_side, side in enumerate(sides):
        store = stores[side]
        if loading:
            loads[side].wait()
        sums, at = {}, 0
        for i, new in enumerate(fresh):
            sums[i] = None if new else carried[at + at_side][...]
            at += 0 if new else len(sides)
        for n, whiches, stacked in stacks:
            part = product(store[:, cuts[n]], stacked)
            columns = stacked.shape[0] // len(whiches)
            for k, i in enumerate(whiches):
                here = part[:, k * columns:(k + 1) * columns]
                sums[i] = here if sums[i] is None else sums[i] + here
        for i in range(count):
            outs[len(sides) * i + at_side][...] = sums[i]


def more_scores(stores, pieces, carries, valid=None, sides=(0, 1), weight=1):
    operands, placed = [], []

    def place(block):
        known = [i for i, operand in enumerate(operands) if operand is block]
        if not known:
            operands.append(block)
        return known[0] if known else len(operands) - 1

    loading = not isinstance(stores, tuple)
    half, depth = stores.shape[0] // 2 if loading else stores[0].shape[0], 0
    flops = 0
    for n, targets in pieces:
        kept = []
        for which, *blocks in targets:
            places = [place(block) for block in blocks]
            kept.append((which, places[0], places[-1]))
            flops += 4 * half * blocks[0].size
        placed.append((n, tuple(kept)))
    columns = operands[0].shape[0]
    fresh = tuple(carry is None for carry in carries)
    first = [in_hbm(stores)] if loading else list(stores)
    operands += [carry[side] for carry in carries if carry for side in sides]
    specs = [far_spec()] if loading else [whole_spec()] * 2
    total = jax.ShapeDtypeStruct((half, columns), jnp.float32)
    more = []
    if loading:
        held = jax.ShapeDtypeStruct((half, stores.shape[1]), stores.dtype)
        more = [held, held]
    if valid is not None:
        first, more = [valid] + first, more + [jax.ShapeDtypeStruct((8, columns), jnp.int32)]
        specs = [pl.BlockSpec(memory_space=pltpu.SMEM)] + specs
    count = len(sides) * len(carries)
    outs = pl.pallas_call(
        functools.partial(scores_kernel, tuple(placed), fresh, loading, valid is not None, sides),
        out_shape=[total] * count + more,
        in_specs=specs + [whole_spec()] * len(operands),
        out_specs=[whole_spec()] * (count + len(more)),
        scratch_shapes=[pltpu.SemaphoreType.DMA((2,))] if loading else [],
        compiler_params=params(),
        cost_estimate=cost(weight * flops, weight * 4 * half * columns * count),
    )(*first, *operands)
    totals = [tuple(outs[i:i + len(sides)]) for i in range(0, count, len(sides))]
    if valid is not None:
        return totals + [outs[-1]]
    return totals + ([tuple(outs[count:])] if loading else [])


def finish_kernel(places, limit, *refs):
    out, summed, left = refs[-3:]
    half, columns = refs[0].shape
    row_ids = lax.broadcasted_iota(jnp.int32, (half, columns), 0) + lax.axis_index("dim") * half
    inside = row_ids < limit[:1, :]
    stores = []
    for n, place in enumerate(places):
        cut = slice(n * columns, (n + 1) * columns)
        summed[:, cut] = jnp.where(inside, refs[2 * n][...] + refs[2 * n + 1][...], 0.0)
        to = out.at[:, place * columns:(place + 1) * columns]
        stores.append(pltpu.make_async_copy(summed.at[:, cut], to, left.at[n]))
        stores[n].start()
    for store in stores:
        store.wait()


def finish(limit, pairs, places, steps, out=None):
    half, columns = pairs[0][0].shape
    operands = [ref for pair in pairs for ref in pair]
    given = [] if out is None else [in_hbm(out)]
    return pl.pallas_call(
        functools.partial(finish_kernel, places),
        out_shape=pltpu.HBM((half, columns * steps), jnp.float32),
        in_specs=[whole_spec()] * (1 + len(operands))
        + [far_spec()] * len(given),
        out_specs=far_spec(),
        scratch_shapes=[
            pltpu.VMEM((half, columns * len(places)), jnp.float32),
            pltpu.SemaphoreType.DMA((len(places),)),
        ],
        input_output_aliases={1 + len(operands): 0} if given else {},
        compiler_params=params(),
        cost_estimate=cost(half * columns * len(pairs), 12 * half * columns * len(pairs)),
    )(limit, *operands, *given)


def after(x, *earlier):
    return lax.optimization_barrier((x, *earlier))[0]


def shards(store, queries, precond, query_rank, valid_rows):
    size = lax.axis_size("ex")
    odd = lax.rem(lax.axis_index("ex"), 2) == 1
    one_ahead = [(i, (i + 1) % size) for i in range(size)]
    ahead = [(i, (i + 2) % size) for i in range(size)]
    even_ahead = ahead[::2]
    swap = [(i, i ^ 1) for i in range(size)]
    over_dim = [(0, 1), (1, 0)]

    def send(block, route, axis="ex"):
        return lax.ppermute(block, axis, route)

    def exchanged(total):
        theirs, ours = total
        return ours, send(theirs, over_dim, "dim")

    def by_parity(at_even, at_odd):
        return jnp.where(odd, at_odd, at_even)

    *own, undivided = prepare(queries, precond[None, :], query_rank)
    first, stores = more_scores(store, [(CHUNKS, [(0, undivided)])], [None])
    own_pair = exchanged(first)
    moved = {}

    def tied(name, block):
        earlier = [first[1]] if name == EARLY else []
        return after(block, *earlier, *(moved[key] for key in TIES.get(name, "").split()))

    def move(name, block, route):
        moved[name] = send(tied(name, block), route)
        return moved[name]

    one_back, three_back, two_back = {}, {}, {}
    for step in ORDER:
        kind, n = step[0], int(step[1:])
        if kind == "B":
            two_back[n] = move(step, own[n], ahead)
        elif kind == "A":
            move(step, own[n], swap)
        elif kind == "C":
            block = two_back[n] if KINDS[n] != "U" else by_parity(own[n], two_back[n])
            move(step, block, swap)
        elif kind == "Z":
            move(step, moved[f"A{n}"], even_ahead)
        elif kind == "E":
            move(step, moved[f"C{n}"], even_ahead if KINDS[n] == "I" else ahead)
        else:
            block = two_back[n] if KINDS[n] == "V" else by_parity(own[n], two_back[n])
            move(step, block, one_ahead)
    for n, kind in enumerate(KINDS):
        if kind == "V":
            one_back[n], three_back[n] = (moved[f"Z{n}"], moved[f"A{n}"]), (moved[f"R{n}"],)
            continue
        swapped = moved[f"C{n}"]
        if kind == "U":
            one_back[n], three_back[n] = (swapped,), (moved[f"E{n}"],)
        elif kind == "I":
            one_back[n], three_back[n] = (swapped, moved[f"A{n}"]), (moved[f"E{n}"], swapped)
        else:
            direct = moved[f"R{n}"]
            one_back[n], three_back[n] = (swapped, direct), (direct, swapped)

    [two] = more_scores(stores, [(n, [(0, two_back[n])]) for n in range(CHUNKS)], [None])
    two_pair = exchanged(two)
    limited = after(valid_rows, two[1])
    one = three = one_pair = None
    todo = set(range(CHUNKS))
    for group in CHAIN:
        pieces = []
        for item in group.split():
            n, parts = int(item[1:]), {"b": (0, 1), "o": (0,), "t": (1,)}[item[0]]
            blocks = one_back[n], three_back[n]
            pieces.append((n, [(part, *blocks[part]) for part in parts]))
            todo -= {n} if 0 in parts else set()
        if one is None:
            one, three, limit = more_scores(
                stores, pieces, [one, three], limited, weight=WEIGHT
            )
        elif one_pair is None:
            one, three = more_scores(stores, pieces, [one, three], weight=WEIGHT)
        else:
            pieces = [(n, [(0, *blocks) for _, *blocks in targets]) for n, targets in pieces]
            [[theirs]] = more_scores(stores, pieces, [three], sides=(0,))
            [[ours]] = more_scores(stores, pieces, [three], sides=(1,))
            three = theirs, ours
        if one_pair is None and not todo:
            one_pair = exchanged(one)
    out = finish(limit, [own_pair, two_pair], (0, 2), STEPS)
    return finish(limit, [one_pair, exchanged(three)], (1, 3), STEPS, out)


def solution(mesh):
    return jax.shard_map(
        shards,
        mesh=mesh,
        in_specs=(
            P(("groups", "ex"), "dim"),
            P(("groups", "ex"), "dim"),
            P("dim"),
            P(("groups", "ex"), None),
            P(("groups", "ex")),
        ),
        out_specs=P(("groups", "ex", "dim"), None),
        check_vma=False,
    )
```

```python
import functools

import jax
import jax.numpy as jnp
from jax import lax
from jax.experimental import pallas as pl
from jax.experimental.pallas import tpu as pltpu
from jax.sharding import PartitionSpec as P

STEPS = 4
KINDS = "UUT"
PARTS = (4, 6, 6)
CHAIN = ("b0", "o1", "b2", "t1")
ORDER = ("B0", "B1", "B2", "C0", "C1", "E0", "E1", "R2", "C2")
TIES = {"C2": "C0", "R2": "C0"}
EARLY = "C0"
WEIGHT = 2
CHUNKS = len(PARTS)
VMEM_BYTES = 16 * 1024 * 1024


def params():
    return pltpu.CompilerParams(vmem_limit_bytes=VMEM_BYTES)


def whole_spec():
    return pl.BlockSpec(memory_space=pltpu.VMEM)


def far_spec():
    return pl.BlockSpec(memory_space=pltpu.HBM)


def in_hbm(x):
    return pltpu.with_memory_space_constraint(x, pltpu.HBM)


def cost(flops, traffic):
    return pl.CostEstimate(flops=flops, bytes_accessed=traffic, transcendentals=0)


def cuts_of(depth):
    ends = [depth * sum(PARTS[:n + 1]) // sum(PARTS) for n in range(CHUNKS)]
    return [slice(start, end) for start, end in zip([0] + ends, ends)]


def product(rows, block):
    return lax.dot_general(
        rows, block, (((1,), (1,)), ((), ())), preferred_element_type=jnp.float32
    )


def prepare_kernel(queries, precond, rank, *refs):
    chunks, (own, held, scale, places, arrived) = refs[:CHUNKS], refs[CHUNKS:]
    rows, depth = queries.shape
    cuts = cuts_of(depth)
    loads = [pltpu.make_async_copy(rank, places, arrived.at[CHUNKS])]
    loads.append(pltpu.make_async_copy(precond, scale, arrived.at[CHUNKS + 1]))
    for n, cut in enumerate(cuts):
        loads.append(pltpu.make_async_copy(queries.at[:, cut], held.at[:, cut], arrived.at[n]))
    for load in loads:
        load.start()
    loads[0].wait()
    loads[1].wait()
    positions = lax.broadcasted_iota(jnp.int32, (rows, rows), 0)
    placing = (positions == places[...]).astype(jnp.bfloat16)
    for n, cut in enumerate(cuts):
        loads[2 + n].wait()
        pre = (held[:, cut].astype(jnp.float32) * scale[:, cut]).astype(jnp.bfloat16)
        ordered = jnp.dot(placing, pre, preferred_element_type=jnp.float32).astype(jnp.bfloat16)
        chunks[n][...] = ordered
        own[:, cut] = ordered


def prepare(queries, precond, rank):
    rows, depth = queries.shape
    shapes = [
        jax.ShapeDtypeStruct((rows, cut.stop - cut.start), jnp.bfloat16) for cut in cuts_of(depth)
    ]
    return pl.pallas_call(
        prepare_kernel,
        out_shape=shapes + [jax.ShapeDtypeStruct((rows, depth), jnp.bfloat16)],
        in_specs=[far_spec()] * 3,
        out_specs=[whole_spec()] * (CHUNKS + 1),
        scratch_shapes=[
            pltpu.VMEM((rows, depth), jnp.bfloat16),
            pltpu.VMEM((1, depth), jnp.float32),
            pltpu.VMEM((1, rows), jnp.int32),
            pltpu.SemaphoreType.DMA((CHUNKS + 2,)),
        ],
        compiler_params=params(),
        cost_estimate=cost(2 * rows * rows * depth, 4 * rows * depth),
    )(in_hbm(queries), in_hbm(precond), in_hbm(rank))


def scores_kernel(pieces, fresh, loading, counted, sides, *refs):
    count = len(fresh)
    if counted:
        valid, *refs, limit = refs
        limit[...] = jnp.full(limit.shape, valid[0], jnp.int32)
    odd = lax.rem(lax.axis_index("ex"), 2) == 1
    loads = []
    if loading:
        store, *refs = refs
        *refs, other, mine, arrived = refs
        stores = other, mine
        half = other.shape[0]
        me = lax.axis_index("dim")
        for side, where in enumerate((1 - me, me)):
            place = pl.ds(pl.multiple_of(where * half, half), half)
            loads.append(pltpu.make_async_copy(store.at[place], stores[side], arrived.at[side]))
            loads[side].start()
    else:
        other, mine, *refs = refs
        stores = other, mine
    count_out = len(sides) * count
    outs = refs[-count_out:]
    carried = refs[-count_out - len(sides) * (count - sum(fresh)):-count_out]
    cuts = cuts_of(other.shape[1]) + [slice(0, other.shape[1])]
    stacks = []
    for n, targets in pieces:
        values = []
        for _, even_place, odd_place in targets:
            value = refs[even_place][...]
            if odd_place != even_place:
                value = jnp.where(odd, refs[odd_place][...], value)
            values.append(value)
        stacked = values[0] if len(values) == 1 else jnp.concatenate(values, axis=0)
        stacks.append((n, [which for which, _, _ in targets], stacked))
    for at_side, side in enumerate(sides):
        store = stores[side]
        if loading:
            loads[side].wait()
        sums, at = {}, 0
        for i, new in enumerate(fresh):
            sums[i] = None if new else carried[at + at_side][...]
            at += 0 if new else len(sides)
        for n, whiches, stacked in stacks:
            part = product(store[:, cuts[n]], stacked)
            columns = stacked.shape[0] // len(whiches)
            for k, i in enumerate(whiches):
                here = part[:, k * columns:(k + 1) * columns]
                sums[i] = here if sums[i] is None else sums[i] + here
        for i in range(count):
            outs[len(sides) * i + at_side][...] = sums[i]


def more_scores(stores, pieces, carries, valid=None, sides=(0, 1), weight=1):
    operands, placed = [], []

    def place(block):
        known = [i for i, operand in enumerate(operands) if operand is block]
        if not known:
            operands.append(block)
        return known[0] if known else len(operands) - 1

    loading = not isinstance(stores, tuple)
    half, depth = stores.shape[0] // 2 if loading else stores[0].shape[0], 0
    flops = 0
    for n, targets in pieces:
        kept = []
        for which, *blocks in targets:
            places = [place(block) for block in blocks]
            kept.append((which, places[0], places[-1]))
            flops += 4 * half * blocks[0].size
        placed.append((n, tuple(kept)))
    columns = operands[0].shape[0]
    fresh = tuple(carry is None for carry in carries)
    first = [in_hbm(stores)] if loading else list(stores)
    operands += [carry[side] for carry in carries if carry for side in sides]
    specs = [far_spec()] if loading else [whole_spec()] * 2
    total = jax.ShapeDtypeStruct((half, columns), jnp.float32)
    more = []
    if loading:
        held = jax.ShapeDtypeStruct((half, stores.shape[1]), stores.dtype)
        more = [held, held]
    if valid is not None:
        first, more = [valid] + first, more + [jax.ShapeDtypeStruct((8, columns), jnp.int32)]
        specs = [pl.BlockSpec(memory_space=pltpu.SMEM)] + specs
    count = len(sides) * len(carries)
    outs = pl.pallas_call(
        functools.partial(scores_kernel, tuple(placed), fresh, loading, valid is not None, sides),
        out_shape=[total] * count + more,
        in_specs=specs + [whole_spec()] * len(operands),
        out_specs=[whole_spec()] * (count + len(more)),
        scratch_shapes=[pltpu.SemaphoreType.DMA((2,))] if loading else [],
        compiler_params=params(),
        cost_estimate=cost(weight * flops, weight * 4 * half * columns * count),
    )(*first, *operands)
    totals = [tuple(outs[i:i + len(sides)]) for i in range(0, count, len(sides))]
    if valid is not None:
        return totals + [outs[-1]]
    return totals + ([tuple(outs[count:])] if loading else [])


def finish_kernel(places, limit, *refs):
    out, summed, left = refs[-3:]
    half, columns = refs[0].shape
    row_ids = lax.broadcasted_iota(jnp.int32, (half, columns), 0) + lax.axis_index("dim") * half
    inside = row_ids < limit[:1, :]
    stores = []
    for n, place in enumerate(places):
        cut = slice(n * columns, (n + 1) * columns)
        summed[:, cut] = jnp.where(inside, refs[2 * n][...] + refs[2 * n + 1][...], 0.0)
        to = out.at[:, place * columns:(place + 1) * columns]
        stores.append(pltpu.make_async_copy(summed.at[:, cut], to, left.at[n]))
        stores[n].start()
    for store in stores:
        store.wait()


def finish(limit, pairs, places, steps, out=None):
    half, columns = pairs[0][0].shape
    operands = [ref for pair in pairs for ref in pair]
    given = [] if out is None else [in_hbm(out)]
    return pl.pallas_call(
        functools.partial(finish_kernel, places),
        out_shape=pltpu.HBM((half, columns * steps), jnp.float32),
        in_specs=[whole_spec()] * (1 + len(operands))
        + [far_spec()] * len(given),
        out_specs=far_spec(),
        scratch_shapes=[
            pltpu.VMEM((half, columns * len(places)), jnp.float32),
            pltpu.SemaphoreType.DMA((len(places),)),
        ],
        input_output_aliases={1 + len(operands): 0} if given else {},
        compiler_params=params(),
        cost_estimate=cost(half * columns * len(pairs), 12 * half * columns * len(pairs)),
    )(limit, *operands, *given)


def after(x, *earlier):
    return lax.optimization_barrier((x, *earlier))[0]


def shards(store, queries, precond, query_rank, valid_rows):
    size = lax.axis_size("ex")
    odd = lax.rem(lax.axis_index("ex"), 2) == 1
    one_ahead = [(i, (i + 1) % size) for i in range(size)]
    ahead = [(i, (i + 2) % size) for i in range(size)]
    even_ahead = ahead[::2]
    swap = [(i, i ^ 1) for i in range(size)]
    over_dim = [(0, 1), (1, 0)]

    def send(block, route, axis="ex"):
        return lax.ppermute(block, axis, route)

    def exchanged(total):
        theirs, ours = total
        return ours, send(theirs, over_dim, "dim")

    def by_parity(at_even, at_odd):
        return jnp.where(odd, at_odd, at_even)

    *own, undivided = prepare(queries, precond[None, :], query_rank)
    first, stores = more_scores(store, [(CHUNKS, [(0, undivided)])], [None])
    own_pair = exchanged(first)
    moved = {}

    def tied(name, block):
        earlier = [first[1]] if name == EARLY else []
        return after(block, *earlier, *(moved[key] for key in TIES.get(name, "").split()))

    def move(name, block, route):
        moved[name] = send(tied(name, block), route)
        return moved[name]

    one_back, three_back, two_back = {}, {}, {}
    for step in ORDER:
        kind, n = step[0], int(step[1:])
        if kind == "B":
            two_back[n] = move(step, own[n], ahead)
        elif kind == "A":
            move(step, own[n], swap)
        elif kind == "C":
            block = two_back[n] if KINDS[n] != "U" else by_parity(own[n], two_back[n])
            move(step, block, swap)
        elif kind == "Z":
            move(step, moved[f"A{n}"], even_ahead)
        elif kind == "E":
            move(step, moved[f"C{n}"], even_ahead if KINDS[n] == "I" else ahead)
        else:
            block = two_back[n] if KINDS[n] == "V" else by_parity(own[n], two_back[n])
            move(step, block, one_ahead)
    for n, kind in enumerate(KINDS):
        if kind == "V":
            one_back[n], three_back[n] = (moved[f"Z{n}"], moved[f"A{n}"]), (moved[f"R{n}"],)
            continue
        swapped = moved[f"C{n}"]
        if kind == "U":
            one_back[n], three_back[n] = (swapped,), (moved[f"E{n}"],)
        elif kind == "I":
            one_back[n], three_back[n] = (swapped, moved[f"A{n}"]), (moved[f"E{n}"], swapped)
        else:
            direct = moved[f"R{n}"]
            one_back[n], three_back[n] = (swapped, direct), (direct, swapped)

    [two] = more_scores(stores, [(n, [(0, two_back[n])]) for n in range(CHUNKS)], [None])
    two_pair = exchanged(two)
    limited = after(valid_rows, two[1])
    one = three = one_pair = None
    todo = set(range(CHUNKS))
    for group in CHAIN:
        pieces = []
        for item in group.split():
            n, parts = int(item[1:]), {"b": (0, 1), "o": (0,), "t": (1,)}[item[0]]
            blocks = one_back[n], three_back[n]
            pieces.append((n, [(part, *blocks[part]) for part in parts]))
            todo -= {n} if 0 in parts else set()
        if one is None:
            one, three, limit = more_scores(
                stores, pieces, [one, three], limited, weight=WEIGHT
            )
        elif one_pair is None:
            one, three = more_scores(stores, pieces, [one, three], weight=WEIGHT)
        else:
            pieces = [(n, [(0, *blocks) for _, *blocks in targets]) for n, targets in pieces]
            [[theirs]] = more_scores(stores, pieces, [three], sides=(0,))
            [[ours]] = more_scores(stores, pieces, [three], sides=(1,))
            three = theirs, ours
        if one_pair is None and not todo:
            one_pair = exchanged(one)
    out = finish(limit, [own_pair, two_pair], (0, 2), STEPS)
    return finish(limit, [one_pair, exchanged(three)], (1, 3), STEPS, out)


def solution(mesh):
    return jax.shard_map(
        shards,
        mesh=mesh,
        in_specs=(
            P(("groups", "ex"), "dim"),
            P(("groups", "ex"), "dim"),
            P("dim"),
            P(("groups", "ex"), None),
            P(("groups", "ex")),
        ),
        out_specs=P(("groups", "ex", "dim"), None),
        check_vma=False,
    )
```

```python
import functools

import jax
import jax.numpy as jnp
from jax import lax
from jax.experimental import pallas as pl
from jax.experimental.pallas import tpu as pltpu
from jax.sharding import PartitionSpec as P

STEPS = 4
KINDS = "UUT"
PARTS = (4, 6, 6)
CHAIN = ("b0", "o1", "b2", "t1")
ORDER = ("B0", "B1", "B2", "C0", "C1", "E0", "E1", "R2", "C2")
TIES = {"C2": "C0"}
EARLY = "none"
WEIGHT = 2
CHUNKS = len(PARTS)
VMEM_BYTES = 16 * 1024 * 1024


def params():
    return pltpu.CompilerParams(vmem_limit_bytes=VMEM_BYTES)


def whole_spec():
    return pl.BlockSpec(memory_space=pltpu.VMEM)


def far_spec():
    return pl.BlockSpec(memory_space=pltpu.HBM)


def in_hbm(x):
    return pltpu.with_memory_space_constraint(x, pltpu.HBM)


def cost(flops, traffic):
    return pl.CostEstimate(flops=flops, bytes_accessed=traffic, transcendentals=0)


def cuts_of(depth):
    ends = [depth * sum(PARTS[:n + 1]) // sum(PARTS) for n in range(CHUNKS)]
    return [slice(start, end) for start, end in zip([0] + ends, ends)]


def product(rows, block):
    return lax.dot_general(
        rows, block, (((1,), (1,)), ((), ())), preferred_element_type=jnp.float32
    )


def prepare_kernel(queries, precond, rank, *refs):
    chunks, (own, held, scale, places, arrived) = refs[:CHUNKS], refs[CHUNKS:]
    rows, depth = queries.shape
    cuts = cuts_of(depth)
    loads = [pltpu.make_async_copy(rank, places, arrived.at[CHUNKS])]
    loads.append(pltpu.make_async_copy(precond, scale, arrived.at[CHUNKS + 1]))
    for n, cut in enumerate(cuts):
        loads.append(pltpu.make_async_copy(queries.at[:, cut], held.at[:, cut], arrived.at[n]))
    for load in loads:
        load.start()
    loads[0].wait()
    loads[1].wait()
    positions = lax.broadcasted_iota(jnp.int32, (rows, rows), 0)
    placing = (positions == places[...]).astype(jnp.bfloat16)
    for n, cut in enumerate(cuts):
        loads[2 + n].wait()
        pre = (held[:, cut].astype(jnp.float32) * scale[:, cut]).astype(jnp.bfloat16)
        ordered = jnp.dot(placing, pre, preferred_element_type=jnp.float32).astype(jnp.bfloat16)
        chunks[n][...] = ordered
        own[:, cut] = ordered


def prepare(queries, precond, rank):
    rows, depth = queries.shape
    shapes = [
        jax.ShapeDtypeStruct((rows, cut.stop - cut.start), jnp.bfloat16) for cut in cuts_of(depth)
    ]
    return pl.pallas_call(
        prepare_kernel,
        out_shape=shapes + [jax.ShapeDtypeStruct((rows, depth), jnp.bfloat16)],
        in_specs=[far_spec()] * 3,
        out_specs=[whole_spec()] * (CHUNKS + 1),
        scratch_shapes=[
            pltpu.VMEM((rows, depth), jnp.bfloat16),
            pltpu.VMEM((1, depth), jnp.float32),
            pltpu.VMEM((1, rows), jnp.int32),
            pltpu.SemaphoreType.DMA((CHUNKS + 2,)),
        ],
        compiler_params=params(),
        cost_estimate=cost(2 * rows * rows * depth, 4 * rows * depth),
    )(in_hbm(queries), in_hbm(precond), in_hbm(rank))


def scores_kernel(pieces, fresh, loading, counted, sides, *refs):
    count = len(fresh)
    if counted:
        valid, *refs, limit = refs
        limit[...] = jnp.full(limit.shape, valid[0], jnp.int32)
    odd = lax.rem(lax.axis_index("ex"), 2) == 1
    loads = []
    if loading:
        store, *refs = refs
        *refs, other, mine, arrived = refs
        stores = other, mine
        half = other.shape[0]
        me = lax.axis_index("dim")
        for side, where in enumerate((1 - me, me)):
            place = pl.ds(pl.multiple_of(where * half, half), half)
            loads.append(pltpu.make_async_copy(store.at[place], stores[side], arrived.at[side]))
            loads[side].start()
    else:
        other, mine, *refs = refs
        stores = other, mine
    count_out = len(sides) * count
    outs = refs[-count_out:]
    carried = refs[-count_out - len(sides) * (count - sum(fresh)):-count_out]
    cuts = cuts_of(other.shape[1]) + [slice(0, other.shape[1])]
    stacks = []
    for n, targets in pieces:
        values = []
        for _, even_place, odd_place in targets:
            value = refs[even_place][...]
            if odd_place != even_place:
                value = jnp.where(odd, refs[odd_place][...], value)
            values.append(value)
        stacked = values[0] if len(values) == 1 else jnp.concatenate(values, axis=0)
        stacks.append((n, [which for which, _, _ in targets], stacked))
    for at_side, side in enumerate(sides):
        store = stores[side]
        if loading:
            loads[side].wait()
        sums, at = {}, 0
        for i, new in enumerate(fresh):
            sums[i] = None if new else carried[at + at_side][...]
            at += 0 if new else len(sides)
        for n, whiches, stacked in stacks:
            part = product(store[:, cuts[n]], stacked)
            columns = stacked.shape[0] // len(whiches)
            for k, i in enumerate(whiches):
                here = part[:, k * columns:(k + 1) * columns]
                sums[i] = here if sums[i] is None else sums[i] + here
        for i in range(count):
            outs[len(sides) * i + at_side][...] = sums[i]


def more_scores(stores, pieces, carries, valid=None, sides=(0, 1), weight=1):
    operands, placed = [], []

    def place(block):
        known = [i for i, operand in enumerate(operands) if operand is block]
        if not known:
            operands.append(block)
        return known[0] if known else len(operands) - 1

    loading = not isinstance(stores, tuple)
    half, depth = stores.shape[0] // 2 if loading else stores[0].shape[0], 0
    flops = 0
    for n, targets in pieces:
        kept = []
        for which, *blocks in targets:
            places = [place(block) for block in blocks]
            kept.append((which, places[0], places[-1]))
            flops += 4 * half * blocks[0].size
        placed.append((n, tuple(kept)))
    columns = operands[0].shape[0]
    fresh = tuple(carry is None for carry in carries)
    first = [in_hbm(stores)] if loading else list(stores)
    operands += [carry[side] for carry in carries if carry for side in sides]
    specs = [far_spec()] if loading else [whole_spec()] * 2
    total = jax.ShapeDtypeStruct((half, columns), jnp.float32)
    more = []
    if loading:
        held = jax.ShapeDtypeStruct((half, stores.shape[1]), stores.dtype)
        more = [held, held]
    if valid is not None:
        first, more = [valid] + first, more + [jax.ShapeDtypeStruct((8, columns), jnp.int32)]
        specs = [pl.BlockSpec(memory_space=pltpu.SMEM)] + specs
    count = len(sides) * len(carries)
    outs = pl.pallas_call(
        functools.partial(scores_kernel, tuple(placed), fresh, loading, valid is not None, sides),
        out_shape=[total] * count + more,
        in_specs=specs + [whole_spec()] * len(operands),
        out_specs=[whole_spec()] * (count + len(more)),
        scratch_shapes=[pltpu.SemaphoreType.DMA((2,))] if loading else [],
        compiler_params=params(),
        cost_estimate=cost(weight * flops, weight * 4 * half * columns * count),
    )(*first, *operands)
    totals = [tuple(outs[i:i + len(sides)]) for i in range(0, count, len(sides))]
    if valid is not None:
        return totals + [outs[-1]]
    return totals + ([tuple(outs[count:])] if loading else [])


def finish_kernel(places, limit, *refs):
    out, summed, left = refs[-3:]
    half, columns = refs[0].shape
    row_ids = lax.broadcasted_iota(jnp.int32, (half, columns), 0) + lax.axis_index("dim") * half
    inside = row_ids < limit[:1, :]
    stores = []
    for n, place in enumerate(places):
        cut = slice(n * columns, (n + 1) * columns)
        summed[:, cut] = jnp.where(inside, refs[2 * n][...] + refs[2 * n + 1][...], 0.0)
        to = out.at[:, place * columns:(place + 1) * columns]
        stores.append(pltpu.make_async_copy(summed.at[:, cut], to, left.at[n]))
        stores[n].start()
    for store in stores:
        store.wait()


def finish(limit, pairs, places, steps, out=None):
    half, columns = pairs[0][0].shape
    operands = [ref for pair in pairs for ref in pair]
    given = [] if out is None else [in_hbm(out)]
    return pl.pallas_call(
        functools.partial(finish_kernel, places),
        out_shape=pltpu.HBM((half, columns * steps), jnp.float32),
        in_specs=[whole_spec()] * (1 + len(operands))
        + [far_spec()] * len(given),
        out_specs=far_spec(),
        scratch_shapes=[
            pltpu.VMEM((half, columns * len(places)), jnp.float32),
            pltpu.SemaphoreType.DMA((len(places),)),
        ],
        input_output_aliases={1 + len(operands): 0} if given else {},
        compiler_params=params(),
        cost_estimate=cost(half * columns * len(pairs), 12 * half * columns * len(pairs)),
    )(limit, *operands, *given)


def after(x, *earlier):
    return lax.optimization_barrier((x, *earlier))[0]


def shards(store, queries, precond, query_rank, valid_rows):
    size = lax.axis_size("ex")
    odd = lax.rem(lax.axis_index("ex"), 2) == 1
    one_ahead = [(i, (i + 1) % size) for i in range(size)]
    ahead = [(i, (i + 2) % size) for i in range(size)]
    even_ahead = ahead[::2]
    swap = [(i, i ^ 1) for i in range(size)]
    over_dim = [(0, 1), (1, 0)]

    def send(block, route, axis="ex"):
        return lax.ppermute(block, axis, route)

    def exchanged(total):
        theirs, ours = total
        return ours, send(theirs, over_dim, "dim")

    def by_parity(at_even, at_odd):
        return jnp.where(odd, at_odd, at_even)

    *own, undivided = prepare(queries, precond[None, :], query_rank)
    first, stores = more_scores(store, [(CHUNKS, [(0, undivided)])], [None])
    own_pair = exchanged(first)
    moved = {}

    def tied(name, block):
        earlier = [first[1]] if name == EARLY else []
        return after(block, *earlier, *(moved[key] for key in TIES.get(name, "").split()))

    def move(name, block, route):
        moved[name] = send(tied(name, block), route)
        return moved[name]

    one_back, three_back, two_back = {}, {}, {}
    for step in ORDER:
        kind, n = step[0], int(step[1:])
        if kind == "B":
            two_back[n] = move(step, own[n], ahead)
        elif kind == "A":
            move(step, own[n], swap)
        elif kind == "C":
            block = two_back[n] if KINDS[n] != "U" else by_parity(own[n], two_back[n])
            move(step, block, swap)
        elif kind == "Z":
            move(step, moved[f"A{n}"], even_ahead)
        elif kind == "E":
            move(step, moved[f"C{n}"], even_ahead if KINDS[n] == "I" else ahead)
        else:
            block = two_back[n] if KINDS[n] == "V" else by_parity(own[n], two_back[n])
            move(step, block, one_ahead)
    for n, kind in enumerate(KINDS):
        if kind == "V":
            one_back[n], three_back[n] = (moved[f"Z{n}"], moved[f"A{n}"]), (moved[f"R{n}"],)
            continue
        swapped = moved[f"C{n}"]
        if kind == "U":
            one_back[n], three_back[n] = (swapped,), (moved[f"E{n}"],)
        elif kind == "I":
            one_back[n], three_back[n] = (swapped, moved[f"A{n}"]), (moved[f"E{n}"], swapped)
        else:
            direct = moved[f"R{n}"]
            one_back[n], three_back[n] = (swapped, direct), (direct, swapped)

    [two] = more_scores(stores, [(n, [(0, two_back[n])]) for n in range(CHUNKS)], [None])
    two_pair = exchanged(two)
    limited = after(valid_rows, two[1])
    one = three = one_pair = None
    todo = set(range(CHUNKS))
    for group in CHAIN:
        pieces = []
        for item in group.split():
            n, parts = int(item[1:]), {"b": (0, 1), "o": (0,), "t": (1,)}[item[0]]
            blocks = one_back[n], three_back[n]
            pieces.append((n, [(part, *blocks[part]) for part in parts]))
            todo -= {n} if 0 in parts else set()
        if one is None:
            one, three, limit = more_scores(
                stores, pieces, [one, three], limited, weight=WEIGHT
            )
        elif one_pair is None:
            one, three = more_scores(stores, pieces, [one, three], weight=WEIGHT)
        else:
            pieces = [(n, [(0, *blocks) for _, *blocks in targets]) for n, targets in pieces]
            [[theirs]] = more_scores(stores, pieces, [three], sides=(0,))
            [[ours]] = more_scores(stores, pieces, [three], sides=(1,))
            three = theirs, ours
        if one_pair is None and not todo:
            one_pair = exchanged(one)
    out = finish(limit, [own_pair, two_pair], (0, 2), STEPS)
    return finish(limit, [one_pair, exchanged(three)], (1, 3), STEPS, out)


def solution(mesh):
    return jax.shard_map(
        shards,
        mesh=mesh,
        in_specs=(
            P(("groups", "ex"), "dim"),
            P(("groups", "ex"), "dim"),
            P("dim"),
            P(("groups", "ex"), None),
            P(("groups", "ex")),
        ),
        out_specs=P(("groups", "ex", "dim"), None),
        check_vma=False,
    )
```

```python
import functools

import jax
import jax.numpy as jnp
from jax import lax
from jax.experimental import pallas as pl
from jax.experimental.pallas import tpu as pltpu
from jax.sharding import PartitionSpec as P

STEPS = 4
KINDS = "UUT"
PARTS = (4, 6, 6)
CHAIN = ("b0", "o1", "b2", "t1")
ORDER = ("B0", "B1", "B2", "C0", "C1", "E0", "E1", "R2", "C2")
TIES = {"C2": "C0"}
EARLY = "C0"
WEIGHT = 2
CHUNKS = len(PARTS)
VMEM_BYTES = 16 * 1024 * 1024


def params():
    return pltpu.CompilerParams(vmem_limit_bytes=VMEM_BYTES)


def whole_spec():
    return pl.BlockSpec(memory_space=pltpu.VMEM)


def far_spec():
    return pl.BlockSpec(memory_space=pltpu.HBM)


def in_hbm(x):
    return pltpu.with_memory_space_constraint(x, pltpu.HBM)


def cost(flops, traffic):
    return pl.CostEstimate(flops=flops, bytes_accessed=traffic, transcendentals=0)


def cuts_of(depth):
    ends = [depth * sum(PARTS[:n + 1]) // sum(PARTS) for n in range(CHUNKS)]
    return [slice(start, end) for start, end in zip([0] + ends, ends)]


def product(rows, block):
    return lax.dot_general(
        rows, block, (((1,), (1,)), ((), ())), preferred_element_type=jnp.float32
    )


def prepare_kernel(queries, precond, rank, *refs):
    chunks, (own, held, scale, places, arrived) = refs[:CHUNKS], refs[CHUNKS:]
    rows, depth = queries.shape
    cuts = cuts_of(depth)
    loads = [pltpu.make_async_copy(rank, places, arrived.at[CHUNKS])]
    loads.append(pltpu.make_async_copy(precond, scale, arrived.at[CHUNKS + 1]))
    for n, cut in enumerate(cuts):
        loads.append(pltpu.make_async_copy(queries.at[:, cut], held.at[:, cut], arrived.at[n]))
    for load in loads[2:] + loads[:2]:
        load.start()
    loads[0].wait()
    positions = lax.broadcasted_iota(jnp.int32, (rows, rows), 0)
    placing = (positions == places[...]).astype(jnp.bfloat16)
    loads[1].wait()
    for n, cut in enumerate(cuts):
        loads[2 + n].wait()
        pre = (held[:, cut].astype(jnp.float32) * scale[:, cut]).astype(jnp.bfloat16)
        ordered = jnp.dot(placing, pre, preferred_element_type=jnp.float32).astype(jnp.bfloat16)
        chunks[n][...] = ordered
        own[:, cut] = ordered


def prepare(queries, precond, rank):
    rows, depth = queries.shape
    shapes = [
        jax.ShapeDtypeStruct((rows, cut.stop - cut.start), jnp.bfloat16) for cut in cuts_of(depth)
    ]
    return pl.pallas_call(
        prepare_kernel,
        out_shape=shapes + [jax.ShapeDtypeStruct((rows, depth), jnp.bfloat16)],
        in_specs=[far_spec()] * 3,
        out_specs=[whole_spec()] * (CHUNKS + 1),
        scratch_shapes=[
            pltpu.VMEM((rows, depth), jnp.bfloat16),
            pltpu.VMEM((1, depth), jnp.float32),
            pltpu.VMEM((1, rows), jnp.int32),
            pltpu.SemaphoreType.DMA((CHUNKS + 2,)),
        ],
        compiler_params=params(),
        cost_estimate=cost(2 * rows * rows * depth, 4 * rows * depth),
    )(in_hbm(queries), in_hbm(precond), in_hbm(rank))


def scores_kernel(pieces, fresh, loading, counted, sides, *refs):
    count = len(fresh)
    if counted:
        valid, *refs, limit = refs
        limit[...] = jnp.full(limit.shape, valid[0], jnp.int32)
    odd = lax.rem(lax.axis_index("ex"), 2) == 1
    loads = []
    if loading:
        store, *refs = refs
        *refs, other, mine, arrived = refs
        stores = other, mine
        half = other.shape[0]
        me = lax.axis_index("dim")
        for side, where in enumerate((1 - me, me)):
            place = pl.ds(pl.multiple_of(where * half, half), half)
            loads.append(pltpu.make_async_copy(store.at[place], stores[side], arrived.at[side]))
            loads[side].start()
    else:
        other, mine, *refs = refs
        stores = other, mine
    count_out = len(sides) * count
    outs = refs[-count_out:]
    carried = refs[-count_out - len(sides) * (count - sum(fresh)):-count_out]
    cuts = cuts_of(other.shape[1]) + [slice(0, other.shape[1])]
    stacks = []
    for n, targets in pieces:
        values = []
        for _, even_place, odd_place in targets:
            value = refs[even_place][...]
            if odd_place != even_place:
                value = jnp.where(odd, refs[odd_place][...], value)
            values.append(value)
        stacked = values[0] if len(values) == 1 else jnp.concatenate(values, axis=0)
        stacks.append((n, [which for which, _, _ in targets], stacked))
    for at_side, side in enumerate(sides):
        store = stores[side]
        if loading:
            loads[side].wait()
        sums, at = {}, 0
        for i, new in enumerate(fresh):
            sums[i] = None if new else carried[at + at_side][...]
            at += 0 if new else len(sides)
        for n, whiches, stacked in stacks:
            part = product(store[:, cuts[n]], stacked)
            columns = stacked.shape[0] // len(whiches)
            for k, i in enumerate(whiches):
                here = part[:, k * columns:(k + 1) * columns]
                sums[i] = here if sums[i] is None else sums[i] + here
        for i in range(count):
            outs[len(sides) * i + at_side][...] = sums[i]


def more_scores(stores, pieces, carries, valid=None, sides=(0, 1), weight=1):
    operands, placed = [], []

    def place(block):
        known = [i for i, operand in enumerate(operands) if operand is block]
        if not known:
            operands.append(block)
        return known[0] if known else len(operands) - 1

    loading = not isinstance(stores, tuple)
    half, depth = stores.shape[0] // 2 if loading else stores[0].shape[0], 0
    flops = 0
    for n, targets in pieces:
        kept = []
        for which, *blocks in targets:
            places = [place(block) for block in blocks]
            kept.append((which, places[0], places[-1]))
            flops += 4 * half * blocks[0].size
        placed.append((n, tuple(kept)))
    columns = operands[0].shape[0]
    fresh = tuple(carry is None for carry in carries)
    first = [in_hbm(stores)] if loading else list(stores)
    operands += [carry[side] for carry in carries if carry for side in sides]
    specs = [far_spec()] if loading else [whole_spec()] * 2
    total = jax.ShapeDtypeStruct((half, columns), jnp.float32)
    more = []
    if loading:
        held = jax.ShapeDtypeStruct((half, stores.shape[1]), stores.dtype)
        more = [held, held]
    if valid is not None:
        first, more = [valid] + first, more + [jax.ShapeDtypeStruct((8, columns), jnp.int32)]
        specs = [pl.BlockSpec(memory_space=pltpu.SMEM)] + specs
    count = len(sides) * len(carries)
    outs = pl.pallas_call(
        functools.partial(scores_kernel, tuple(placed), fresh, loading, valid is not None, sides),
        out_shape=[total] * count + more,
        in_specs=specs + [whole_spec()] * len(operands),
        out_specs=[whole_spec()] * (count + len(more)),
        scratch_shapes=[pltpu.SemaphoreType.DMA((2,))] if loading else [],
        compiler_params=params(),
        cost_estimate=cost(weight * flops, weight * 4 * half * columns * count),
    )(*first, *operands)
    totals = [tuple(outs[i:i + len(sides)]) for i in range(0, count, len(sides))]
    if valid is not None:
        return totals + [outs[-1]]
    return totals + ([tuple(outs[count:])] if loading else [])


def finish_kernel(places, limit, *refs):
    out, summed, left = refs[-3:]
    half, columns = refs[0].shape
    row_ids = lax.broadcasted_iota(jnp.int32, (half, columns), 0) + lax.axis_index("dim") * half
    inside = row_ids < limit[:1, :]
    stores = []
    for n, place in enumerate(places):
        cut = slice(n * columns, (n + 1) * columns)
        summed[:, cut] = jnp.where(inside, refs[2 * n][...] + refs[2 * n + 1][...], 0.0)
        to = out.at[:, place * columns:(place + 1) * columns]
        stores.append(pltpu.make_async_copy(summed.at[:, cut], to, left.at[n]))
        stores[n].start()
    for store in stores:
        store.wait()


def finish(limit, pairs, places, steps, out=None):
    half, columns = pairs[0][0].shape
    operands = [ref for pair in pairs for ref in pair]
    given = [] if out is None else [in_hbm(out)]
    return pl.pallas_call(
        functools.partial(finish_kernel, places),
        out_shape=pltpu.HBM((half, columns * steps), jnp.float32),
        in_specs=[whole_spec()] * (1 + len(operands))
        + [far_spec()] * len(given),
        out_specs=far_spec(),
        scratch_shapes=[
            pltpu.VMEM((half, columns * len(places)), jnp.float32),
            pltpu.SemaphoreType.DMA((len(places),)),
        ],
        input_output_aliases={1 + len(operands): 0} if given else {},
        compiler_params=params(),
        cost_estimate=cost(half * columns * len(pairs), 12 * half * columns * len(pairs)),
    )(limit, *operands, *given)


def after(x, *earlier):
    return lax.optimization_barrier((x, *earlier))[0]


def shards(store, queries, precond, query_rank, valid_rows):
    size = lax.axis_size("ex")
    odd = lax.rem(lax.axis_index("ex"), 2) == 1
    one_ahead = [(i, (i + 1) % size) for i in range(size)]
    ahead = [(i, (i + 2) % size) for i in range(size)]
    even_ahead = ahead[::2]
    swap = [(i, i ^ 1) for i in range(size)]
    over_dim = [(0, 1), (1, 0)]

    def send(block, route, axis="ex"):
        return lax.ppermute(block, axis, route)

    def exchanged(total):
        theirs, ours = total
        return ours, send(theirs, over_dim, "dim")

    def by_parity(at_even, at_odd):
        return jnp.where(odd, at_odd, at_even)

    *own, undivided = prepare(queries, precond[None, :], query_rank)
    first, stores = more_scores(store, [(CHUNKS, [(0, undivided)])], [None])
    own_pair = exchanged(first)
    moved = {}

    def tied(name, block):
        earlier = [first[1]] if name == EARLY else []
        return after(block, *earlier, *(moved[key] for key in TIES.get(name, "").split()))

    def move(name, block, route):
        moved[name] = send(tied(name, block), route)
        return moved[name]

    one_back, three_back, two_back = {}, {}, {}
    for step in ORDER:
        kind, n = step[0], int(step[1:])
        if kind == "B":
            two_back[n] = move(step, own[n], ahead)
        elif kind == "A":
            move(step, own[n], swap)
        elif kind == "C":
            block = two_back[n] if KINDS[n] != "U" else by_parity(own[n], two_back[n])
            move(step, block, swap)
        elif kind == "Z":
            move(step, moved[f"A{n}"], even_ahead)
        elif kind == "E":
            move(step, moved[f"C{n}"], even_ahead if KINDS[n] == "I" else ahead)
        else:
            block = two_back[n] if KINDS[n] == "V" else by_parity(own[n], two_back[n])
            move(step, block, one_ahead)
    for n, kind in enumerate(KINDS):
        if kind == "V":
            one_back[n], three_back[n] = (moved[f"Z{n}"], moved[f"A{n}"]), (moved[f"R{n}"],)
            continue
        swapped = moved[f"C{n}"]
        if kind == "U":
            one_back[n], three_back[n] = (swapped,), (moved[f"E{n}"],)
        elif kind == "I":
            one_back[n], three_back[n] = (swapped, moved[f"A{n}"]), (moved[f"E{n}"], swapped)
        else:
            direct = moved[f"R{n}"]
            one_back[n], three_back[n] = (swapped, direct), (direct, swapped)

    [two] = more_scores(stores, [(n, [(0, two_back[n])]) for n in range(CHUNKS)], [None])
    two_pair = exchanged(two)
    limited = after(valid_rows, two[1])
    one = three = one_pair = None
    todo = set(range(CHUNKS))
    for group in CHAIN:
        pieces = []
        for item in group.split():
            n, parts = int(item[1:]), {"b": (0, 1), "o": (0,), "t": (1,)}[item[0]]
            blocks = one_back[n], three_back[n]
            pieces.append((n, [(part, *blocks[part]) for part in parts]))
            todo -= {n} if 0 in parts else set()
        if one is None:
            one, three, limit = more_scores(
                stores, pieces, [one, three], limited, weight=WEIGHT
            )
        elif one_pair is None:
            one, three = more_scores(stores, pieces, [one, three], weight=WEIGHT)
        else:
            pieces = [(n, [(0, *blocks) for _, *blocks in targets]) for n, targets in pieces]
            [[theirs]] = more_scores(stores, pieces, [three], sides=(0,))
            [[ours]] = more_scores(stores, pieces, [three], sides=(1,))
            three = theirs, ours
        if one_pair is None and not todo:
            one_pair = exchanged(one)
    out = finish(limit, [own_pair, two_pair], (0, 2), STEPS)
    return finish(limit, [one_pair, exchanged(three)], (1, 3), STEPS, out)


def solution(mesh):
    return jax.shard_map(
        shards,
        mesh=mesh,
        in_specs=(
            P(("groups", "ex"), "dim"),
            P(("groups", "ex"), "dim"),
            P("dim"),
            P(("groups", "ex"), None),
            P(("groups", "ex")),
        ),
        out_specs=P(("groups", "ex", "dim"), None),
        check_vma=False,
    )
```

```python
import functools

import jax
import jax.numpy as jnp
from jax import lax
from jax.experimental import pallas as pl
from jax.experimental.pallas import tpu as pltpu
from jax.sharding import PartitionSpec as P

STEPS = 4
KINDS = "UUT"
PARTS = (4, 6, 6)
CHAIN = ("b0", "o1", "b2", "t1")
ORDER = ("B0", "B1", "B2", "C0", "C1", "E0", "E1", "R2", "C2")
TIES = {"C2": "C0"}
EARLY = "C0"
WEIGHT = 2
CHUNKS = len(PARTS)
VMEM_BYTES = 16 * 1024 * 1024


def params():
    return pltpu.CompilerParams(vmem_limit_bytes=VMEM_BYTES)


def whole_spec():
    return pl.BlockSpec(memory_space=pltpu.VMEM)


def far_spec():
    return pl.BlockSpec(memory_space=pltpu.HBM)


def in_hbm(x):
    return pltpu.with_memory_space_constraint(x, pltpu.HBM)


def cost(flops, traffic):
    return pl.CostEstimate(flops=flops, bytes_accessed=traffic, transcendentals=0)


def cuts_of(depth):
    ends = [depth * sum(PARTS[:n + 1]) // sum(PARTS) for n in range(CHUNKS)]
    return [slice(start, end) for start, end in zip([0] + ends, ends)]


def product(rows, block):
    return lax.dot_general(
        rows, block, (((1,), (1,)), ((), ())), preferred_element_type=jnp.float32
    )


def prepare_kernel(queries, precond, rank, *refs):
    chunks, (own, held, scale, places, arrived) = refs[:CHUNKS], refs[CHUNKS:]
    rows, depth = queries.shape
    cuts = cuts_of(depth)
    loads = [pltpu.make_async_copy(rank, places, arrived.at[CHUNKS])]
    loads.append(pltpu.make_async_copy(precond, scale, arrived.at[CHUNKS + 1]))
    for n, cut in enumerate(cuts):
        loads.append(pltpu.make_async_copy(queries.at[:, cut], held.at[:, cut], arrived.at[n]))
    for load in loads:
        load.start()
    loads[0].wait()
    loads[1].wait()
    positions = lax.broadcasted_iota(jnp.int32, (rows, rows), 0)
    placing = (positions == places[...]).astype(jnp.bfloat16)
    for n, cut in enumerate(cuts):
        loads[2 + n].wait()
        pre = (held[:, cut].astype(jnp.float32) * scale[:, cut]).astype(jnp.bfloat16)
        ordered = jnp.dot(placing, pre, preferred_element_type=jnp.float32).astype(jnp.bfloat16)
        chunks[n][...] = ordered
        own[:, cut] = ordered


def prepare(queries, precond, rank):
    rows, depth = queries.shape
    shapes = [
        jax.ShapeDtypeStruct((rows, cut.stop - cut.start), jnp.bfloat16) for cut in cuts_of(depth)
    ]
    return pl.pallas_call(
        prepare_kernel,
        out_shape=shapes + [jax.ShapeDtypeStruct((rows, depth), jnp.bfloat16)],
        in_specs=[far_spec()] * 3,
        out_specs=[whole_spec()] * (CHUNKS + 1),
        scratch_shapes=[
            pltpu.VMEM((rows, depth), jnp.bfloat16),
            pltpu.VMEM((1, depth), jnp.float32),
            pltpu.VMEM((1, rows), jnp.int32),
            pltpu.SemaphoreType.DMA((CHUNKS + 2,)),
        ],
        compiler_params=params(),
        cost_estimate=cost(2 * rows * rows * depth, 4 * rows * depth),
    )(in_hbm(queries), in_hbm(precond), in_hbm(rank))


def scores_kernel(pieces, fresh, loading, counted, sides, *refs):
    count = len(fresh)
    if counted:
        valid, *refs, limit = refs
        limit[...] = jnp.full(limit.shape, valid[0], jnp.int32)
    odd = lax.rem(lax.axis_index("ex"), 2) == 1
    loads = []
    if loading:
        store, *refs = refs
        *refs, other, mine, arrived = refs
        stores = other, mine
        half = other.shape[0]
        me = lax.axis_index("dim")
        for side, where in enumerate((1 - me, me)):
            place = pl.ds(pl.multiple_of(where * half, half), half)
            loads.append(pltpu.make_async_copy(store.at[place], stores[side], arrived.at[side]))
            loads[side].start()
    else:
        other, mine, *refs = refs
        stores = other, mine
    count_out = len(sides) * count
    outs = refs[-count_out:]
    carried = refs[-count_out - len(sides) * (count - sum(fresh)):-count_out]
    cuts = cuts_of(other.shape[1]) + [slice(0, other.shape[1])]
    stacks = []
    for n, targets in pieces:
        values = []
        for _, even_place, odd_place in targets:
            value = refs[even_place][...]
            if odd_place != even_place:
                value = jnp.where(odd, refs[odd_place][...], value)
            values.append(value)
        stacked = values[0] if len(values) == 1 else jnp.concatenate(values, axis=0)
        stacks.append((n, [which for which, _, _ in targets], stacked))
    for at_side, side in enumerate(sides):
        store = stores[side]
        if loading:
            loads[side].wait()
        sums, at = {}, 0
        for i, new in enumerate(fresh):
            sums[i] = None if new else carried[at + at_side][...]
            at += 0 if new else len(sides)
        for n, whiches, stacked in stacks:
            part = product(store[:, cuts[n]], stacked)
            columns = stacked.shape[0] // len(whiches)
            for k, i in enumerate(whiches):
                here = part[:, k * columns:(k + 1) * columns]
                sums[i] = here if sums[i] is None else sums[i] + here
        for i in range(count):
            outs[len(sides) * i + at_side][...] = sums[i]


def more_scores(stores, pieces, carries, valid=None, sides=(0, 1), weight=1):
    operands, placed = [], []

    def place(block):
        known = [i for i, operand in enumerate(operands) if operand is block]
        if not known:
            operands.append(block)
        return known[0] if known else len(operands) - 1

    loading = not isinstance(stores, tuple)
    half, depth = stores.shape[0] // 2 if loading else stores[0].shape[0], 0
    flops = 0
    for n, targets in pieces:
        kept = []
        for which, *blocks in targets:
            places = [place(block) for block in blocks]
            kept.append((which, places[0], places[-1]))
            flops += 4 * half * blocks[0].size
        placed.append((n, tuple(kept)))
    columns = operands[0].shape[0]
    fresh = tuple(carry is None for carry in carries)
    first = [in_hbm(stores)] if loading else list(stores)
    operands += [carry[side] for carry in carries if carry for side in sides]
    specs = [far_spec()] if loading else [whole_spec()] * 2
    total = jax.ShapeDtypeStruct((half, columns), jnp.float32)
    more = []
    if loading:
        held = jax.ShapeDtypeStruct((half, stores.shape[1]), stores.dtype)
        more = [held, held]
    if valid is not None:
        first, more = [valid] + first, more + [jax.ShapeDtypeStruct((8, columns), jnp.int32)]
        specs = [pl.BlockSpec(memory_space=pltpu.SMEM)] + specs
    count = len(sides) * len(carries)
    outs = pl.pallas_call(
        functools.partial(scores_kernel, tuple(placed), fresh, loading, valid is not None, sides),
        out_shape=[total] * count + more,
        in_specs=specs + [whole_spec()] * len(operands),
        out_specs=[whole_spec()] * (count + len(more)),
        scratch_shapes=[pltpu.SemaphoreType.DMA((2,))] if loading else [],
        compiler_params=params(),
        cost_estimate=cost(weight * flops, weight * 4 * half * columns * count),
    )(*first, *operands)
    totals = [tuple(outs[i:i + len(sides)]) for i in range(0, count, len(sides))]
    if valid is not None:
        return totals + [outs[-1]]
    return totals + ([tuple(outs[count:])] if loading else [])


def finish_kernel(places, limit, *refs):
    out, summed, left = refs[-3:]
    half, columns = refs[0].shape
    row_ids = lax.broadcasted_iota(jnp.int32, (half, columns), 0) + lax.axis_index("dim") * half
    inside = row_ids < limit[:1, :]
    stores = []
    for n, place in enumerate(places):
        cut = slice(n * columns, (n + 1) * columns)
        for part in range(2):
            rows = slice(part * half // 2, (part + 1) * half // 2)
            total = refs[2 * n][rows, :] + refs[2 * n + 1][rows, :]
            summed[rows, cut] = jnp.where(inside[rows, :], total, 0.0)
            to = out.at[rows, place * columns:(place + 1) * columns]
            stores.append(
                pltpu.make_async_copy(summed.at[rows, cut], to, left.at[2 * n + part])
            )
            stores[-1].start()
    for store in stores:
        store.wait()


def finish(limit, pairs, places, steps, out=None):
    half, columns = pairs[0][0].shape
    operands = [ref for pair in pairs for ref in pair]
    given = [] if out is None else [in_hbm(out)]
    return pl.pallas_call(
        functools.partial(finish_kernel, places),
        out_shape=pltpu.HBM((half, columns * steps), jnp.float32),
        in_specs=[whole_spec()] * (1 + len(operands))
        + [far_spec()] * len(given),
        out_specs=far_spec(),
        scratch_shapes=[
            pltpu.VMEM((half, columns * len(places)), jnp.float32),
            pltpu.SemaphoreType.DMA((2 * len(places),)),
        ],
        input_output_aliases={1 + len(operands): 0} if given else {},
        compiler_params=params(),
        cost_estimate=cost(half * columns * len(pairs), 12 * half * columns * len(pairs)),
    )(limit, *operands, *given)


def after(x, *earlier):
    return lax.optimization_barrier((x, *earlier))[0]


def shards(store, queries, precond, query_rank, valid_rows):
    size = lax.axis_size("ex")
    odd = lax.rem(lax.axis_index("ex"), 2) == 1
    one_ahead = [(i, (i + 1) % size) for i in range(size)]
    ahead = [(i, (i + 2) % size) for i in range(size)]
    even_ahead = ahead[::2]
    swap = [(i, i ^ 1) for i in range(size)]
    over_dim = [(0, 1), (1, 0)]

    def send(block, route, axis="ex"):
        return lax.ppermute(block, axis, route)

    def exchanged(total):
        theirs, ours = total
        return ours, send(theirs, over_dim, "dim")

    def by_parity(at_even, at_odd):
        return jnp.where(odd, at_odd, at_even)

    *own, undivided = prepare(queries, precond[None, :], query_rank)
    first, stores = more_scores(store, [(CHUNKS, [(0, undivided)])], [None])
    own_pair = exchanged(first)
    moved = {}

    def tied(name, block):
        earlier = [first[1]] if name == EARLY else []
        return after(block, *earlier, *(moved[key] for key in TIES.get(name, "").split()))

    def move(name, block, route):
        moved[name] = send(tied(name, block), route)
        return moved[name]

    one_back, three_back, two_back = {}, {}, {}
    for step in ORDER:
        kind, n = step[0], int(step[1:])
        if kind == "B":
            two_back[n] = move(step, own[n], ahead)
        elif kind == "A":
            move(step, own[n], swap)
        elif kind == "C":
            block = two_back[n] if KINDS[n] != "U" else by_parity(own[n], two_back[n])
            move(step, block, swap)
        elif kind == "Z":
            move(step, moved[f"A{n}"], even_ahead)
        elif kind == "E":
            move(step, moved[f"C{n}"], even_ahead if KINDS[n] == "I" else ahead)
        else:
            block = two_back[n] if KINDS[n] == "V" else by_parity(own[n], two_back[n])
            move(step, block, one_ahead)
    for n, kind in enumerate(KINDS):
        if kind == "V":
            one_back[n], three_back[n] = (moved[f"Z{n}"], moved[f"A{n}"]), (moved[f"R{n}"],)
            continue
        swapped = moved[f"C{n}"]
        if kind == "U":
            one_back[n], three_back[n] = (swapped,), (moved[f"E{n}"],)
        elif kind == "I":
            one_back[n], three_back[n] = (swapped, moved[f"A{n}"]), (moved[f"E{n}"], swapped)
        else:
            direct = moved[f"R{n}"]
            one_back[n], three_back[n] = (swapped, direct), (direct, swapped)

    [two] = more_scores(stores, [(n, [(0, two_back[n])]) for n in range(CHUNKS)], [None])
    two_pair = exchanged(two)
    limited = after(valid_rows, two[1])
    one = three = one_pair = None
    todo = set(range(CHUNKS))
    for group in CHAIN:
        pieces = []
        for item in group.split():
            n, parts = int(item[1:]), {"b": (0, 1), "o": (0,), "t": (1,)}[item[0]]
            blocks = one_back[n], three_back[n]
            pieces.append((n, [(part, *blocks[part]) for part in parts]))
            todo -= {n} if 0 in parts else set()
        if one is None:
            one, three, limit = more_scores(
                stores, pieces, [one, three], limited, weight=WEIGHT
            )
        elif one_pair is None:
            one, three = more_scores(stores, pieces, [one, three], weight=WEIGHT)
        else:
            pieces = [(n, [(0, *blocks) for _, *blocks in targets]) for n, targets in pieces]
            [[theirs]] = more_scores(stores, pieces, [three], sides=(0,))
            [[ours]] = more_scores(stores, pieces, [three], sides=(1,))
            three = theirs, ours
        if one_pair is None and not todo:
            one_pair = exchanged(one)
    out = finish(limit, [own_pair, two_pair], (0, 2), STEPS)
    return finish(limit, [one_pair, exchanged(three)], (1, 3), STEPS, out)


def solution(mesh):
    return jax.shard_map(
        shards,
        mesh=mesh,
        in_specs=(
            P(("groups", "ex"), "dim"),
            P(("groups", "ex"), "dim"),
            P("dim"),
            P(("groups", "ex"), None),
            P(("groups", "ex")),
        ),
        out_specs=P(("groups", "ex", "dim"), None),
        check_vma=False,
    )
```

```python
import functools

import jax
import jax.numpy as jnp
from jax import lax
from jax.experimental import pallas as pl
from jax.experimental.pallas import tpu as pltpu
from jax.sharding import PartitionSpec as P

STEPS = 4
KINDS = "UUT"
PARTS = (4, 6, 6)
CHAIN = ("b0", "o1", "b2", "t1")
ORDER = ("B0", "B1", "B2", "C0", "C1", "E0", "E1", "R2", "C2")
TIES = {"C2": "C0"}
EARLY = "C0"
OUT = False
WEIGHT = 2
CHUNKS = len(PARTS)
VMEM_BYTES = 16 * 1024 * 1024


def params():
    return pltpu.CompilerParams(vmem_limit_bytes=VMEM_BYTES)


def whole_spec():
    return pl.BlockSpec(memory_space=pltpu.VMEM)


def far_spec():
    return pl.BlockSpec(memory_space=pltpu.HBM)


def in_hbm(x):
    return pltpu.with_memory_space_constraint(x, pltpu.HBM)


def cost(flops, traffic):
    return pl.CostEstimate(flops=flops, bytes_accessed=traffic, transcendentals=0)


def cuts_of(depth):
    ends = [depth * sum(PARTS[:n + 1]) // sum(PARTS) for n in range(CHUNKS)]
    return [slice(start, end) for start, end in zip([0] + ends, ends)]


def product(rows, block):
    return lax.dot_general(
        rows, block, (((1,), (1,)), ((), ())), preferred_element_type=jnp.float32
    )


def prepare_kernel(queries, precond, rank, *refs):
    chunks, (held, scale, places, arrived) = refs[:CHUNKS], refs[CHUNKS:]
    rows, depth = queries.shape
    cuts = cuts_of(depth)
    loads = [pltpu.make_async_copy(rank, places, arrived.at[CHUNKS])]
    loads.append(pltpu.make_async_copy(precond, scale, arrived.at[CHUNKS + 1]))
    for n, cut in enumerate(cuts):
        loads.append(pltpu.make_async_copy(queries.at[:, cut], held.at[:, cut], arrived.at[n]))
    for load in loads:
        load.start()
    loads[0].wait()
    loads[1].wait()
    positions = lax.broadcasted_iota(jnp.int32, (rows, rows), 0)
    placing = (positions == places[...]).astype(jnp.bfloat16)
    for n, cut in enumerate(cuts):
        loads[2 + n].wait()
        pre = (held[:, cut].astype(jnp.float32) * scale[:, cut]).astype(jnp.bfloat16)
        chunks[n][...] = jnp.dot(placing, pre, preferred_element_type=jnp.float32).astype(
            jnp.bfloat16
        )


def prepare(queries, precond, rank):
    rows, depth = queries.shape
    shapes = [
        jax.ShapeDtypeStruct((rows, cut.stop - cut.start), jnp.bfloat16) for cut in cuts_of(depth)
    ]
    return pl.pallas_call(
        prepare_kernel,
        out_shape=shapes,
        in_specs=[far_spec()] * 3,
        out_specs=[whole_spec()] * CHUNKS,
        scratch_shapes=[
            pltpu.VMEM((rows, depth), jnp.bfloat16),
            pltpu.VMEM((1, depth), jnp.float32),
            pltpu.VMEM((1, rows), jnp.int32),
            pltpu.SemaphoreType.DMA((CHUNKS + 2,)),
        ],
        compiler_params=params(),
        cost_estimate=cost(2 * rows * rows * depth, 4 * rows * depth),
    )(in_hbm(queries), in_hbm(precond), in_hbm(rank))


def scores_kernel(pieces, fresh, loading, counted, sides, *refs):
    count = len(fresh)
    if counted:
        valid, *refs, limit = refs
        limit[...] = jnp.full(limit.shape, valid[0], jnp.int32)
    odd = lax.rem(lax.axis_index("ex"), 2) == 1
    loads = []
    if loading:
        store, *refs = refs
        *refs, other, mine, arrived = refs
        stores = other, mine
        half = other.shape[0]
        me = lax.axis_index("dim")
        for side, where in enumerate((1 - me, me)):
            place = pl.ds(pl.multiple_of(where * half, half), half)
            loads.append(pltpu.make_async_copy(store.at[place], stores[side], arrived.at[side]))
            loads[side].start()
    else:
        other, mine, *refs = refs
        stores = other, mine
    count_out = len(sides) * count
    outs = refs[-count_out:]
    carried = refs[-count_out - len(sides) * (count - sum(fresh)):-count_out]
    cuts = cuts_of(other.shape[1])
    stacks = []
    for n, targets in pieces:
        values = []
        for _, even_place, odd_place in targets:
            value = refs[even_place][...]
            if odd_place != even_place:
                value = jnp.where(odd, refs[odd_place][...], value)
            values.append(value)
        stacked = values[0] if len(values) == 1 else jnp.concatenate(values, axis=0)
        stacks.append((n, [which for which, _, _ in targets], stacked))
    for at_side, side in enumerate(sides):
        store = stores[side]
        if loading:
            loads[side].wait()
        sums, at = {}, 0
        for i, new in enumerate(fresh):
            sums[i] = None if new else carried[at + at_side][...]
            at += 0 if new else len(sides)
        for n, whiches, stacked in stacks:
            part = product(store[:, cuts[n]], stacked)
            columns = stacked.shape[0] // len(whiches)
            for k, i in enumerate(whiches):
                here = part[:, k * columns:(k + 1) * columns]
                sums[i] = here if sums[i] is None else sums[i] + here
        for i in range(count):
            outs[len(sides) * i + at_side][...] = sums[i]


def more_scores(stores, pieces, carries, valid=None, sides=(0, 1), weight=1):
    operands, placed = [], []

    def place(block):
        known = [i for i, operand in enumerate(operands) if operand is block]
        if not known:
            operands.append(block)
        return known[0] if known else len(operands) - 1

    loading = not isinstance(stores, tuple)
    half, depth = stores.shape[0] // 2 if loading else stores[0].shape[0], 0
    flops = 0
    for n, targets in pieces:
        kept = []
        for which, *blocks in targets:
            places = [place(block) for block in blocks]
            kept.append((which, places[0], places[-1]))
            flops += 4 * half * blocks[0].size
        placed.append((n, tuple(kept)))
    columns = operands[0].shape[0]
    fresh = tuple(carry is None for carry in carries)
    first = [in_hbm(stores)] if loading else list(stores)
    operands += [carry[side] for carry in carries if carry for side in sides]
    specs = [far_spec()] if loading else [whole_spec()] * 2
    total = jax.ShapeDtypeStruct((half, columns), jnp.float32)
    more = []
    if loading:
        held = jax.ShapeDtypeStruct((half, stores.shape[1]), stores.dtype)
        more = [held, held]
    if valid is not None:
        first, more = [valid] + first, more + [jax.ShapeDtypeStruct((8, columns), jnp.int32)]
        specs = [pl.BlockSpec(memory_space=pltpu.SMEM)] + specs
    count = len(sides) * len(carries)
    outs = pl.pallas_call(
        functools.partial(scores_kernel, tuple(placed), fresh, loading, valid is not None, sides),
        out_shape=[total] * count + more,
        in_specs=specs + [whole_spec()] * len(operands),
        out_specs=[whole_spec()] * (count + len(more)),
        scratch_shapes=[pltpu.SemaphoreType.DMA((2,))] if loading else [],
        compiler_params=params(),
        cost_estimate=cost(weight * flops, weight * 4 * half * columns * count),
    )(*first, *operands)
    totals = [tuple(outs[i:i + len(sides)]) for i in range(0, count, len(sides))]
    if valid is not None:
        return totals + [outs[-1]]
    return totals + ([tuple(outs[count:])] if loading else [])


def finish_kernel(places, limit, *refs):
    out, summed, left = refs[-3:]
    half, columns = refs[0].shape
    row_ids = lax.broadcasted_iota(jnp.int32, (half, columns), 0) + lax.axis_index("dim") * half
    inside = row_ids < limit[:1, :]
    stores = []
    for n, place in enumerate(places):
        cut = slice(n * columns, (n + 1) * columns)
        summed[:, cut] = jnp.where(inside, refs[2 * n][...] + refs[2 * n + 1][...], 0.0)
        to = out.at[:, place * columns:(place + 1) * columns]
        stores.append(pltpu.make_async_copy(summed.at[:, cut], to, left.at[n]))
        stores[n].start()
    for store in stores:
        store.wait()


def finish(limit, pairs, places, steps, out=None):
    half, columns = pairs[0][0].shape
    operands = [ref for pair in pairs for ref in pair]
    given = [] if out is None else [in_hbm(out)]
    return pl.pallas_call(
        functools.partial(finish_kernel, places),
        out_shape=pltpu.HBM((half, columns * steps), jnp.float32),
        in_specs=[whole_spec()] * (1 + len(operands))
        + [far_spec()] * len(given),
        out_specs=far_spec(),
        scratch_shapes=[
            pltpu.VMEM((half, columns * len(places)), jnp.float32),
            pltpu.SemaphoreType.DMA((len(places),)),
        ],
        input_output_aliases={1 + len(operands): 0} if given else {},
        compiler_params=params(),
        cost_estimate=cost(half * columns * len(pairs), 12 * half * columns * len(pairs)),
    )(limit, *operands, *given)


def after(x, *earlier):
    return lax.optimization_barrier((x, *earlier))[0]


def shards(store, queries, precond, query_rank, valid_rows):
    size = lax.axis_size("ex")
    odd = lax.rem(lax.axis_index("ex"), 2) == 1
    one_ahead = [(i, (i + 1) % size) for i in range(size)]
    ahead = [(i, (i + 2) % size) for i in range(size)]
    even_ahead = ahead[::2]
    swap = [(i, i ^ 1) for i in range(size)]
    over_dim = [(0, 1), (1, 0)]

    def send(block, route, axis="ex"):
        return lax.ppermute(block, axis, route)

    def exchanged(total):
        theirs, ours = total
        return ours, send(theirs, over_dim, "dim")

    def by_parity(at_even, at_odd):
        return jnp.where(odd, at_odd, at_even)

    own = prepare(queries, precond[None, :], query_rank)
    first, stores = more_scores(store, [(n, [(0, own[n])]) for n in range(CHUNKS)], [None])
    own_pair = exchanged(first)
    moved = {}

    def tied(name, block):
        earlier = [first[1]] if name == EARLY else []
        return after(block, *earlier, *(moved[key] for key in TIES.get(name, "").split()))

    def move(name, block, route):
        moved[name] = send(tied(name, block), route)
        return moved[name]

    one_back, three_back, two_back = {}, {}, {}
    for step in ORDER:
        kind, n = step[0], int(step[1:])
        if kind == "B":
            two_back[n] = move(step, own[n], ahead)
        elif kind == "A":
            move(step, own[n], swap)
        elif kind == "C":
            block = two_back[n] if KINDS[n] != "U" else by_parity(own[n], two_back[n])
            move(step, block, swap)
        elif kind == "Z":
            move(step, moved[f"A{n}"], even_ahead)
        elif kind == "E":
            move(step, moved[f"C{n}"], even_ahead if KINDS[n] == "I" else ahead)
        else:
            block = two_back[n] if KINDS[n] == "V" else by_parity(own[n], two_back[n])
            move(step, block, one_ahead)
    for n, kind in enumerate(KINDS):
        if kind == "V":
            one_back[n], three_back[n] = (moved[f"Z{n}"], moved[f"A{n}"]), (moved[f"R{n}"],)
            continue
        swapped = moved[f"C{n}"]
        if kind == "U":
            one_back[n], three_back[n] = (swapped,), (moved[f"E{n}"],)
        elif kind == "I":
            one_back[n], three_back[n] = (swapped, moved[f"A{n}"]), (moved[f"E{n}"], swapped)
        else:
            direct = moved[f"R{n}"]
            one_back[n], three_back[n] = (swapped, direct), (direct, swapped)

    [two] = more_scores(stores, [(n, [(0, two_back[n])]) for n in range(CHUNKS)], [None])
    two_pair = exchanged(two)
    limited = after(valid_rows, two[1])
    one = three = None
    def pieces_of(group):
        pieces = []
        for item in group.split():
            n, parts = int(item[1:]), {"b": (0, 1), "o": (0,), "t": (1,)}[item[0]]
            blocks = one_back[n], three_back[n]
            pieces.append((n, [(part, *blocks[part]) for part in parts]))
        return pieces

    for group in CHAIN[:-2]:
        if one is None:
            one, three, limit = more_scores(
                stores, pieces_of(group), [one, three], limited, weight=WEIGHT
            )
        else:
            one, three = more_scores(stores, pieces_of(group), [one, three], weight=WEIGHT)
    out = finish(limit, [own_pair, two_pair], (0, 2), STEPS)
    if OUT:
        one = after(one[0], out), one[1]
    late, last = pieces_of(CHAIN[-2]), pieces_of(CHAIN[-1])
    [one_theirs], [three_theirs] = more_scores(stores, late, [one, three], sides=(0,))
    one_came = send(one_theirs, over_dim, "dim")
    only = [(n, [(0, *blocks) for _, *blocks in targets]) for n, targets in last]
    [[three_theirs]] = more_scores(stores, only, [(three_theirs, None)], sides=(0,))
    three_came = send(three_theirs, over_dim, "dim")
    [one_ours], [three_ours] = more_scores(stores, late, [one, three], sides=(1,))
    [[three_ours]] = more_scores(stores, only, [(None, three_ours)], sides=(1,))
    return finish(limit, [(one_ours, one_came), (three_ours, three_came)], (1, 3), STEPS, out)


def solution(mesh):
    return jax.shard_map(
        shards,
        mesh=mesh,
        in_specs=(
            P(("groups", "ex"), "dim"),
            P(("groups", "ex"), "dim"),
            P("dim"),
            P(("groups", "ex"), None),
            P(("groups", "ex")),
        ),
        out_specs=P(("groups", "ex", "dim"), None),
        check_vma=False,
    )
```
